256 devices in a mesh: space: 16 (over y, z_hi, core), batch: 16 (over z_lo, x).
Axes of the slice: x: 4, y: 4, z: 8 (z_hi: 2, z_lo: 4; z = z_hi * 4 + z_lo), core: 2. Of those that a mesh axis runs over, the one named last changes fastest.
Arguments:
- activations: bfloat16 [16, 48, 16, 16, 128], P('batch', 'space'), may hold values from -6 to 6
- conv1_weight: bfloat16 [3, 3, 128, 128], replicated, may hold values from -0.1875 to 0.1875
- conv2_weight: bfloat16 [3, 3, 128, 128], replicated, may hold values from -0.1875 to 0.1875
- coarse_kernel_weight: bfloat16 [2, 2, 128, 128], replicated, may hold values from -0.25 to 0.25
- skip_cotangent: bfloat16 [16, 48, 16, 16, 128], P('batch', 'space'), may hold values from -6 to 6
- down_cotangent: bfloat16 [16, 48, 8, 8, 128], P('batch', 'space'), may hold values from -6 to 6
- face_neighbours: int32 [48, 4], replicated, may hold values from 0 to 47, as said below
- seam_codes: int32 [48, 4], replicated, may hold values from 0 to 7, as said below
- tile_slots: int32 [48], replicated, may hold values from 0 to 47, each once
Outputs:
- coarse_field: bfloat16 [16, 48, 8, 8, 128], P('batch', 'space')
- input_grad: bfloat16 [16, 48, 16, 16, 128], P('batch', 'space')
- conv1_grad: float32 [3, 3, 128, 128], replicated
- conv2_grad: float32 [3, 3, 128, 128], replicated
- down_grad: float32 [2, 2, 128, 128], replicated
The draws below stay inside these ranges and needn't reach their ends.
Inputs may be any that keep to these rules, and one draw needn't show every extreme that they name: `face_neighbours`: sides pair up: if side s of tile t names tile u with code c, then side c // 2 of tile u names tile t with code 2 s + c % 2. Every tile is named by some side. `seam_codes`: c // 2 is the touching side of the named tile; c % 2 = 1 means its row runs the opposite way. `tile_slots`: each slot holds one tile.
All inputs are finite; a program needn't handle non-finite values.
Results may differ from the reference program's by a relative error of at most 0.009.
Values may be sent and summed in bfloat16 or wider, within the bound.
No kernel may reach another device: no remote copies, remote signals or barrier semaphores. Data moves between devices by JAX's collectives and lax.ppermute only.
A program may use at most 64 MiB of HBM per device.

```python
import math
import jax
import jax.numpy as jnp
import numpy as np
from jax import lax

C = 128
TILE = 16
FACES = 12
FACE_TILES = 2
NT = 48
MEMBERS = 16
HALF = 8


def seam_tables(key):
    per_face = FACE_TILES
    number = FACES * per_face * per_face
    cell_ids = np.arange(number * 4)
    tile_ids = cell_ids // 4
    side_ids = cell_ids % 4
    face_ids = tile_ids // (per_face * per_face)
    tile_row = tile_ids % (per_face * per_face) // per_face
    tile_col = tile_ids % per_face
    next_row = tile_row + np.array([-1, 0, 1, 0])[side_ids]
    next_col = tile_col + np.array([0, 1, 0, -1])[side_ids]
    inside = (next_row >= 0) & (next_row < per_face) & (next_col >= 0) & (next_col < per_face)
    inner_link = face_ids * per_face * per_face + np.clip(next_row, 0, per_face - 1) * per_face + np.clip(next_col, 0, per_face - 1)
    inner_code = (side_ids + 2) % 4 * 2
    position = np.where(side_ids % 2 == 0, tile_col, tile_row)
    face_slot = face_ids * 4 + side_ids
    ordering = jax.random.permutation(key, FACES * 4).astype(jnp.int32)
    adjacent_face = jnp.zeros((FACES * 4,), jnp.int32).at[ordering[0::2]].set(ordering[1::2]).at[ordering[1::2]].set(ordering[0::2])
    flip_bits = jax.random.randint(jax.random.fold_in(key, 1), (FACES * 2,), 0, 2).astype(jnp.int32)
    flip_slot = jnp.zeros((FACES * 4,), jnp.int32).at[ordering[0::2]].set(flip_bits).at[ordering[1::2]].set(flip_bits)
    flip_slot = flip_slot.at[3].set(1).at[adjacent_face[3]].set(1)
    matched = adjacent_face[face_slot]
    other_face = matched // 4
    other_side = matched % 4
    reverse = flip_slot[face_slot]
    other_pos = jnp.where(reverse == 1, per_face - 1 - position, position)
    other_row = jnp.where(other_side == 0, 0, jnp.where(other_side == 2, per_face - 1, other_pos))
    other_col = jnp.where(other_side == 1, per_face - 1, jnp.where(other_side == 3, 0, other_pos))
    outer_link = other_face * per_face * per_face + other_row * per_face + other_col
    outer_code = other_side * 2 + reverse
    links = jnp.where(inside, inner_link, outer_link).reshape(number, 4).astype(jnp.int32)
    codes = jnp.where(inside, inner_code, outer_code).reshape(number, 4).astype(jnp.int32)
    return (links, codes)


def draw_face_neighbours(key, part):
    return seam_tables(key)[0]


def draw_seam_codes(key, part):
    return seam_tables(key)[1]


def block_scale(own_key, dims, pieces, smallest, top_value):
    def one(axis_at, parts):
        draws = jax.random.uniform(jax.random.fold_in(jax.random.fold_in(own_key, 6), axis_at), (parts,), jnp.float32, smallest / len(pieces), top_value / len(pieces))
        return jnp.repeat(jnp.exp(draws), dims[axis_at] // parts).reshape((-1,) + (1,) * (len(dims) - axis_at - 1))

    loudness = one(*pieces[0])
    for cut in pieces[1:]:
        loudness = loudness * one(*cut)
    return loudness


def gaussian(key, dims, scale, reach, cuts=(), held_as=jnp.bfloat16):
    values = jax.random.normal(key, dims, jnp.float32) * scale
    if len(cuts) > 0:
        values = block_scale(key, dims, cuts, -0.22, 0.18) * values
    return jnp.clip(values, min=-reach, max=reach).astype(held_as)


def setup_inputs(seed: int = 0) -> dict:
    streams_of = jax.random.split(jax.random.key(seed), 10)
    activations = gaussian(streams_of[0], (MEMBERS, NT, TILE, TILE, C), 1.0, 6.0, ((0, 16), (1, 16)))
    conv1_weight = gaussian(streams_of[1], (3, 3, C, C), (9 * C) ** -0.5, 0.1875)
    conv2_weight = gaussian(streams_of[2], (3, 3, C, C), (9 * C) ** -0.5, 0.1875)
    coarse_kernel_weight = gaussian(streams_of[3], (2, 2, C, C), (4 * C) ** -0.5, 0.25)
    skip_cotangent = gaussian(streams_of[4], (MEMBERS, NT, TILE, TILE, C), 1.0, 6.0, ((0, 16), (1, 16)))
    down_cotangent = gaussian(streams_of[5], (MEMBERS, NT, HALF, HALF, C), 1.0, 6.0, ((0, 16), (1, 16)))
    face_neighbours = draw_face_neighbours(jax.random.fold_in(streams_of[9], 71), 0)
    seam_codes = draw_seam_codes(jax.random.fold_in(streams_of[9], 71), 0)
    tile_slots = jax.random.permutation(streams_of[8], NT).astype(jnp.int32)
    return dict(activations=activations, conv1_weight=conv1_weight, conv2_weight=conv2_weight, coarse_kernel_weight=coarse_kernel_weight, skip_cotangent=skip_cotangent, down_cotangent=down_cotangent, face_neighbours=face_neighbours, seam_codes=seam_codes, tile_slots=tile_slots)


def edge_rows(value_entries):
    return jnp.stack([value_entries[:, 0], value_entries[:, :, -1], value_entries[:, -1], value_entries[:, :, 0]], axis=1)

def orient(picked, reverse):
    return jnp.where(reverse[:, :, None, None] == 1, picked[:, :, ::-1], picked)

def attach(value_entries, seams):
    number = value_entries.shape[0]
    channels = value_entries.shape[-1]
    corner = jnp.zeros((number, 1, channels), value_entries.dtype)
    top_row = jnp.concatenate([corner, seams[:, 0], corner], axis=1)[:, None]
    bottom = jnp.concatenate([corner, seams[:, 2], corner], axis=1)[:, None]
    middle = jnp.concatenate([seams[:, 3][:, :, None], value_entries, seams[:, 1][:, :, None]], axis=2)
    return jnp.concatenate([top_row, middle, bottom], axis=1)

def convolve(padded, weight_tensor):
    number = padded.shape[0]
    extent = padded.shape[1] - 2
    channels = weight_tensor.shape[-1]
    running = jnp.zeros((number * extent * extent, channels), jnp.float32)
    for a in range(3):
        for b in range(3):
            window = padded[:, a:a + extent, b:b + extent].reshape(-1, padded.shape[-1])
            running = running + jnp.dot(window, weight_tensor[a, b], preferred_element_type=jnp.float32)
    return running.reshape(number, extent, extent, channels)

def flipped(weight_tensor):
    return jnp.transpose(weight_tensor[::-1, ::-1], (0, 1, 3, 2))

def kernel_grad(padded, cotangent):
    extent = cotangent.shape[1]
    flattened = cotangent.reshape(-1, cotangent.shape[-1])
    kernel_rows = []
    for a in range(3):
        row_parts = []
        for b in range(3):
            window = padded[:, a:a + extent, b:b + extent].reshape(-1, padded.shape[-1])
            row_parts.append(lax.dot_general(window, flattened, (((0,), (0,)), ((), ())), preferred_element_type=jnp.float32))
        kernel_rows.append(jnp.stack(row_parts))
    return jnp.stack(kernel_rows)

def halve_resolution(value_entries, weight_tensor):
    number, extent, _, channels = value_entries.shape
    reduced = extent // 2
    blocks = value_entries.reshape(number, reduced, 2, reduced, 2, channels)
    running = jnp.zeros((number * reduced * reduced, channels), jnp.float32)
    for a in range(2):
        for b in range(2):
            running = running + jnp.dot(blocks[:, :, a, :, b].reshape(-1, channels), weight_tensor[a, b], preferred_element_type=jnp.float32)
    return running.reshape(number, reduced, reduced, channels)

def down_back(cotangent, weight_tensor):
    number, reduced, _, channels = cotangent.shape
    flattened = cotangent.reshape(-1, channels)
    halves = []
    for a in range(2):
        parts_b = [jnp.dot(flattened, weight_tensor[a, b].T, preferred_element_type=jnp.float32).reshape(number, reduced, reduced, channels) for b in range(2)]
        halves.append(jnp.stack(parts_b, axis=3))
    return jnp.stack(halves, axis=2).reshape(number, 2 * reduced, 2 * reduced, channels)

def down_kernel_grad(value_entries, cotangent):
    number, extent, _, channels = value_entries.shape
    reduced = extent // 2
    blocks = value_entries.reshape(number, reduced, 2, reduced, 2, channels)
    flattened = cotangent.reshape(-1, channels)
    kernel_rows = []
    for a in range(2):
        row_parts = []
        for b in range(2):
            window = blocks[:, :, a, :, b].reshape(-1, channels)
            row_parts.append(lax.dot_general(window, flattened, (((0,), (0,)), ((), ())), preferred_element_type=jnp.float32))
        kernel_rows.append(jnp.stack(row_parts))
    return jnp.stack(kernel_rows)

def gelu_back(preact, cotangent):
    return jax.vjp(jax.nn.gelu, preact)[1](cotangent)[0]

def add_sides(interior, returned_rows):
    interior = interior.at[:, 0].add(returned_rows[:, 0])
    interior = interior.at[:, :, -1].add(returned_rows[:, 1])
    interior = interior.at[:, -1].add(returned_rows[:, 2])
    return interior.at[:, :, 0].add(returned_rows[:, 3])

def reference(activations, conv1_weight, conv2_weight, coarse_kernel_weight, skip_cotangent, down_cotangent, face_neighbours, seam_codes, tile_slots):
    tile_of = jnp.zeros((NT,), jnp.int32).at[tile_slots].set(jnp.arange(NT, dtype=jnp.int32))
    own_codes = seam_codes[tile_of]
    source_slot = tile_slots[face_neighbours[tile_of]]
    source_side = own_codes // 2
    reverse = own_codes % 2

    def seams_of(value_entries):
        return orient(edge_rows(value_entries)[source_slot, source_side], reverse)

    def adjoint(cotangent, weight_tensor):
        wide = jnp.pad(cotangent, ((0, 0), (2, 2), (2, 2), (0, 0)))
        whole = convolve(wide, flipped(weight_tensor))
        rim_terms = jnp.stack([whole[:, 0, 1:-1], whole[:, 1:-1, -1], whole[:, -1, 1:-1], whole[:, 1:-1, 0]], axis=1)
        returned_rows = orient(rim_terms[source_slot, source_side], reverse)
        return add_sides(whole[:, 1:-1, 1:-1], returned_rows)

    def member(inputs):
        value_entries, skip_part, down_part = inputs
        initial_padded_tile = attach(value_entries, seams_of(value_entries))
        first_pre = convolve(initial_padded_tile, conv1_weight)
        first_act = jax.nn.gelu(first_pre).astype(jnp.bfloat16)
        second_pad = attach(first_act, seams_of(first_act))
        second_pre = convolve(second_pad, conv2_weight)
        later_activation = jax.nn.gelu(second_pre).astype(jnp.bfloat16)
        coarse_field = halve_resolution(later_activation, coarse_kernel_weight).astype(jnp.bfloat16)
        second_cot = skip_part.astype(jnp.float32) + down_back(down_part, coarse_kernel_weight)
        second_delta = gelu_back(second_pre, second_cot).astype(jnp.bfloat16)
        down_grad = down_kernel_grad(later_activation, down_part)
        second_grad = kernel_grad(second_pad, second_delta)
        first_cot = adjoint(second_delta, conv2_weight)
        first_delta = gelu_back(first_pre, first_cot).astype(jnp.bfloat16)
        first_grad = kernel_grad(initial_padded_tile, first_delta)
        input_grad = adjoint(first_delta, conv1_weight).astype(jnp.bfloat16)
        return (coarse_field, input_grad, first_grad, second_grad, down_grad)
    results = lax.map(member, (activations, skip_cotangent, down_cotangent))
    grad_scale = 1.0 / math.sqrt(MEMBERS * NT * TILE * TILE)
    return (results[0], results[1], lax.optimization_barrier(jnp.sum(results[2], axis=0)) * grad_scale, lax.optimization_barrier(jnp.sum(results[3], axis=0)) * grad_scale, lax.optimization_barrier(jnp.sum(results[4], axis=0)) * grad_scale)
```

```python
import math

import jax
import jax.numpy as jnp
from jax import lax
from jax.sharding import Mesh
from jax.sharding import PartitionSpec as P

CHIPS = ("y", "z")
PLANE = ("x", "y")
DEPTH = ("z", "w")


def edge_rows(value_entries):
    return jnp.stack(
        [
            value_entries[:, 0],
            value_entries[:, :, -1],
            value_entries[:, -1],
            value_entries[:, :, 0],
        ],
        axis=1,
    )


def orient(picked, reverse):
    return jnp.where(reverse[:, :, None, None] == 1, picked[:, :, ::-1], picked)


def attach(value_entries, seams):
    number = value_entries.shape[0]
    channels = value_entries.shape[-1]
    corner = jnp.zeros((number, 1, channels), value_entries.dtype)
    top_row = jnp.concatenate([corner, seams[:, 0], corner], axis=1)[:, None]
    bottom = jnp.concatenate([corner, seams[:, 2], corner], axis=1)[:, None]
    middle = jnp.concatenate(
        [seams[:, 3][:, :, None], value_entries, seams[:, 1][:, :, None]], axis=2
    )
    return jnp.concatenate([top_row, middle, bottom], axis=1)


def convolve(padded, weight_tensor):
    number = padded.shape[0]
    extent = padded.shape[1] - 2
    channels = weight_tensor.shape[-1]
    running = jnp.zeros((number * extent * extent, channels), jnp.float32)
    for a in range(3):
        for b in range(3):
            window = padded[:, a : a + extent, b : b + extent].reshape(-1, padded.shape[-1])
            running = running + jnp.dot(
                window, weight_tensor[a, b], preferred_element_type=jnp.float32
            )
    return running.reshape(number, extent, extent, channels)


def flipped(weight_tensor):
    return jnp.transpose(weight_tensor[::-1, ::-1], (0, 1, 3, 2))


def kernel_grad(padded, cotangent):
    extent = cotangent.shape[1]
    flattened = cotangent.reshape(-1, cotangent.shape[-1])
    kernel_rows = []
    for a in range(3):
        row_parts = []
        for b in range(3):
            window = padded[:, a : a + extent, b : b + extent].reshape(-1, padded.shape[-1])
            row_parts.append(
                lax.dot_general(
                    window, flattened, (((0,), (0,)), ((), ())), preferred_element_type=jnp.float32
                )
            )
        kernel_rows.append(jnp.stack(row_parts))
    return jnp.stack(kernel_rows)


def halve_resolution(value_entries, weight_tensor):
    number, extent, _, channels = value_entries.shape
    reduced = extent // 2
    blocks = value_entries.reshape(number, reduced, 2, reduced, 2, channels)
    running = jnp.zeros((number * reduced * reduced, channels), jnp.float32)
    for a in range(2):
        for b in range(2):
            running = running + jnp.dot(
                blocks[:, :, a, :, b].reshape(-1, channels),
                weight_tensor[a, b],
                preferred_element_type=jnp.float32,
            )
    return running.reshape(number, reduced, reduced, channels)


def down_back(cotangent, weight_tensor):
    number, reduced, _, channels = cotangent.shape
    flattened = cotangent.reshape(-1, channels)
    halves = []
    for a in range(2):
        parts_b = [
            jnp.dot(flattened, weight_tensor[a, b].T, preferred_element_type=jnp.float32).reshape(
                number, reduced, reduced, channels
            )
            for b in range(2)
        ]
        halves.append(jnp.stack(parts_b, axis=3))
    return jnp.stack(halves, axis=2).reshape(number, 2 * reduced, 2 * reduced, channels)


def down_kernel_grad(value_entries, cotangent):
    number, extent, _, channels = value_entries.shape
    reduced = extent // 2
    blocks = value_entries.reshape(number, reduced, 2, reduced, 2, channels)
    flattened = cotangent.reshape(-1, channels)
    kernel_rows = []
    for a in range(2):
        row_parts = []
        for b in range(2):
            window = blocks[:, :, a, :, b].reshape(-1, channels)
            row_parts.append(
                lax.dot_general(
                    window, flattened, (((0,), (0,)), ((), ())), preferred_element_type=jnp.float32
                )
            )
        kernel_rows.append(jnp.stack(row_parts))
    return jnp.stack(kernel_rows)


def gelu_back(preact, cotangent):
    return jax.vjp(jax.nn.gelu, preact)[1](cotangent)[0]


def add_sides(interior, returned_rows):
    interior = interior.at[:, 0].add(returned_rows[:, 0])
    interior = interior.at[:, :, -1].add(returned_rows[:, 1])
    interior = interior.at[:, -1].add(returned_rows[:, 2])
    return interior.at[:, :, 0].add(returned_rows[:, 3])


def side_kernels(weight_tensor):
    return [weight_tensor[0], weight_tensor[:, 2], weight_tensor[2], weight_tensor[:, 0]]


def edge_conv(border, triple):
    number, extent, channels = border.shape
    blank = jnp.zeros((number, 1, channels), border.dtype)
    leading = jnp.concatenate([border[:, 1:], blank], axis=1).reshape(-1, channels)
    trailing = jnp.concatenate([blank, border[:, :-1]], axis=1).reshape(-1, channels)
    running = jnp.dot(leading, triple[0].T, preferred_element_type=jnp.float32)
    running = running + jnp.dot(
        border.reshape(-1, channels), triple[1].T, preferred_element_type=jnp.float32
    )
    running = running + jnp.dot(trailing, triple[2].T, preferred_element_type=jnp.float32)
    return running.reshape(number, extent, channels)


def swap_core(block):
    return lax.ppermute(block, "c", [(0, 1), (1, 0)])


def spread(block, axes):
    number = lax.axis_size(axes)
    copies = jnp.broadcast_to(block[None], (number,) + block.shape)
    return lax.all_to_all(copies, axes, 0, 0)


def gather_space(block):
    mine = spread(block, CHIPS)
    both = jnp.stack([mine, swap_core(mine)])
    return both.reshape((-1,) + block.shape[1:])


def gathered_slot(slot, tiles_here):
    chips = lax.axis_size(CHIPS)
    owner = slot // tiles_here
    other = (owner + lax.axis_index("c")) % 2
    return (other * chips + owner // 2) * tiles_here + slot % tiles_here


def total_sum(parts):
    rows = jnp.concatenate([part.reshape(-1, part.shape[-1]) for part in parts])
    half = rows.shape[0] // 2
    core = lax.axis_index("c")
    keep = lax.dynamic_slice_in_dim(rows, core * half, half)
    give = lax.dynamic_slice_in_dim(rows, (1 - core) * half, half)
    keep = keep + swap_core(give)
    number = lax.axis_size(PLANE)
    pieces = keep.astype(jnp.bfloat16).reshape(number, half // number, -1)
    piece = jnp.sum(lax.all_to_all(pieces, PLANE, 0, 0).astype(jnp.float32), axis=0)
    piece = jnp.sum(spread(piece, DEPTH), axis=0).astype(jnp.bfloat16)
    mine = spread(piece, PLANE).reshape(half, -1)
    other = swap_core(mine)
    first = core == 0
    rows = jnp.concatenate([jnp.where(first, mine, other), jnp.where(first, other, mine)])
    rows = rows.astype(jnp.float32)
    results = []
    at = 0
    for part in parts:
        size = part.size // part.shape[-1]
        results.append(rows[at : at + size].reshape(part.shape))
        at += size
    return results


def shards(
    activations,
    conv1_weight,
    conv2_weight,
    coarse_kernel_weight,
    skip_cotangent,
    down_cotangent,
    face_neighbours,
    seam_codes,
    tile_slots,
):
    value_entries = activations[0]
    tiles_here = value_entries.shape[0]
    extent = value_entries.shape[1]
    total_tiles = tile_slots.shape[0]
    first_slot = lax.axis_index(("y", "z", "c")) * tiles_here
    own_slots = first_slot + jnp.arange(tiles_here, dtype=jnp.int32)
    matches = tile_slots[None, :] == own_slots[:, None]
    own_tiles = jnp.sum(
        jnp.where(matches, jnp.arange(total_tiles, dtype=jnp.int32)[None, :], 0), axis=1
    )
    own_codes = seam_codes[own_tiles]
    source_slot = gathered_slot(tile_slots[face_neighbours[own_tiles]], tiles_here)
    source_side = own_codes // 2
    reverse = own_codes % 2

    def seams_of(field_values):
        gathered = gather_space(edge_rows(field_values))
        return orient(gathered[source_slot, source_side], reverse)

    def adjoint(cotangent, weight_tensor):
        narrow = jnp.pad(cotangent, ((0, 0), (1, 1), (1, 1), (0, 0)))
        interior = convolve(narrow, flipped(weight_tensor))
        triples = side_kernels(weight_tensor)
        own_edges = edge_rows(cotangent)
        rim_terms = jnp.stack(
            [edge_conv(own_edges[:, facing], triples[facing]) for facing in range(4)], axis=1
        )
        gathered = gather_space(rim_terms.astype(jnp.bfloat16)).astype(rim_terms.dtype)
        returned_rows = orient(gathered[source_slot, source_side], reverse)
        return add_sides(interior, returned_rows)

    grad_scale = 1.0 / math.sqrt(
        lax.axis_size(("w", "x")) * total_tiles * extent * extent
    )
    initial_padded_tile = attach(value_entries, seams_of(value_entries))
    first_pre = convolve(initial_padded_tile, conv1_weight)
    first_act = jax.nn.gelu(first_pre).astype(jnp.bfloat16)
    second_pad = attach(first_act, seams_of(first_act))
    second_pre = convolve(second_pad, conv2_weight)
    later_activation = jax.nn.gelu(second_pre).astype(jnp.bfloat16)
    coarse_field = halve_resolution(later_activation, coarse_kernel_weight).astype(jnp.bfloat16)
    down_part = down_cotangent[0]
    second_cot = skip_cotangent[0].astype(jnp.float32) + down_back(down_part, coarse_kernel_weight)
    second_delta = gelu_back(second_pre, second_cot).astype(jnp.bfloat16)
    down_grad = down_kernel_grad(later_activation, down_part) * grad_scale
    second_grad = kernel_grad(second_pad, second_delta) * grad_scale
    first_cot = adjoint(second_delta, conv2_weight)
    first_delta = gelu_back(first_pre, first_cot).astype(jnp.bfloat16)
    first_grad = kernel_grad(initial_padded_tile, first_delta) * grad_scale
    input_grad = adjoint(first_delta, conv1_weight).astype(jnp.bfloat16)
    first_grad, second_grad, down_grad = total_sum([first_grad, second_grad, down_grad])
    return (coarse_field[None], input_grad[None], first_grad, second_grad, down_grad)


def solution(mesh):
    batch = mesh.shape["batch"]
    along_x = 4 if batch % 4 == 0 else 1
    fine = Mesh(
        mesh.devices.reshape(4, 2, 2, batch // along_x, along_x), ("y", "z", "c", "w", "x")
    )
    field = P(("w", "x"), ("y", "z", "c"), None, None, None)
    return jax.shard_map(
        shards,
        mesh=fine,
        in_specs=(field, P(), P(), P(), field, field, P(), P(), P()),
        out_specs=(field, field, P(), P(), P()),
        check_vma=False,
    )
```

```python
import functools
import math

import jax
import jax.numpy as jnp
from jax import lax
from jax.experimental import pallas as pl
from jax.experimental.pallas import tpu as pltpu
from jax.sharding import Mesh
from jax.sharding import PartitionSpec as P

CHIPS = ("y", "z")
PLANE = ("x", "y")
DEPTH = ("z", "w")
SLOPE = math.sqrt(2.0 / math.pi)
CUBIC = 0.044715
BF16 = jnp.bfloat16
F32 = jnp.float32
EDGE = 16
CH = 128


def swap_core(block):
    return lax.ppermute(block, "c", [(0, 1), (1, 0)])


def spread(block, axes):
    number = lax.axis_size(axes)
    copies = jnp.broadcast_to(block[None], (number,) + block.shape)
    return lax.all_to_all(copies, axes, 0, 0)


def swap_apart(block, axis, apart):
    number = lax.axis_size(axis)
    return lax.ppermute(block, axis, [(i, i ^ apart) for i in range(number)])


def rings(field_values):
    return jnp.stack(
        [
            field_values[:, :2],
            jnp.swapaxes(field_values[:, :, :-3:-1], 1, 2),
            field_values[:, :-3:-1],
            jnp.swapaxes(field_values[:, :, :2], 1, 2),
        ],
        axis=1,
    )


def side_frames(weight_tensor):
    turned = jnp.swapaxes(weight_tensor, 0, 1)
    return jnp.stack([weight_tensor, turned[::-1], weight_tensor[::-1], turned])


def flipped(weight_tensor):
    return jnp.transpose(weight_tensor[::-1, ::-1], (0, 1, 3, 2))


def frame_adjoint(frames):
    return jnp.transpose(frames, (1, 2, 4, 0, 3)).reshape(-1, 4 * CH)


def gelu(v):
    return 0.5 * v * (1.0 + jnp.tanh(SLOPE * (v + CUBIC * v * v * v)))


def gelu_slope(v):
    t = jnp.tanh(SLOPE * (v + CUBIC * v * v * v))
    return 0.5 * (1.0 + t) + (0.5 * SLOPE) * v * (1.0 - t * t) * (1.0 + (3.0 * CUBIC) * v * v)


def dot(left, right):
    return jnp.dot(left, right, preferred_element_type=F32)


def dot_rows(left, right):
    return lax.dot_general(left, right, (((0,), (0,)), ((), ())), preferred_element_type=F32)


def turned(turn, rows):
    high = rows.astype(BF16)
    low = (rows - high.astype(F32)).astype(BF16)
    return dot(turn, high) + dot(turn, low)


def as_rows(block):
    return block.reshape(-1, CH)


def windows(pad_ref, cols_ref):
    for a in range(3):
        for b in range(3):
            part = pad_ref[:, a : a + EDGE, b : b + EDGE, :].astype(BF16)
            cols_ref[:, (3 * a + b) * CH : (3 * a + b + 1) * CH] = as_rows(part)


def triples(line_ref, cols_ref):
    for at in range(3):
        part = line_ref[:, 2 - at : 2 - at + EDGE, :].astype(BF16)
        cols_ref[0 : line_ref.shape[0] * EDGE, at * CH : (at + 1) * CH] = as_rows(part)


def pick(rows_ref, at, count, side, base=0):
    lanes = pl.ds(pl.multiple_of(base + side * CH, CH), CH)
    return rows_ref[pl.ds(at, count), lanes]


def pad_place(side):
    return {0: 0, 1: EDGE + 1, 2: EDGE + 1, 3: 0}[side]


def edge_place(side):
    return {0: 1, 1: EDGE, 2: EDGE, 3: 1}[side]


def put_side(pad_ref, tile, side, place, rows, add=False):
    if side % 2 == 0:
        if add:
            rows = rows + pad_ref[tile, place, 1 : EDGE + 1, :]
        pad_ref[tile, place, 1 : EDGE + 1, :] = rows
        return
    for i in range(EDGE):
        row = rows[i : i + 1]
        if add:
            row = row + pad_ref[tile, 1 + i, place : place + 1, :]
        pad_ref[tile, 1 + i, place : place + 1, :] = row


def get_side(pad_ref, tile, side, place):
    if side % 2 == 0:
        return pad_ref[tile, place, 1 : EDGE + 1, :]
    rows = [pad_ref[tile, 1 + i, place : place + 1, :] for i in range(EDGE)]
    return jnp.concatenate(rows, axis=0)


def near_at(n):
    return 8 * n


def lateral_at(j):
    return 96 + 8 * j


def table_kernel(near_ref, code_ref, slot_ref, index_ref, turn_ref):
    total = slot_ref.shape[0]
    tiles = 3
    core = lax.axis_index("c")
    at_y = lax.axis_index("y")
    at_z = lax.axis_index("z")
    first = ((at_y * 2 + at_z) * 2 + core) * tiles

    def look(i, found):
        here = slot_ref[i]
        return tuple(jnp.where(here == first + k, i, found[k]) for k in range(tiles))

    own = lax.fori_loop(0, total, look, (jnp.int32(0),) * tiles)

    def place(tile):
        slot = slot_ref[tile]
        owner = slot // tiles
        chip = ((owner // 4) ^ at_y) * 2 + ((owner // 2) % 2 ^ at_z)
        local = slot % tiles
        return (owner + core) % 2, (owner // 2) * tiles + local, chip * tiles + local

    column = lax.broadcasted_iota(jnp.int32, (EDGE, 12 * EDGE), 1)
    row = lax.broadcasted_iota(jnp.int32, (EDGE, 12 * EDGE), 0)
    for side in range(4):
        for k in range(tiles):
            n = side * tiles + k
            near = near_ref[own[k], side]
            code = code_ref[own[k], side]
            near_side = code // 2
            reverse = code % 2
            other, slot, crossed = place(near)
            index_ref[near_at(n)] = other
            index_ref[near_at(n) + 1] = slot
            index_ref[near_at(n) + 4] = crossed
            index_ref[near_at(n) + 2] = near_side
            index_ref[near_at(n) + 3] = reverse
            source = jnp.where(reverse == 1, EDGE - 1 - row, row) + n * EDGE
            turn_ref[n * EDGE : (n + 1) * EDGE, :] = (
                jnp.where(column == source, 1.0, 0.0).astype(F32).astype(BF16)
            )
            upright = near_side % 2
            far = jnp.where((near_side == 1) | (near_side == 2), 1, 0)
            for h in range(2):
                lateral = jnp.where(upright == 1, (0, 2)[h], (3, 1)[h])
                tile = near_ref[near, lateral]
                lateral_code = code_ref[near, lateral]
                other, slot, crossed = place(tile)
                at = lateral_at(2 * n + h)
                index_ref[at] = other
                index_ref[at + 1] = slot
                index_ref[at + 4] = crossed
                index_ref[at + 2] = lateral_code // 2
                index_ref[at + 3] = (far + lateral_code) % 2


def table_row(mine_ref, other_ref, index_ref, at, depth, crossed=False):
    slot = index_ref[at + (4 if crossed else 1)]
    side = index_ref[at + 2]
    mine = mine_ref[slot, side, depth]
    other = other_ref[slot, side, depth]
    return jnp.where(index_ref[at] == 0, mine.astype(F32), other.astype(F32))


def end_rows(mine_ref, other_ref, index_ref, j, crossed=False):
    row = table_row(mine_ref, other_ref, index_ref, lateral_at(j), 0, crossed)
    far = index_ref[lateral_at(j) + 3] == 1
    last = EDGE - 1
    return far, jnp.where(far, row[last:], row[:1]), jnp.where(far, row[last - 1 : last], row[1:2])


def forward_kernel(
    index_ref, turn_ref, x_ref, ring_ref, mine_ref, other_ref, skip_ref, down_ref,
    w1_ref, w1_sides_ref, w2_ref, w2_back_ref, w2_adjoint_ref, wc_ref, wc_back_ref,
    coarse_ref, delta_ring_ref, grad_ref, pre_ref, inner_ref, strip_pre_ref, sent_ref,
    pad_ref, pad2_ref, patch_ref, cols_ref, cols2_ref, strip_ref, wide_ref, split_ref,
    line_ref, line_cols_ref, fine_ref, down_cols_ref,
):
    tiles = x_ref.shape[0]
    patch_ref[...] = jnp.zeros_like(patch_ref)
    pad_ref[...] = jnp.zeros_like(pad_ref)
    pad2_ref[...] = jnp.zeros_like(pad2_ref)
    line_ref[...] = jnp.zeros_like(line_ref)
    split_ref[...] = jnp.zeros_like(split_ref)
    turn = turn_ref[...]

    pad_ref[:, 1 : EDGE + 1, 1 : EDGE + 1, :] = x_ref[...].astype(F32)
    near = []
    own = []
    for n in range(12):
        side, k = n // tiles, n % tiles
        own.append(ring_ref[k, side, 0])
        edge = table_row(mine_ref, other_ref, index_ref, near_at(n), 0)
        near.append(edge)
        patch_ref[n, 1, 1 : EDGE + 1, :] = edge
        patch_ref[n, 2, 1 : EDGE + 1, :] = table_row(
            mine_ref, other_ref, index_ref, near_at(n), 1
        )
        for h in range(2):
            _, outer, inner = end_rows(mine_ref, other_ref, index_ref, 2 * n + h)
            at = (0, EDGE + 1)[h]
            patch_ref[n, 1, at : at + 1, :] = outer
            patch_ref[n, 2, at : at + 1, :] = inner
    seams = dot(turn, jnp.concatenate(near, axis=0).astype(BF16))
    own_turned = dot(turn, jnp.concatenate(own, axis=0))
    patch_ref[:, 0, 1 : EDGE + 1, :] = own_turned.reshape(12, EDGE, CH)
    for n in range(12):
        side, k = n // tiles, n % tiles
        put_side(pad_ref, k, side, pad_place(side), seams[n * EDGE : (n + 1) * EDGE])
    for r in range(3):
        for b in range(3):
            part = patch_ref[:, r, b : b + EDGE, :].astype(BF16)
            strip_ref[:, (3 * r + b) * CH : (3 * r + b + 1) * CH] = as_rows(part)
    wide_ref[...] = dot(strip_ref[...], w1_sides_ref[...])
    for n in range(12):
        strip_pre_ref[n * EDGE : (n + 1) * EDGE, :] = pick(
            wide_ref, n * EDGE, EDGE, index_ref[near_at(n) + 2]
        )
    windows(pad_ref, cols_ref)
    pre_ref[...] = dot(cols_ref[...], w1_ref[...])
    first_act = gelu(pre_ref[...]).astype(BF16).astype(F32)
    pad2_ref[:, 1 : EDGE + 1, 1 : EDGE + 1, :] = first_act.reshape(tiles, EDGE, EDGE, CH)
    strip_act = dot(turn, gelu(strip_pre_ref[...]).astype(BF16))
    for n in range(12):
        side, k = n // tiles, n % tiles
        put_side(pad2_ref, k, side, pad_place(side), strip_act[n * EDGE : (n + 1) * EDGE])
    windows(pad2_ref, cols2_ref)
    second_pre = dot(cols2_ref[...], w2_ref[...])
    second_act = gelu(second_pre).astype(BF16).astype(F32)
    fine_ref[...] = second_act.reshape(tiles, EDGE, EDGE, CH)
    half = EDGE // 2
    for a in range(2):
        for b in range(2):
            part = fine_ref[:, pl.ds(a, half, 2), pl.ds(b, half, 2), :]
            down_cols_ref[:, (2 * a + b) * CH : (2 * a + b + 1) * CH] = as_rows(part).astype(BF16)
    coarse_ref[...] = dot(down_cols_ref[...], wc_ref[...]).astype(BF16)
    down = down_ref[...]
    spread_down = dot(down, wc_back_ref[...])
    for a in range(2):
        for b in range(2):
            part = spread_down[:, (2 * a + b) * CH : (2 * a + b + 1) * CH]
            fine_ref[:, pl.ds(a, half, 2), pl.ds(b, half, 2), :] = part.reshape(
                tiles, half, half, CH
            )
    second_cot = skip_ref[...].astype(F32) + fine_ref[...]
    delta = (gelu_slope(second_pre) * as_rows(second_cot)).astype(BF16)
    pad_ref[...] = jnp.zeros_like(pad_ref)
    pad_ref[:, 1 : EDGE + 1, 1 : EDGE + 1, :] = delta.astype(F32).reshape(tiles, EDGE, EDGE, CH)
    for side in range(4):
        step = (1, -1, -1, 1)[side]
        for k in range(tiles):
            for depth in range(2):
                rows = get_side(pad_ref, k, side, edge_place(side) + step * depth)
                delta_ring_ref[k, side, depth] = rows.astype(BF16)
                if depth == 0:
                    line_ref[side * tiles + k, 1 : EDGE + 1, :] = rows
    core = lax.axis_index("c")

    def put_grad(at, block):
        half = at // 11
        rows = slice(at % 11 * CH, (at % 11 + 1) * CH)
        grad_ref[jnp.where(core == half, 0, 1), rows, :] = block

    down_grad = dot_rows(down_cols_ref[...], down)
    for at in range(4):
        put_grad(18 + at, down_grad[at * CH : (at + 1) * CH])
    second_grad = dot_rows(cols2_ref[...], delta)
    for at in range(9):
        put_grad(9 + at, second_grad[at * CH : (at + 1) * CH])

    windows(pad_ref, cols2_ref)
    inner = dot(cols2_ref[...], w2_back_ref[...])
    inner_ref[...] = inner
    inner_delta = (gelu_slope(pre_ref[...]) * inner).astype(BF16)
    triples(line_ref, line_cols_ref)
    rims = []
    for side in range(4):
        rows = slice(side * tiles * EDGE, (side + 1) * tiles * EDGE)
        lanes = slice(side * CH, (side + 1) * CH)
        rims.append(dot(line_cols_ref[rows, :], w2_adjoint_ref[: 3 * CH, lanes]))
    sent = turned(turn, jnp.concatenate(rims, axis=0))
    sent_ref[...] = sent
    sent_delta = (gelu_slope(strip_pre_ref[...]) * sent).astype(BF16)
    for n in range(12):
        lanes = pl.ds(pl.multiple_of(index_ref[near_at(n) + 2] * CH, CH), CH)
        rows = slice(n * EDGE, (n + 1) * EDGE)
        split_ref[rows, lanes] = sent_delta[rows]
    sent_grad = dot_rows(strip_ref[...], split_ref[...])
    first_grad = dot_rows(cols_ref[...], inner_delta)
    for a in range(3):
        for b in range(3):
            at = (3 * a + b) * CH
            block = first_grad[at : at + CH]
            for side, r, k in ((0, a, b), (1, 2 - b, a), (2, 2 - a, b), (3, b, a)):
                source = (3 * r + k) * CH
                block = block + sent_grad[source : source + CH, side * CH : (side + 1) * CH]
            put_grad(3 * a + b, block)


def backward_kernel(
    index_ref, turn_ref, mine_ref, other_ref, pre_ref, inner_ref, strip_pre_ref, sent_ref,
    w1_back_ref, w1_adjoint_ref, w2_adjoint_ref,
    out_ref,
    pad_ref, cols_ref, line_ref, deep_ref, line_cols_ref, deep_cols_ref, ends_ref, wide_ref,
    strip_wide_ref, cot_ref,
):
    tiles = out_ref.shape[0]
    turn = turn_ref[...]
    line_ref[...] = jnp.zeros_like(line_ref)
    deep_ref[...] = jnp.zeros_like(deep_ref)
    ends_ref[...] = jnp.zeros_like(ends_ref)
    pad_ref[...] = jnp.zeros_like(pad_ref)
    for n in range(12):
        for depth, rows_ref in ((0, line_ref), (1, deep_ref)):
            rows_ref[n, 1 : EDGE + 1, :] = table_row(
                mine_ref, other_ref, index_ref, near_at(n), depth, True
            )
    for j in range(24):
        far, outer, inner = end_rows(mine_ref, other_ref, index_ref, j, True)
        blank = jnp.zeros_like(inner)
        ends_ref[j : j + 1, :CH] = jnp.where(far, blank, inner)
        ends_ref[j : j + 1, CH : 2 * CH] = outer
        ends_ref[j : j + 1, 2 * CH :] = jnp.where(far, inner, blank)
    strip_rows = 12 * EDGE
    triples(line_ref, line_cols_ref)
    line_cols_ref[strip_rows:, :] = ends_ref[...].astype(BF16)
    triples(deep_ref, deep_cols_ref)
    wide_ref[...] = dot(line_cols_ref[...], w2_adjoint_ref[: 3 * CH])
    strip_wide_ref[...] = dot(deep_cols_ref[...], w2_adjoint_ref[: 3 * CH]) + dot(
        line_cols_ref[:strip_rows, :], w2_adjoint_ref[3 * CH :]
    )
    cot_ref[...] = sent_ref[...]
    rims = []
    for n in range(12):
        side = index_ref[near_at(n) + 2]
        rows = slice(n * EDGE, (n + 1) * EDGE)
        rims.append(pick(wide_ref, n * EDGE, EDGE, side))
        cot_ref[rows, :] += pick(strip_wide_ref, n * EDGE, EDGE, side)
        for h in range(2):
            j = 2 * n + h
            at = n * EDGE + (0, EDGE - 1)[h]
            cot_ref[at : at + 1, :] += pick(
                wide_ref, strip_rows + j, 1, index_ref[lateral_at(j) + 2]
            )
    rims = turned(turn, jnp.concatenate(rims, axis=0))
    pad_ref[:, 1 : EDGE + 1, 1 : EDGE + 1, :] = inner_ref[...].reshape(tiles, EDGE, EDGE, CH)
    for n in range(12):
        side, k = n // tiles, n % tiles
        rows = rims[n * EDGE : (n + 1) * EDGE]
        put_side(pad_ref, k, side, edge_place(side), rows, add=True)
    middle = pad_ref[:, 1 : EDGE + 1, 1 : EDGE + 1, :]
    delta = gelu_slope(pre_ref[...]) * as_rows(middle)
    delta = delta.astype(BF16).astype(F32)
    pad_ref[:, 1 : EDGE + 1, 1 : EDGE + 1, :] = delta.reshape(tiles, EDGE, EDGE, CH)
    windows(pad_ref, cols_ref)
    strip_delta = (gelu_slope(strip_pre_ref[...]) * cot_ref[...]).astype(BF16).astype(F32)
    line_ref[:, 1 : EDGE + 1, :] = strip_delta.reshape(12, EDGE, CH)
    triples(line_ref, deep_cols_ref)
    strip_wide_ref[...] = dot(deep_cols_ref[...], w1_adjoint_ref[...])
    rims = []
    for n in range(12):
        rims.append(pick(strip_wide_ref, n * EDGE, EDGE, index_ref[near_at(n) + 2]))
    rims = turned(turn, jnp.concatenate(rims, axis=0))
    grad = dot(cols_ref[...], w1_back_ref[...])
    pad_ref[:, 1 : EDGE + 1, 1 : EDGE + 1, :] = grad.reshape(tiles, EDGE, EDGE, CH)
    for n in range(12):
        side, k = n // tiles, n % tiles
        rows = rims[n * EDGE : (n + 1) * EDGE]
        put_side(pad_ref, k, side, edge_place(side), rows, add=True)
    out_ref[...] = pad_ref[:, 1 : EDGE + 1, 1 : EDGE + 1, :].astype(BF16)


def pin_kernel(*refs):
    pass


def first_sum_kernel(pieces_ref, own_ref, across_ref, copies_ref, pair_ref):
    total = jnp.sum(pieces_ref[...].astype(F32), axis=0)
    for at in range(copies_ref.shape[0]):
        copies_ref[at] = total
    pair_ref[0] = own_ref[...]
    pair_ref[1] = across_ref[...]


def second_sum_kernel(pieces_ref, own_ref, one_ref, two_ref, three_ref, copies_ref, table_ref):
    total = jnp.sum(pieces_ref[...], axis=0).astype(BF16)
    for at in range(copies_ref.shape[0]):
        copies_ref[at] = total
    for at, part_ref in enumerate((own_ref, one_ref, two_ref, three_ref)):
        table_ref[at] = part_ref[...]


def finish_kernel(scale, mine_ref, other_ref, first_ref, second_ref, down_ref):
    core = lax.axis_index("c")
    for at in range(22):
        half = at // 11
        rows = slice(at % 11 * CH, (at % 11 + 1) * CH)
        block = jnp.where(core == half, mine_ref[rows, :], other_ref[rows, :])
        out_ref, base = ((first_ref, 0), (second_ref, 9), (down_ref, 18))[at // 9]
        out_ref[at - base] = block.astype(F32) * scale


def whole(space):
    return pl.BlockSpec(memory_space=space)


def shards(
    activations,
    conv1_weight,
    conv2_weight,
    coarse_kernel_weight,
    skip_cotangent,
    down_cotangent,
    face_neighbours,
    seam_codes,
    tile_slots,
):
    value_entries = activations[0]
    tiles = value_entries.shape[0]
    total_tiles = tile_slots.shape[0]
    cells = tiles * EDGE * EDGE
    strips = 4 * tiles * EDGE
    half = EDGE // 2
    smem, vmem = whole(pltpu.SMEM), whole(pltpu.VMEM)
    shape = jax.ShapeDtypeStruct
    params = pltpu.CompilerParams(vmem_limit_bytes=40 * 1024 * 1024)

    own_rings = rings(value_entries)
    mine = spread(own_rings, CHIPS)

    index, turn = pl.pallas_call(
        table_kernel,
        out_shape=(shape((288,), jnp.int32), shape((strips, strips), BF16)),
        in_specs=[smem] * 3,
        out_specs=(smem, vmem),
        compiler_params=params,
    )(face_neighbours, seam_codes, tile_slots)
    frames1 = side_frames(conv1_weight)
    frames2 = side_frames(conv2_weight)
    w1_sides = jnp.transpose(frames1, (1, 2, 3, 0, 4)).reshape(9 * CH, 4 * CH)
    w1_adjoint = frame_adjoint(frames1[:, :1])
    w2_adjoint = frame_adjoint(frames2[:, :2])
    w1_back = flipped(conv1_weight).reshape(9 * CH, CH)
    w2_back = flipped(conv2_weight).reshape(9 * CH, CH)
    wc_back = jnp.transpose(coarse_kernel_weight, (3, 0, 1, 2)).reshape(CH, 4 * CH)

    ready = [index, turn, w1_sides, w1_adjoint, w2_adjoint, w1_back, w2_back, wc_back]
    anywhere = whole(pl.ANY)
    mine = pl.pallas_call(
        pin_kernel,
        out_shape=shape(mine.shape, BF16),
        in_specs=[anywhere] * (1 + len(ready)),
        out_specs=anywhere,
        input_output_aliases={0: 0},
    )(mine, *ready)
    other = swap_core(mine)

    def table(block):
        return block.reshape((-1,) + own_rings.shape[1:])

    coarse, delta_rings, grads, pre, inner, strip_pre, sent = pl.pallas_call(
        forward_kernel,
        out_shape=(
            shape((tiles * half * half, CH), BF16),
            shape(own_rings.shape, BF16),
            shape((2, 11 * CH, CH), F32),
            shape((cells, CH), F32),
            shape((cells, CH), F32),
            shape((strips, CH), F32),
            shape((strips, CH), F32),
        ),
        in_specs=[smem] + [vmem] * 14,
        out_specs=(vmem,) * 7,
        scratch_shapes=[
            pltpu.VMEM((tiles, EDGE + 2, EDGE + 8, CH), F32),
            pltpu.VMEM((tiles, EDGE + 2, EDGE + 8, CH), F32),
            pltpu.VMEM((4 * tiles, 3, EDGE + 8, CH), F32),
            pltpu.VMEM((cells, 9 * CH), BF16),
            pltpu.VMEM((cells, 9 * CH), BF16),
            pltpu.VMEM((strips, 9 * CH), BF16),
            pltpu.VMEM((strips, 4 * CH), F32),
            pltpu.VMEM((strips, 4 * CH), BF16),
            pltpu.VMEM((4 * tiles, EDGE + 8, CH), F32),
            pltpu.VMEM((strips, 3 * CH), BF16),
            pltpu.VMEM((tiles, EDGE, EDGE, CH), F32),
            pltpu.VMEM((tiles * half * half, 4 * CH), BF16),
        ],
        compiler_params=params,
    )(
        index, turn, value_entries, own_rings, table(mine), table(other), skip_cotangent[0],
        down_cotangent.reshape(-1, CH), conv1_weight.reshape(9 * CH, CH), w1_sides,
        conv2_weight.reshape(9 * CH, CH), w2_back, w2_adjoint,
        coarse_kernel_weight.reshape(4 * CH, CH), wc_back,
    )
    across = swap_apart(delta_rings, "z", 1)
    kept = (grads[0] + swap_core(grads[1])).astype(BF16)
    plane = lax.axis_size(PLANE)
    part = kept.shape[0] // plane
    pieces = lax.all_to_all(kept.reshape(plane, part, CH), PLANE, 0, 0)
    deep = lax.axis_size(DEPTH)
    copies, pair = pl.pallas_call(
        first_sum_kernel,
        out_shape=(shape((deep, part, CH), F32), shape((2,) + delta_rings.shape, BF16)),
        in_specs=[vmem] * 3,
        out_specs=(vmem,) * 2,
        compiler_params=params,
    )(pieces, delta_rings, across)
    along = [swap_apart(pair, "y", apart) for apart in (1, 2, 3)]
    pieces = lax.all_to_all(copies, DEPTH, 0, 0)
    copies, mine = pl.pallas_call(
        second_sum_kernel,
        out_shape=(shape((plane, part, CH), BF16), shape((4,) + pair.shape, BF16)),
        in_specs=[vmem] * 5,
        out_specs=(vmem,) * 2,
        compiler_params=params,
    )(pieces, pair, *along)
    other = swap_core(mine)
    summed = lax.all_to_all(copies, PLANE, 0, 0).reshape(-1, CH)
    summed_other = swap_core(summed)
    input_grad = pl.pallas_call(
        backward_kernel,
        out_shape=shape(value_entries.shape, BF16),
        in_specs=[smem] + [vmem] * 10,
        out_specs=vmem,
        scratch_shapes=[
            pltpu.VMEM((tiles, EDGE + 2, EDGE + 8, CH), F32),
            pltpu.VMEM((cells, 9 * CH), BF16),
            pltpu.VMEM((4 * tiles, EDGE + 8, CH), F32),
            pltpu.VMEM((4 * tiles, EDGE + 8, CH), F32),
            pltpu.VMEM((strips + 32, 3 * CH), BF16),
            pltpu.VMEM((strips, 3 * CH), BF16),
            pltpu.VMEM((32, 3 * CH), F32),
            pltpu.VMEM((strips + 32, 4 * CH), F32),
            pltpu.VMEM((strips, 4 * CH), F32),
            pltpu.VMEM((strips, CH), F32),
        ],
        compiler_params=params,
    )(
        index, turn, table(mine), table(other), pre, inner, strip_pre, sent,
        w1_back, w1_adjoint, w2_adjoint,
    )
    scale = 1.0 / math.sqrt(lax.axis_size(("w", "x")) * total_tiles * EDGE * EDGE)
    first_grad, second_grad, down_grad = pl.pallas_call(
        functools.partial(finish_kernel, scale),
        out_shape=tuple(shape((count, CH, CH), F32) for count in (9, 9, 4)),
        in_specs=[vmem] * 2,
        out_specs=(vmem,) * 3,
        compiler_params=params,
    )(summed, summed_other)
    return (
        coarse.reshape((1, tiles, half, half, CH)),
        input_grad[None],
        first_grad.reshape(conv1_weight.shape),
        second_grad.reshape(conv2_weight.shape),
        down_grad.reshape(coarse_kernel_weight.shape),
    )


def solution(mesh):
    batch = mesh.shape["batch"]
    along_x = 4 if batch % 4 == 0 else 1
    fine = Mesh(
        mesh.devices.reshape(4, 2, 2, batch // along_x, along_x), ("y", "z", "c", "w", "x")
    )
    field = P(("w", "x"), ("y", "z", "c"), None, None, None)
    return jax.shard_map(
        shards,
        mesh=fine,
        in_specs=(field, P(), P(), P(), field, field, P(), P(), P()),
        out_specs=(field, field, P(), P(), P()),
        check_vma=False,
    )
```

```python
import functools
import math

import jax
import jax.numpy as jnp
from jax import lax
from jax.experimental import pallas as pl
from jax.experimental.pallas import tpu as pltpu
from jax.sharding import Mesh
from jax.sharding import PartitionSpec as P

PLANE = ("x", "y")
DEPTH = ("z", "w")
SLOPE = math.sqrt(2.0 / math.pi)
CUBIC = 0.044715
BF16 = jnp.bfloat16
F32 = jnp.float32
EDGE = 16
CH = 128


def swap_core(block):
    return lax.ppermute(block, "c", [(0, 1), (1, 0)])


def swap_apart(block, axis, apart):
    number = lax.axis_size(axis)
    return lax.ppermute(block, axis, [(i, i ^ apart) for i in range(number)])


def fetch(sources, targets, sems):
    copies = []
    for at, (source, target) in enumerate(zip(sources, targets)):
        copies.append(pltpu.make_async_copy(source, target, sems.at[at]))
        copies[-1].start()
    return copies


def finish(copies):
    for copy in copies:
        copy.wait()


def gelu(v):
    return 0.5 * v * (1.0 + jnp.tanh(SLOPE * (v + CUBIC * v * v * v)))


def gelu_slope(v):
    t = jnp.tanh(SLOPE * (v + CUBIC * v * v * v))
    return 0.5 * (1.0 + t) + (0.5 * SLOPE) * v * (1.0 - t * t) * (1.0 + (3.0 * CUBIC) * v * v)


def dot(left, right):
    return jnp.dot(left, right, preferred_element_type=F32)


def dot_rows(left, right):
    return lax.dot_general(left, right, (((0,), (0,)), ((), ())), preferred_element_type=F32)


def turned(turn, rows):
    high = rows.astype(BF16)
    low = (rows - high.astype(F32)).astype(BF16)
    return dot(turn, high) + dot(turn, low)


def as_rows(block):
    return block.reshape(-1, CH)


def lanes(at, count=1):
    return slice(at * CH, (at + count) * CH)


def strip(n):
    return slice(n * EDGE, (n + 1) * EDGE)


def as_cells(rows):
    return rows.reshape(-1, EDGE, EDGE, CH)


def fill_pad(pad_ref, rows):
    pad_ref[:, 1 : EDGE + 1, 1 : EDGE + 1, :] = as_cells(rows)


def windows(pad_ref, cols_ref):
    for a in range(3):
        for b in range(3):
            part = pad_ref[:, a : a + EDGE, b : b + EDGE, :].astype(BF16)
            cols_ref[:, lanes(3 * a + b)] = as_rows(part)


def triples(line_ref, cols_ref, order):
    for at, start in enumerate(order):
        part = line_ref[:, start : start + EDGE, :].astype(BF16)
        cols_ref[0 : line_ref.shape[0] * EDGE, lanes(at)] = as_rows(part)


def pick(rows_ref, at, count, side):
    chosen = pl.ds(pl.multiple_of(side * CH, CH), CH)
    return rows_ref[pl.ds(at, count), chosen]


def side_cells(tile, side, depth=0):
    near = (depth, EDGE - 1 - depth)[side in (1, 2)]
    if side % 2 == 0:
        return pl.ds(tile * EDGE * EDGE + near * EDGE, EDGE)
    return pl.ds(tile * EDGE * EDGE + near, EDGE, EDGE)


def add_sides(cells_ref, rows):
    for n in range(12):
        cells = side_cells(n % 3, n // 3)
        cells_ref[cells, :] = cells_ref[cells, :] + rows[strip(n)]


def put_seams(pad_ref, rows):
    for n in range(12):
        side, k = n // 3, n % 3
        place = (0, EDGE + 1, EDGE + 1, 0)[side]
        seam = rows[strip(n)]
        if side % 2 == 0:
            pad_ref[k, place, 1 : EDGE + 1, :] = seam
        else:
            for i in range(EDGE):
                pad_ref[k, 1 + i, place : place + 1, :] = seam[i : i + 1]


def near_at(n):
    return 8 * n


def lateral_at(j):
    return 96 + 8 * j


def frame_source(side, r, k):
    return ((r, k), (k, 2 - r), (2 - r, k), (k, r))[side]


def ring_kernel(x_ref, ring_ref, cells_ref):
    cells_ref[...] = as_rows(x_ref[...]).astype(F32)
    for n in range(12):
        for depth in range(2):
            rows = cells_ref[side_cells(n % 3, n // 3, depth), :].astype(BF16)
            ring_ref[n % 3, n // 3, depth] = rows


W1_SIDES, W2, TAIL, X = (slice(0, 512), slice(512, 640), slice(640, 768), slice(768, 896))
W2_BACK, W1_BACK, ADJOINT = slice(0, 128), slice(128, 256), slice(256, 768)


def stage_kernel(
    near_ref, code_ref, slot_ref, x_hbm, skip_hbm, down_hbm, w1_hbm, w2_hbm, wc_hbm,
    index_ref, turn_hbm, early_hbm, late_hbm, cells_hbm,
    x_ref, skip_ref, down_ref, w1_ref, w2_ref, wc_ref,
    turn_ref, early_ref, late_ref, cells_ref,
    pad_ref, cot_ref, cols_ref, wc_back_ref, in_sems, out_sems,
):
    arrivals = fetch(
        (w1_hbm, w2_hbm, wc_hbm, x_hbm, down_hbm, skip_hbm),
        (w1_ref, w2_ref, wc_ref, x_ref, down_ref, skip_ref),
        in_sems,
    )
    pad_ref[...] = jnp.zeros_like(pad_ref)
    early_ref[704:, TAIL] = jnp.zeros_like(early_ref[704:, TAIL])
    early_ref[768:, X] = jnp.zeros_like(early_ref[768:, X])
    total = slot_ref.shape[0]
    tiles = 3
    core = lax.axis_index("c")
    at_y = lax.axis_index("y")
    at_z = lax.axis_index("z")
    first = ((at_y * 2 + at_z) * 2 + core) * tiles

    def look(i, found):
        here = slot_ref[i]
        return tuple(jnp.where(here == first + k, i, found[k]) for k in range(tiles))

    own = lax.fori_loop(0, total, look, (jnp.int32(0),) * tiles)

    def place(at, tile):
        slot = slot_ref[tile]
        owner = slot // tiles
        local = slot % tiles
        chip = ((owner // 4) ^ at_y) * 2 + ((owner // 2) % 2 ^ at_z)
        index_ref[at] = (owner + core) % 2
        index_ref[at + 1] = chip * tiles + local

    column = lax.broadcasted_iota(jnp.int32, (EDGE, 12 * EDGE), 1)
    row = lax.broadcasted_iota(jnp.int32, (EDGE, 12 * EDGE), 0)
    for n in range(12):
        side, k = n // tiles, n % tiles
        near = near_ref[side, own[k]]
        code = code_ref[side, own[k]]
        near_side = code // 2
        reverse = code % 2
        place(near_at(n), near)
        index_ref[near_at(n) + 2] = near_side
        source = jnp.where(reverse == 1, EDGE - 1 - row, row) + n * EDGE
        turn_ref[strip(n), :] = jnp.where(column == source, 1.0, 0.0).astype(F32).astype(BF16)
        upright = near_side % 2
        far = jnp.where((near_side == 1) | (near_side == 2), 1, 0)
        for h in range(2):
            lateral = jnp.where(upright == 1, (0, 2)[h], (3, 1)[h])
            at = lateral_at(2 * n + h)
            place(at, near_ref[lateral, near])
            lateral_code = code_ref[lateral, near]
            index_ref[at + 2] = lateral_code // 2
            index_ref[at + 3] = (far + lateral_code) % 2

    finish(arrivals)

    def flip(block):
        return jnp.transpose(block.astype(F32)).astype(BF16)

    for a in range(3):
        for b in range(3):
            block = w1_ref[lanes(3 * a + b), :]
            first_flip = flip(block)
            second_flip = flip(w2_ref[lanes(3 * a + b), :])
            back = lanes(8 - 3 * a - b)
            late_ref[back, W1_BACK] = first_flip
            late_ref[back, W2_BACK] = second_flip
            for side in range(4):
                for r in range(3):
                    for k in range(3):
                        if frame_source(side, r, k) != (a, b):
                            continue
                        early_ref[lanes(3 * r + k), lanes(side)] = block
                        if r == 0:
                            late_ref[lanes(6 + k), lanes(2 + side)] = first_flip
                        if r <= 1:
                            late_ref[lanes(3 * r + k), lanes(2 + side)] = second_flip
    early_ref[:, W2] = w2_ref[...]
    early_ref[:512, TAIL] = wc_ref[...]
    down = down_ref[...]
    early_ref[512:704, TAIL] = down
    x_rows = as_rows(x_ref[...])
    early_ref[:768, X] = x_rows
    departures = fetch(
        (early_ref, late_ref, turn_ref), (early_hbm, late_hbm, turn_hbm), out_sems
    )
    for at in range(4):
        wc_back_ref[:, lanes(at)] = flip(wc_ref[lanes(at), :])
    spread_down = dot(down, wc_back_ref[...])
    half = EDGE // 2
    for a in range(2):
        for b in range(2):
            part = spread_down[:, lanes(2 * a + b)].reshape(tiles, half, half, CH)
            cot_ref[:, pl.ds(a, half, 2), pl.ds(b, half, 2), :] = part
    cells_ref[:, lanes(1)] = as_rows(cot_ref[...] + skip_ref[...].astype(F32))
    fill_pad(pad_ref, x_rows.astype(F32))
    windows(pad_ref, cols_ref)
    cells_ref[:, lanes(0)] = dot(cols_ref[...], w1_ref[...])
    last = pltpu.make_async_copy(cells_ref, cells_hbm, out_sems.at[3])
    last.start()
    finish(departures + [last])


def table_row(mine_ref, other_ref, index_ref, at, depth):
    slot = index_ref[at + 1]
    side = index_ref[at + 2]
    mine = mine_ref[slot, side, depth]
    other = other_ref[slot, side, depth]
    return jnp.where(index_ref[at] == 0, mine.astype(F32), other.astype(F32))


def end_rows(mine_ref, other_ref, index_ref, j):
    row = table_row(mine_ref, other_ref, index_ref, lateral_at(j), 0)
    far = index_ref[lateral_at(j) + 3] == 1
    last = EDGE - 1
    return far, jnp.where(far, row[last:], row[:1]), jnp.where(far, row[last - 1 : last], row[1:2])


def forward_kernel(
    index_ref, turn_ref, mine_ref, other_ref, early_ref, staged_ref,
    coarse_ref, delta_ring_ref, pre_ref, strip_pre_ref, seam_ref, cols2_ref, strip_ref,
    down_cols_ref, delta_ref, line_ref,
    pad_ref, patch_ref, wide_ref, fine_ref, cells_ref, line_cols_ref,
):
    tiles = 3
    patch_ref[...] = jnp.zeros_like(patch_ref)
    pad_ref[...] = jnp.zeros_like(pad_ref)
    line_ref[...] = jnp.zeros_like(line_ref)
    turn = turn_ref[...]
    near = []
    own = []
    for n in range(12):
        own.append(mine_ref[n % tiles, n // tiles, 0])
        edge = table_row(mine_ref, other_ref, index_ref, near_at(n), 0)
        near.append(edge)
        patch_ref[n, 1, 1 : EDGE + 1, :] = edge
        patch_ref[n, 2, 1 : EDGE + 1, :] = table_row(
            mine_ref, other_ref, index_ref, near_at(n), 1
        )
        for h in range(2):
            _, outer, inner = end_rows(mine_ref, other_ref, index_ref, 2 * n + h)
            at = (0, EDGE + 1)[h]
            patch_ref[n, 1, at : at + 1, :] = outer
            patch_ref[n, 2, at : at + 1, :] = inner
    seams = dot(turn, jnp.concatenate(near, axis=0).astype(BF16))
    seam_ref[...] = seams
    own_turned = dot(turn, jnp.concatenate(own, axis=0))
    patch_ref[:, 0, 1 : EDGE + 1, :] = own_turned.reshape(12, EDGE, CH)
    for r in range(3):
        for b in range(3):
            part = patch_ref[:, r, b : b + EDGE, :].astype(BF16)
            strip_ref[:, lanes(3 * r + b)] = as_rows(part)
    wide_ref[...] = dot(strip_ref[...], early_ref[:, W1_SIDES])
    for n in range(12):
        strip_pre_ref[strip(n), :] = pick(wide_ref, n * EDGE, EDGE, index_ref[near_at(n) + 2])
    line_ref[:, 1 : EDGE + 1, :] = seams.reshape(12, EDGE, CH)
    triples(line_ref, line_cols_ref, (0, 1, 2))
    pre_ref[...] = staged_ref[:, lanes(0)]
    parts = []
    for side in range(4):
        rows = slice(side * tiles * EDGE, (side + 1) * tiles * EDGE)
        parts.append(dot(line_cols_ref[rows, :], early_ref[: 3 * CH, lanes(side)]))
    add_sides(pre_ref, jnp.concatenate(parts, axis=0))
    fill_pad(pad_ref, gelu(pre_ref[...]).astype(BF16).astype(F32))
    put_seams(pad_ref, dot(turn, gelu(strip_pre_ref[...]).astype(BF16)))
    windows(pad_ref, cols2_ref)
    second_pre = dot(cols2_ref[...], early_ref[:, W2])
    delta = (gelu_slope(second_pre) * staged_ref[:, lanes(1)]).astype(BF16)
    delta_ref[...] = delta
    cells_ref[...] = delta.astype(F32)
    for n in range(12):
        for depth in range(2):
            rows = cells_ref[side_cells(n % tiles, n // tiles, depth), :]
            delta_ring_ref[n % tiles, n // tiles, depth] = rows.astype(BF16)
            if depth == 0:
                line_ref[n, 1 : EDGE + 1, :] = rows
    fine_ref[...] = as_cells(gelu(second_pre).astype(BF16).astype(F32))
    half = EDGE // 2
    for a in range(2):
        for b in range(2):
            part = fine_ref[:, pl.ds(a, half, 2), pl.ds(b, half, 2), :]
            down_cols_ref[:, lanes(2 * a + b)] = as_rows(part).astype(BF16)
    coarse_ref[...] = dot(down_cols_ref[...], early_ref[:512, TAIL]).astype(BF16)


def gradient_kernel(
    index_ref, turn_ref, early_ref, late_ref, pre_ref, strip_pre_ref, seam_ref, cols2_ref, strip_ref, down_cols_ref, delta_ref, line_ref,
    grad_ref, rest_ref,
    pad_ref, cols_ref, cols3_ref, split_ref, line_cols_ref,
):
    tiles = 3
    core = lax.axis_index("c")

    def put_grad(at, block):
        half = at // 11
        grad_ref[jnp.where(core == half, 0, 1), lanes(at % 11), :] = block

    split_ref[...] = jnp.zeros_like(split_ref)
    turn = turn_ref[...]
    down_grad = dot_rows(down_cols_ref[...], early_ref[512:704, TAIL])
    for at in range(4):
        put_grad(18 + at, down_grad[lanes(at)])
    delta = delta_ref[...]
    second_grad = dot_rows(cols2_ref[...], delta)
    for at in range(9):
        put_grad(9 + at, second_grad[lanes(at)])
    pad_ref[...] = jnp.zeros_like(pad_ref)
    fill_pad(pad_ref, delta.astype(F32))
    windows(pad_ref, cols3_ref)
    inner = dot(cols3_ref[...], late_ref[:, W2_BACK])
    rest_ref[:768, lanes(0)] = pre_ref[...]
    rest_ref[:768, lanes(1)] = inner
    inner_delta = (gelu_slope(pre_ref[...]) * inner).astype(BF16)
    triples(line_ref, line_cols_ref, (2, 1, 0))
    rims = []
    for side in range(4):
        rows = slice(side * tiles * EDGE, (side + 1) * tiles * EDGE)
        rims.append(dot(line_cols_ref[rows, :], late_ref[: 3 * CH, lanes(2 + side)]))
    sent = turned(turn, jnp.concatenate(rims, axis=0))
    rest_ref[768:, lanes(0)] = strip_pre_ref[...]
    rest_ref[768:, lanes(1)] = sent
    sent_delta = (gelu_slope(strip_pre_ref[...]) * sent).astype(BF16)
    for n in range(12):
        chosen = pl.ds(pl.multiple_of(index_ref[near_at(n) + 2] * CH, CH), CH)
        split_ref[strip(n), chosen] = sent_delta[strip(n)]
    sent_grad = dot_rows(strip_ref[...], split_ref[...])
    fill_pad(pad_ref, early_ref[:768, X].astype(F32))
    put_seams(pad_ref, seam_ref[...])
    windows(pad_ref, cols_ref)
    first_grad = dot_rows(cols_ref[...], inner_delta)
    for a in range(3):
        for b in range(3):
            block = first_grad[lanes(3 * a + b)]
            for side in range(4):
                for r in range(3):
                    for k in range(3):
                        if frame_source(side, r, k) == (a, b):
                            block = block + sent_grad[lanes(3 * r + k), lanes(side)]
            put_grad(3 * a + b, block)


def backward_kernel(
    index_ref, turn_ref, mine_ref, other_ref, late_ref, rest_ref,
    out_ref, flag_ref,
    pad_ref, cols_ref, line_ref, deep_ref, line_cols_ref, deep_cols_ref, ends_ref, wide_ref,
    strip_wide_ref, cot_ref, cells_ref,
):
    flag_ref[...] = jnp.zeros_like(flag_ref)
    turn = turn_ref[...]
    line_ref[...] = jnp.zeros_like(line_ref)
    deep_ref[...] = jnp.zeros_like(deep_ref)
    ends_ref[...] = jnp.zeros_like(ends_ref)
    pad_ref[...] = jnp.zeros_like(pad_ref)
    for n in range(12):
        for depth, rows_ref in ((0, line_ref), (1, deep_ref)):
            rows_ref[n, 1 : EDGE + 1, :] = table_row(
                mine_ref, other_ref, index_ref, near_at(n), depth
            )
    for j in range(24):
        far, outer, inner = end_rows(mine_ref, other_ref, index_ref, j)
        blank = jnp.zeros_like(inner)
        ends_ref[j : j + 1, lanes(0)] = jnp.where(far, blank, inner)
        ends_ref[j : j + 1, lanes(1)] = outer
        ends_ref[j : j + 1, lanes(2)] = jnp.where(far, inner, blank)
    strip_rows = 12 * EDGE
    triples(line_ref, line_cols_ref, (2, 1, 0))
    line_cols_ref[strip_rows:, :] = ends_ref[...].astype(BF16)
    triples(deep_ref, deep_cols_ref, (2, 1, 0))
    wide_ref[...] = dot(line_cols_ref[...], late_ref[: 3 * CH, ADJOINT])
    strip_wide_ref[...] = dot(deep_cols_ref[...], late_ref[: 3 * CH, ADJOINT]) + dot(
        line_cols_ref[:strip_rows, :], late_ref[3 * CH : 6 * CH, ADJOINT]
    )
    cot_ref[...] = rest_ref[768:, lanes(1)]
    rims = []
    for n in range(12):
        side = index_ref[near_at(n) + 2]
        rims.append(pick(wide_ref, n * EDGE, EDGE, side))
        cot_ref[strip(n), :] += pick(strip_wide_ref, n * EDGE, EDGE, side)
        for h in range(2):
            j = 2 * n + h
            at = n * EDGE + (0, EDGE - 1)[h]
            cot_ref[at : at + 1, :] += pick(
                wide_ref, strip_rows + j, 1, index_ref[lateral_at(j) + 2]
            )
    cells_ref[...] = rest_ref[:768, lanes(1)]
    add_sides(cells_ref, turned(turn, jnp.concatenate(rims, axis=0)))
    delta = gelu_slope(rest_ref[:768, lanes(0)]) * cells_ref[...]
    fill_pad(pad_ref, delta.astype(BF16).astype(F32))
    windows(pad_ref, cols_ref)
    strip_delta = (gelu_slope(rest_ref[768:, lanes(0)]) * cot_ref[...]).astype(BF16).astype(F32)
    line_ref[:, 1 : EDGE + 1, :] = strip_delta.reshape(12, EDGE, CH)
    triples(line_ref, deep_cols_ref, (2, 1, 0))
    strip_wide_ref[...] = dot(deep_cols_ref[...], late_ref[6 * CH :, ADJOINT])
    rims = []
    for n in range(12):
        rims.append(pick(strip_wide_ref, n * EDGE, EDGE, index_ref[near_at(n) + 2]))
    cells_ref[...] = dot(cols_ref[...], late_ref[:, W1_BACK])
    add_sides(cells_ref, turned(turn, jnp.concatenate(rims, axis=0)))
    out_ref[...] = as_cells(cells_ref[...]).astype(BF16)


def first_pair_kernel(own_ref, across_ref, pair_ref):
    pair_ref[0] = own_ref[...]
    pair_ref[1] = across_ref[...]


def first_table_kernel(own_ref, one_ref, two_ref, three_ref, index_ref, table_ref):
    for at, part_ref in enumerate((own_ref, one_ref, two_ref, three_ref)):
        table_ref[at] = part_ref[...]


def pair_kernel(own_ref, across_ref, grads_ref, pair_ref, give_ref):
    pair_ref[0] = own_ref[...]
    pair_ref[1] = across_ref[...]
    give_ref[...] = grads_ref[1]


def table_kernel(own_ref, one_ref, two_ref, three_ref, table_ref):
    for at, part_ref in enumerate((own_ref, one_ref, two_ref, three_ref)):
        table_ref[at] = part_ref[...]


def spread_sum(pieces_ref, copies_ref):
    total = jnp.sum(pieces_ref[...].astype(F32), axis=0).astype(BF16)
    for at in range(copies_ref.shape[0]):
        copies_ref[at] = total


def first_sum_kernel(pieces_ref, table_ref, copies_ref, out_ref):
    spread_sum(pieces_ref, copies_ref)
    out_ref[...] = table_ref[...]


def second_sum_kernel(pieces_ref, flag_ref, copies_ref):
    spread_sum(pieces_ref, copies_ref)


def finish_kernel(scale, mine_ref, other_ref, first_ref, second_ref, down_ref):
    core = lax.axis_index("c")
    for at in range(22):
        half = at // 11
        rows = slice(at % 11 * CH, (at % 11 + 1) * CH)
        block = jnp.where(core == half, mine_ref[rows, :], other_ref[rows, :])
        out_ref, base = ((first_ref, 0), (second_ref, 9), (down_ref, 18))[at // 9]
        out_ref[at - base] = block.astype(F32) * scale


def whole(space):
    return pl.BlockSpec(memory_space=space)


def shards(
    activations,
    conv1_weight,
    conv2_weight,
    coarse_kernel_weight,
    skip_cotangent,
    down_cotangent,
    face_neighbours,
    seam_codes,
    tile_slots,
):
    x = activations[0]
    tiles = x.shape[0]
    total_tiles = tile_slots.shape[0]
    cells = tiles * EDGE * EDGE
    strips = 4 * tiles * EDGE
    half = EDGE // 2
    quarter = tiles * half * half
    smem, vmem, hbm = whole(pltpu.SMEM), whole(pltpu.VMEM), whole(pltpu.HBM)
    shape = jax.ShapeDtypeStruct
    plane = lax.axis_size(PLANE)
    deep = lax.axis_size(DEPTH)
    pad = shape((tiles, EDGE + 2, EDGE + 8, CH), F32)
    line = shape((4 * tiles, EDGE + 8, CH), F32)
    ring = shape((tiles, 4, 2, EDGE, CH), BF16)

    def call(
        kernel, outs, operands, scratch=(), sems=(), specs=None, out_specs=None, cost=1, room=24
    ):
        single = not isinstance(outs, tuple)
        scratch = [pltpu.VMEM(one.shape, one.dtype) for one in scratch]
        scratch += [pltpu.SemaphoreType.DMA((count,)) for count in sems]
        return pl.pallas_call(
            kernel,
            out_shape=outs,
            in_specs=specs or [vmem] * len(operands),
            out_specs=out_specs or (vmem if single else (vmem,) * len(outs)),
            scratch_shapes=scratch,
            compiler_params=pltpu.CompilerParams(vmem_limit_bytes=room * 1024 * 1024),
            cost_estimate=pl.CostEstimate(
                flops=cost * cells * 18 * CH * CH, bytes_accessed=2 * 1024 * 1024, transcendentals=0
            ),
        )(*operands)

    wide = shape((strips, 4 * CH), F32)
    all_cols = shape((cells, 9 * CH), BF16)
    cell_rows = shape((cells, CH), F32)
    strip_rows = shape((strips, CH), F32)
    flag = shape((8, CH), F32)
    own_ring = call(ring_kernel, ring, [x], [cell_rows])
    across = swap_apart(own_ring, "z", 1)
    operands = [
        x,
        skip_cotangent[0],
        down_cotangent.reshape(-1, CH),
        conv1_weight.reshape(9 * CH, CH),
        conv2_weight.reshape(9 * CH, CH),
        coarse_kernel_weight.reshape(4 * CH, CH),
    ]
    staged = (
        shape((strips, strips), BF16),
        shape((9 * CH, 7 * CH), BF16),
        shape((9 * CH, 6 * CH), BF16),
        shape((cells, 2 * CH), F32),
    )
    index, turn, early, late, staged_cells = call(
        stage_kernel,
        (shape((296,), jnp.int32),) + staged,
        [face_neighbours.T, seam_codes.T, tile_slots] + operands,
        tuple(operands) + staged
        + (pad, shape(x.shape, F32), all_cols, shape((CH, 4 * CH), BF16)),
        (len(operands), len(staged)),
        specs=[smem] * 3 + [hbm] * 6,
        out_specs=(smem,) + (hbm,) * 4,
        cost=4,
        room=60,
    )
    pair = call(first_pair_kernel, shape((2,) + ring.shape, BF16), [own_ring, across])
    along = [swap_apart(pair, "y", apart) for apart in (1, 2, 3)]
    mine = call(
        first_table_kernel,
        shape((4,) + pair.shape, BF16),
        [pair] + along + [index],
        specs=[vmem] * 4 + [smem],
    )
    other = swap_core(mine)

    def table(block):
        return block.reshape((-1,) + ring.shape[1:])

    (
        coarse, delta_ring, pre, strip_pre, seam, cols2, strip_cols, down_cols, delta, line_rows,
    ) = call(
        forward_kernel,
        (
            shape((quarter, CH), BF16),
            ring,
            cell_rows,
            strip_rows,
            strip_rows,
            all_cols,
            shape((strips, 9 * CH), BF16),
            shape((quarter, 4 * CH), BF16),
            shape((cells, CH), BF16),
            line,
        ),
        [index, turn, table(mine), table(other), early, staged_cells],
        [
            pad,
            shape((4 * tiles, 3, EDGE + 8, CH), F32),
            wide,
            shape(x.shape, F32),
            cell_rows,
            shape((strips, 3 * CH), BF16),
        ],
        specs=[smem] + [vmem] * 5,
        cost=2,
    )
    across = swap_apart(delta_ring, "z", 1)
    grads, rest = call(
        gradient_kernel,
        (shape((2, 11 * CH, CH), F32), shape((cells + strips, 2 * CH), F32)),
        [
            index, turn, early, late, pre, strip_pre, seam, cols2, strip_cols, down_cols, delta,
            line_rows,
        ],
        [
            pad,
            all_cols,
            all_cols,
            shape((strips, 4 * CH), BF16),
            shape((strips, 3 * CH), BF16),
        ],
        specs=[smem] + [vmem] * 11,
        cost=4,
    )
    pair, give = call(
        pair_kernel,
        (shape((2,) + ring.shape, BF16), shape(grads.shape[1:], F32)),
        [delta_ring, across, grads],
    )
    kept = (grads[0] + swap_core(give)).astype(BF16)
    along = [swap_apart(pair, "y", apart) for apart in (1, 2, 3)]
    part = kept.shape[0] // plane
    pieces = lax.all_to_all(kept.reshape(plane, part, CH), PLANE, 0, 0)
    mine = call(table_kernel, shape((4,) + pair.shape, BF16), [pair] + along, cost=100)
    copies, mine = call(
        first_sum_kernel,
        (shape((deep, part, CH), BF16), shape(mine.shape, BF16)),
        [pieces, mine],
    )
    other = swap_core(mine)
    pieces = lax.all_to_all(copies, DEPTH, 0, 0)
    input_grad, done = call(
        backward_kernel,
        (shape(x.shape, BF16), flag),
        [index, turn, table(mine), table(other), late, rest],
        [
            pad,
            all_cols,
            line,
            line,
            shape((strips + 32, 3 * CH), BF16),
            shape((strips, 3 * CH), BF16),
            shape((32, 3 * CH), F32),
            shape((strips + 32, 4 * CH), F32),
            wide,
            strip_rows,
            cell_rows,
        ],
        specs=[smem] + [vmem] * 5,
        cost=4,
    )
    copies = call(second_sum_kernel, shape((plane, part, CH), BF16), [pieces, done])
    summed = lax.all_to_all(copies, PLANE, 0, 0).reshape(-1, CH)
    scale = 1.0 / math.sqrt(lax.axis_size(("w", "x")) * total_tiles * EDGE * EDGE)
    first_grad, second_grad, down_grad = call(
        functools.partial(finish_kernel, scale),
        tuple(shape((count, CH, CH), F32) for count in (9, 9, 4)),
        [summed, swap_core(summed)],
    )
    return (
        coarse.reshape((1, tiles, half, half, CH)),
        input_grad[None],
        first_grad.reshape(conv1_weight.shape),
        second_grad.reshape(conv2_weight.shape),
        down_grad.reshape(coarse_kernel_weight.shape),
    )


def solution(mesh):
    batch = mesh.shape["batch"]
    along_x = 4 if batch % 4 == 0 else 1
    fine = Mesh(
        mesh.devices.reshape(4, 2, 2, batch // along_x, along_x), ("y", "z", "c", "w", "x")
    )
    field = P(("w", "x"), ("y", "z", "c"), None, None, None)
    return jax.shard_map(
        shards,
        mesh=fine,
        in_specs=(field, P(), P(), P(), field, field, P(), P(), P()),
        out_specs=(field, field, P(), P(), P()),
        check_vma=False,
    )
```

```python
import functools
import math

import jax
import jax.numpy as jnp
from jax import lax
from jax.experimental import pallas as pl
from jax.experimental.pallas import tpu as pltpu
from jax.sharding import Mesh
from jax.sharding import PartitionSpec as P

PLANE = ("x", "y")
DEPTH = ("z", "w")
SLOPE = math.sqrt(2.0 / math.pi)
CUBIC = 0.044715
BF16 = jnp.bfloat16
F32 = jnp.float32
EDGE = 16
CH = 128


def swap_core(block):
    return lax.ppermute(block, "c", [(0, 1), (1, 0)])


def swap_apart(block, axis, apart):
    number = lax.axis_size(axis)
    return lax.ppermute(block, axis, [(i, i ^ apart) for i in range(number)])


def fetch(sources, targets, sems):
    copies = []
    for at, (source, target) in enumerate(zip(sources, targets)):
        copies.append(pltpu.make_async_copy(source, target, sems.at[at]))
        copies[-1].start()
    return copies


def finish(copies):
    for copy in copies:
        copy.wait()


def gelu(v):
    return 0.5 * v * (1.0 + jnp.tanh(SLOPE * (v + CUBIC * v * v * v)))


def gelu_slope(v):
    t = jnp.tanh(SLOPE * (v + CUBIC * v * v * v))
    return 0.5 * (1.0 + t) + (0.5 * SLOPE) * v * (1.0 - t * t) * (1.0 + (3.0 * CUBIC) * v * v)


def dot(left, right):
    return jnp.dot(left, right, preferred_element_type=F32)


def dot_rows(left, right):
    return lax.dot_general(left, right, (((0,), (0,)), ((), ())), preferred_element_type=F32)


def turned(turn, rows):
    high = rows.astype(BF16)
    low = (rows - high.astype(F32)).astype(BF16)
    return dot(turn, high) + dot(turn, low)


def as_rows(block):
    return block.reshape(-1, CH)


def lanes(at, count=1):
    return slice(at * CH, (at + count) * CH)


def strip(n):
    return slice(n * EDGE, (n + 1) * EDGE)


def as_cells(rows):
    return rows.reshape(-1, EDGE, EDGE, CH)


def fill_pad(pad_ref, rows):
    pad_ref[:, 1 : EDGE + 1, 1 : EDGE + 1, :] = as_cells(rows)


def windows(pad_ref, cols_ref):
    for a in range(3):
        for b in range(3):
            part = pad_ref[:, a : a + EDGE, b : b + EDGE, :].astype(BF16)
            cols_ref[:, lanes(3 * a + b)] = as_rows(part)


def triples(line_ref, cols_ref, order):
    for at, start in enumerate(order):
        part = line_ref[:, start : start + EDGE, :].astype(BF16)
        cols_ref[0 : line_ref.shape[0] * EDGE, lanes(at)] = as_rows(part)


def pick(rows_ref, at, count, side):
    chosen = pl.ds(pl.multiple_of(side * CH, CH), CH)
    return rows_ref[pl.ds(at, count), chosen]


def side_cells(tile, side, depth=0):
    near = (depth, EDGE - 1 - depth)[side in (1, 2)]
    if side % 2 == 0:
        return pl.ds(tile * EDGE * EDGE + near * EDGE, EDGE)
    return pl.ds(tile * EDGE * EDGE + near, EDGE, EDGE)


def add_sides(cells_ref, rows):
    for n in range(12):
        cells = side_cells(n % 3, n // 3)
        cells_ref[cells, :] = cells_ref[cells, :] + rows[strip(n)]


def put_seams(pad_ref, rows):
    for n in range(12):
        side, k = n // 3, n % 3
        place = (0, EDGE + 1, EDGE + 1, 0)[side]
        seam = rows[strip(n)]
        if side % 2 == 0:
            pad_ref[k, place, 1 : EDGE + 1, :] = seam
        else:
            for i in range(EDGE):
                pad_ref[k, 1 + i, place : place + 1, :] = seam[i : i + 1]


def near_at(n):
    return 8 * n


def lateral_at(j):
    return 96 + 8 * j


def frame_source(side, r, k):
    return ((r, k), (k, 2 - r), (2 - r, k), (k, r))[side]


def ring_kernel(x_ref, ring_ref, cells_ref):
    cells_ref[...] = as_rows(x_ref[...]).astype(F32)
    for n in range(12):
        for depth in range(2):
            rows = cells_ref[side_cells(n % 3, n // 3, depth), :].astype(BF16)
            ring_ref[n % 3, n // 3, depth] = rows


W1_SIDES, W2, TAIL, X = (slice(0, 512), slice(512, 640), slice(640, 768), slice(768, 896))
W2_BACK, W1_BACK, ADJOINT = slice(0, 128), slice(128, 256), slice(256, 768)


def stage_kernel(
    near_ref, code_ref, slot_ref, x_hbm, skip_hbm, down_hbm, w1_hbm, w2_hbm, wc_hbm,
    index_ref, turn_hbm, early_hbm, late_hbm, cells_hbm,
    x_ref, skip_ref, down_ref, w1_ref, w2_ref, wc_ref,
    turn_ref, early_ref, late_ref, cells_ref,
    pad_ref, cot_ref, cols_ref, wc_back_ref, in_sems, out_sems,
):
    arrivals = fetch(
        (w1_hbm, w2_hbm, wc_hbm, x_hbm, down_hbm, skip_hbm),
        (w1_ref, w2_ref, wc_ref, x_ref, down_ref, skip_ref),
        in_sems,
    )
    pad_ref[...] = jnp.zeros_like(pad_ref)
    early_ref[704:, TAIL] = jnp.zeros_like(early_ref[704:, TAIL])
    early_ref[768:, X] = jnp.zeros_like(early_ref[768:, X])
    total = slot_ref.shape[0]
    tiles = 3
    core = lax.axis_index("c")
    at_y = lax.axis_index("y")
    at_z = lax.axis_index("z")
    first = ((at_y * 2 + at_z) * 2 + core) * tiles

    def look(i, found):
        here = slot_ref[i]
        return tuple(jnp.where(here == first + k, i, found[k]) for k in range(tiles))

    own = lax.fori_loop(0, total, look, (jnp.int32(0),) * tiles)

    def place(at, tile):
        slot = slot_ref[tile]
        owner = slot // tiles
        local = slot % tiles
        chip = ((owner // 4) ^ at_y) * 2 + ((owner // 2) % 2 ^ at_z)
        index_ref[at] = (owner + core) % 2
        index_ref[at + 1] = chip * tiles + local

    column = lax.broadcasted_iota(jnp.int32, (EDGE, 12 * EDGE), 1)
    row = lax.broadcasted_iota(jnp.int32, (EDGE, 12 * EDGE), 0)
    for n in range(12):
        side, k = n // tiles, n % tiles
        near = near_ref[side, own[k]]
        code = code_ref[side, own[k]]
        near_side = code // 2
        reverse = code % 2
        place(near_at(n), near)
        index_ref[near_at(n) + 2] = near_side
        source = jnp.where(reverse == 1, EDGE - 1 - row, row) + n * EDGE
        turn_ref[strip(n), :] = jnp.where(column == source, 1.0, 0.0).astype(F32).astype(BF16)
        upright = near_side % 2
        far = jnp.where((near_side == 1) | (near_side == 2), 1, 0)
        for h in range(2):
            lateral = jnp.where(upright == 1, (0, 2)[h], (3, 1)[h])
            at = lateral_at(2 * n + h)
            place(at, near_ref[lateral, near])
            lateral_code = code_ref[lateral, near]
            index_ref[at + 2] = lateral_code // 2
            index_ref[at + 3] = (far + lateral_code) % 2

    finish(arrivals)

    def flip(block):
        return jnp.transpose(block.astype(F32)).astype(BF16)

    for a in range(3):
        for b in range(3):
            block = w1_ref[lanes(3 * a + b), :]
            first_flip = flip(block)
            second_flip = flip(w2_ref[lanes(3 * a + b), :])
            back = lanes(8 - 3 * a - b)
            late_ref[back, W1_BACK] = first_flip
            late_ref[back, W2_BACK] = second_flip
            for side in range(4):
                for r in range(3):
                    for k in range(3):
                        if frame_source(side, r, k) != (a, b):
                            continue
                        early_ref[lanes(3 * r + k), lanes(side)] = block
                        if r == 0:
                            late_ref[lanes(6 + k), lanes(2 + side)] = first_flip
                        if r <= 1:
                            late_ref[lanes(3 * r + k), lanes(2 + side)] = second_flip
    early_ref[:, W2] = w2_ref[...]
    early_ref[:512, TAIL] = wc_ref[...]
    down = down_ref[...]
    early_ref[512:704, TAIL] = down
    x_rows = as_rows(x_ref[...])
    early_ref[:768, X] = x_rows
    departures = fetch(
        (early_ref, late_ref, turn_ref), (early_hbm, late_hbm, turn_hbm), out_sems
    )
    for at in range(4):
        wc_back_ref[:, lanes(at)] = flip(wc_ref[lanes(at), :])
    spread_down = dot(down, wc_back_ref[...])
    half = EDGE // 2
    for a in range(2):
        for b in range(2):
            part = spread_down[:, lanes(2 * a + b)].reshape(tiles, half, half, CH)
            cot_ref[:, pl.ds(a, half, 2), pl.ds(b, half, 2), :] = part
    cells_ref[:, lanes(1)] = as_rows(cot_ref[...] + skip_ref[...].astype(F32))
    fill_pad(pad_ref, x_rows.astype(F32))
    windows(pad_ref, cols_ref)
    cells_ref[:, lanes(0)] = dot(cols_ref[...], w1_ref[...])
    last = pltpu.make_async_copy(cells_ref, cells_hbm, out_sems.at[3])
    last.start()
    finish(departures + [last])


def table_row(mine_ref, other_ref, index_ref, at, depth):
    slot = index_ref[at + 1]
    side = index_ref[at + 2]
    mine = mine_ref[slot, side, depth]
    other = other_ref[slot, side, depth]
    return jnp.where(index_ref[at] == 0, mine.astype(F32), other.astype(F32))


def end_rows(mine_ref, other_ref, index_ref, j):
    row = table_row(mine_ref, other_ref, index_ref, lateral_at(j), 0)
    far = index_ref[lateral_at(j) + 3] == 1
    last = EDGE - 1
    return far, jnp.where(far, row[last:], row[:1]), jnp.where(far, row[last - 1 : last], row[1:2])


def forward_kernel(
    index_ref, turn_ref, mine_ref, other_ref, early_ref, staged_ref,
    coarse_ref, delta_ring_ref, pre_ref, strip_pre_ref, seam_ref, cols2_ref, strip_ref,
    down_cols_ref, delta_ref, line_ref,
    pad_ref, patch_ref, wide_ref, fine_ref, cells_ref, line_cols_ref,
):
    tiles = 3
    patch_ref[...] = jnp.zeros_like(patch_ref)
    pad_ref[...] = jnp.zeros_like(pad_ref)
    line_ref[...] = jnp.zeros_like(line_ref)
    turn = turn_ref[...]
    near = []
    own = []
    for n in range(12):
        own.append(mine_ref[n % tiles, n // tiles, 0])
        edge = table_row(mine_ref, other_ref, index_ref, near_at(n), 0)
        near.append(edge)
        patch_ref[n, 1, 1 : EDGE + 1, :] = edge
        patch_ref[n, 2, 1 : EDGE + 1, :] = table_row(
            mine_ref, other_ref, index_ref, near_at(n), 1
        )
        for h in range(2):
            _, outer, inner = end_rows(mine_ref, other_ref, index_ref, 2 * n + h)
            at = (0, EDGE + 1)[h]
            patch_ref[n, 1, at : at + 1, :] = outer
            patch_ref[n, 2, at : at + 1, :] = inner
    seams = dot(turn, jnp.concatenate(near, axis=0).astype(BF16))
    seam_ref[...] = seams
    own_turned = dot(turn, jnp.concatenate(own, axis=0))
    patch_ref[:, 0, 1 : EDGE + 1, :] = own_turned.reshape(12, EDGE, CH)
    for r in range(3):
        for b in range(3):
            part = patch_ref[:, r, b : b + EDGE, :].astype(BF16)
            strip_ref[:, lanes(3 * r + b)] = as_rows(part)
    wide_ref[...] = dot(strip_ref[...], early_ref[:, W1_SIDES])
    for n in range(12):
        strip_pre_ref[strip(n), :] = pick(wide_ref, n * EDGE, EDGE, index_ref[near_at(n) + 2])
    line_ref[:, 1 : EDGE + 1, :] = seams.reshape(12, EDGE, CH)
    triples(line_ref, line_cols_ref, (0, 1, 2))
    pre_ref[...] = staged_ref[:, lanes(0)]
    parts = []
    for side in range(4):
        rows = slice(side * tiles * EDGE, (side + 1) * tiles * EDGE)
        parts.append(dot(line_cols_ref[rows, :], early_ref[: 3 * CH, lanes(side)]))
    add_sides(pre_ref, jnp.concatenate(parts, axis=0))
    fill_pad(pad_ref, gelu(pre_ref[...]).astype(BF16).astype(F32))
    put_seams(pad_ref, dot(turn, gelu(strip_pre_ref[...]).astype(BF16)))
    windows(pad_ref, cols2_ref)
    second_pre = dot(cols2_ref[...], early_ref[:, W2])
    delta = (gelu_slope(second_pre) * staged_ref[:, lanes(1)]).astype(BF16)
    delta_ref[...] = delta
    cells_ref[...] = delta.astype(F32)
    for n in range(12):
        for depth in range(2):
            rows = cells_ref[side_cells(n % tiles, n // tiles, depth), :]
            delta_ring_ref[n % tiles, n // tiles, depth] = rows.astype(BF16)
            if depth == 0:
                line_ref[n, 1 : EDGE + 1, :] = rows
    fine_ref[...] = as_cells(gelu(second_pre).astype(BF16).astype(F32))
    half = EDGE // 2
    for a in range(2):
        for b in range(2):
            part = fine_ref[:, pl.ds(a, half, 2), pl.ds(b, half, 2), :]
            down_cols_ref[:, lanes(2 * a + b)] = as_rows(part).astype(BF16)
    coarse_ref[...] = dot(down_cols_ref[...], early_ref[:512, TAIL]).astype(BF16)


def gradient_kernel(
    index_ref, turn_ref, early_ref, late_ref, pre_ref, strip_pre_ref, seam_ref, cols2_ref, strip_ref, down_cols_ref, delta_ref, line_ref,
    grad_ref, rest_ref,
    pad_ref, cols_ref, cols3_ref, split_ref, line_cols_ref,
):
    tiles = 3
    core = lax.axis_index("c")

    def put_grad(at, block):
        half = at // 11
        grad_ref[jnp.where(core == half, 0, 1), lanes(at % 11), :] = block

    split_ref[...] = jnp.zeros_like(split_ref)
    turn = turn_ref[...]
    down_grad = dot_rows(down_cols_ref[...], early_ref[512:704, TAIL])
    for at in range(4):
        put_grad(18 + at, down_grad[lanes(at)])
    delta = delta_ref[...]
    second_grad = dot_rows(cols2_ref[...], delta)
    for at in range(9):
        put_grad(9 + at, second_grad[lanes(at)])
    pad_ref[...] = jnp.zeros_like(pad_ref)
    fill_pad(pad_ref, delta.astype(F32))
    windows(pad_ref, cols3_ref)
    inner = dot(cols3_ref[...], late_ref[:, W2_BACK])
    rest_ref[:768, lanes(0)] = pre_ref[...]
    rest_ref[:768, lanes(1)] = inner
    inner_delta = (gelu_slope(pre_ref[...]) * inner).astype(BF16)
    triples(line_ref, line_cols_ref, (2, 1, 0))
    rims = []
    for side in range(4):
        rows = slice(side * tiles * EDGE, (side + 1) * tiles * EDGE)
        rims.append(dot(line_cols_ref[rows, :], late_ref[: 3 * CH, lanes(2 + side)]))
    sent = turned(turn, jnp.concatenate(rims, axis=0))
    rest_ref[768:, lanes(0)] = strip_pre_ref[...]
    rest_ref[768:, lanes(1)] = sent
    sent_delta = (gelu_slope(strip_pre_ref[...]) * sent).astype(BF16)
    for n in range(12):
        chosen = pl.ds(pl.multiple_of(index_ref[near_at(n) + 2] * CH, CH), CH)
        split_ref[strip(n), chosen] = sent_delta[strip(n)]
    sent_grad = dot_rows(strip_ref[...], split_ref[...])
    fill_pad(pad_ref, early_ref[:768, X].astype(F32))
    put_seams(pad_ref, seam_ref[...])
    windows(pad_ref, cols_ref)
    first_grad = dot_rows(cols_ref[...], inner_delta)
    for a in range(3):
        for b in range(3):
            block = first_grad[lanes(3 * a + b)]
            for side in range(4):
                for r in range(3):
                    for k in range(3):
                        if frame_source(side, r, k) == (a, b):
                            block = block + sent_grad[lanes(3 * r + k), lanes(side)]
            put_grad(3 * a + b, block)


def backward_kernel(
    index_ref, turn_ref, mine_ref, other_ref, late_ref, rest_ref,
    out_ref, flag_ref,
    pad_ref, cols_ref, line_ref, deep_ref, line_cols_ref, deep_cols_ref, ends_ref, wide_ref,
    strip_wide_ref, cot_ref, cells_ref,
):
    flag_ref[...] = jnp.zeros_like(flag_ref)
    turn = turn_ref[...]
    line_ref[...] = jnp.zeros_like(line_ref)
    deep_ref[...] = jnp.zeros_like(deep_ref)
    ends_ref[...] = jnp.zeros_like(ends_ref)
    pad_ref[...] = jnp.zeros_like(pad_ref)
    for n in range(12):
        for depth, rows_ref in ((0, line_ref), (1, deep_ref)):
            rows_ref[n, 1 : EDGE + 1, :] = table_row(
                mine_ref, other_ref, index_ref, near_at(n), depth
            )
    for j in range(24):
        far, outer, inner = end_rows(mine_ref, other_ref, index_ref, j)
        blank = jnp.zeros_like(inner)
        ends_ref[j : j + 1, lanes(0)] = jnp.where(far, blank, inner)
        ends_ref[j : j + 1, lanes(1)] = outer
        ends_ref[j : j + 1, lanes(2)] = jnp.where(far, inner, blank)
    strip_rows = 12 * EDGE
    triples(line_ref, line_cols_ref, (2, 1, 0))
    line_cols_ref[strip_rows:, :] = ends_ref[...].astype(BF16)
    triples(deep_ref, deep_cols_ref, (2, 1, 0))
    wide_ref[...] = dot(line_cols_ref[...], late_ref[: 3 * CH, ADJOINT])
    strip_wide_ref[...] = dot(deep_cols_ref[...], late_ref[: 3 * CH, ADJOINT]) + dot(
        line_cols_ref[:strip_rows, :], late_ref[3 * CH : 6 * CH, ADJOINT]
    )
    cot_ref[...] = rest_ref[768:, lanes(1)]
    rims = []
    for n in range(12):
        side = index_ref[near_at(n) + 2]
        rims.append(pick(wide_ref, n * EDGE, EDGE, side))
        cot_ref[strip(n), :] += pick(strip_wide_ref, n * EDGE, EDGE, side)
        for h in range(2):
            j = 2 * n + h
            at = n * EDGE + (0, EDGE - 1)[h]
            cot_ref[at : at + 1, :] += pick(
                wide_ref, strip_rows + j, 1, index_ref[lateral_at(j) + 2]
            )
    cells_ref[...] = rest_ref[:768, lanes(1)]
    add_sides(cells_ref, turned(turn, jnp.concatenate(rims, axis=0)))
    delta = gelu_slope(rest_ref[:768, lanes(0)]) * cells_ref[...]
    fill_pad(pad_ref, delta.astype(BF16).astype(F32))
    windows(pad_ref, cols_ref)
    strip_delta = (gelu_slope(rest_ref[768:, lanes(0)]) * cot_ref[...]).astype(BF16).astype(F32)
    line_ref[:, 1 : EDGE + 1, :] = strip_delta.reshape(12, EDGE, CH)
    triples(line_ref, deep_cols_ref, (2, 1, 0))
    strip_wide_ref[...] = dot(deep_cols_ref[...], late_ref[6 * CH :, ADJOINT])
    rims = []
    for n in range(12):
        rims.append(pick(strip_wide_ref, n * EDGE, EDGE, index_ref[near_at(n) + 2]))
    cells_ref[...] = dot(cols_ref[...], late_ref[:, W1_BACK])
    add_sides(cells_ref, turned(turn, jnp.concatenate(rims, axis=0)))
    out_ref[...] = as_cells(cells_ref[...]).astype(BF16)


def first_pair_kernel(own_ref, across_ref, index_ref, pair_ref):
    pair_ref[0] = own_ref[...]
    pair_ref[1] = across_ref[...]


def gate_kernel(*refs):
    refs[-1][...] = jnp.zeros_like(refs[-1])


def table_kernel(own_ref, one_ref, two_ref, three_ref, table_ref):
    for at, part_ref in enumerate((own_ref, one_ref, two_ref, three_ref)):
        table_ref[at] = part_ref[...]


def spread_sum(pieces_ref, copies_ref):
    total = jnp.sum(pieces_ref[...].astype(F32), axis=0).astype(BF16)
    for at in range(copies_ref.shape[0]):
        copies_ref[at] = total


def first_sum_kernel(pieces_ref, flag_ref, own_ref, across_ref, copies_ref, pair_ref):
    spread_sum(pieces_ref, copies_ref)
    pair_ref[0] = own_ref[...]
    pair_ref[1] = across_ref[...]


def second_sum_kernel(
    pieces_ref, flag_ref, own_ref, one_ref, two_ref, three_ref, copies_ref, table_ref
):
    spread_sum(pieces_ref, copies_ref)
    table_kernel(own_ref, one_ref, two_ref, three_ref, table_ref)


def hold_kernel(block_ref, flag_ref, out_ref):
    out_ref[...] = block_ref[...]


def finish_kernel(scale, mine_ref, other_ref, first_ref, second_ref, down_ref):
    core = lax.axis_index("c")
    for at in range(22):
        half = at // 11
        rows = slice(at % 11 * CH, (at % 11 + 1) * CH)
        block = jnp.where(core == half, mine_ref[rows, :], other_ref[rows, :])
        out_ref, base = ((first_ref, 0), (second_ref, 9), (down_ref, 18))[at // 9]
        out_ref[at - base] = block.astype(F32) * scale


def whole(space):
    return pl.BlockSpec(memory_space=space)


def shards(
    activations,
    conv1_weight,
    conv2_weight,
    coarse_kernel_weight,
    skip_cotangent,
    down_cotangent,
    face_neighbours,
    seam_codes,
    tile_slots,
):
    x = activations[0]
    tiles = x.shape[0]
    total_tiles = tile_slots.shape[0]
    cells = tiles * EDGE * EDGE
    strips = 4 * tiles * EDGE
    half = EDGE // 2
    quarter = tiles * half * half
    smem, vmem, hbm = whole(pltpu.SMEM), whole(pltpu.VMEM), whole(pltpu.HBM)
    shape = jax.ShapeDtypeStruct
    plane = lax.axis_size(PLANE)
    deep = lax.axis_size(DEPTH)
    pad = shape((tiles, EDGE + 2, EDGE + 8, CH), F32)
    line = shape((4 * tiles, EDGE + 8, CH), F32)
    ring = shape((tiles, 4, 2, EDGE, CH), BF16)

    def call(
        kernel, outs, operands, scratch=(), sems=(), specs=None, out_specs=None, cost=1, room=24
    ):
        single = not isinstance(outs, tuple)
        scratch = [pltpu.VMEM(one.shape, one.dtype) for one in scratch]
        scratch += [pltpu.SemaphoreType.DMA((count,)) for count in sems]
        return pl.pallas_call(
            kernel,
            out_shape=outs,
            in_specs=specs or [vmem] * len(operands),
            out_specs=out_specs or (vmem if single else (vmem,) * len(outs)),
            scratch_shapes=scratch,
            compiler_params=pltpu.CompilerParams(vmem_limit_bytes=room * 1024 * 1024),
            cost_estimate=pl.CostEstimate(
                flops=cost * cells * 18 * CH * CH, bytes_accessed=2 * 1024 * 1024, transcendentals=0
            ),
        )(*operands)

    wide = shape((strips, 4 * CH), F32)
    all_cols = shape((cells, 9 * CH), BF16)
    cell_rows = shape((cells, CH), F32)
    strip_rows = shape((strips, CH), F32)
    flag = shape((8, CH), F32)
    own_ring = call(ring_kernel, ring, [x], [cell_rows])
    across = swap_apart(own_ring, "z", 1)
    operands = [
        x,
        skip_cotangent[0],
        down_cotangent.reshape(-1, CH),
        conv1_weight.reshape(9 * CH, CH),
        conv2_weight.reshape(9 * CH, CH),
        coarse_kernel_weight.reshape(4 * CH, CH),
    ]
    staged = (
        shape((strips, strips), BF16),
        shape((9 * CH, 7 * CH), BF16),
        shape((9 * CH, 6 * CH), BF16),
        shape((cells, 2 * CH), F32),
    )
    index, turn, early, late, staged_cells = call(
        stage_kernel,
        (shape((296,), jnp.int32),) + staged,
        [face_neighbours.T, seam_codes.T, tile_slots] + operands,
        tuple(operands) + staged
        + (pad, shape(x.shape, F32), all_cols, shape((CH, 4 * CH), BF16)),
        (len(operands), len(staged)),
        specs=[smem] * 3 + [hbm] * 6,
        out_specs=(smem,) + (hbm,) * 4,
        cost=4,
        room=60,
    )
    pair = call(first_pair_kernel, shape((2,) + ring.shape, BF16), [own_ring, across, index], specs=[vmem, vmem, smem])
    along = [swap_apart(pair, "y", apart) for apart in (1, 2, 3)]
    mine = call(table_kernel, shape((4,) + pair.shape, BF16), [pair] + along)
    other = swap_core(mine)

    def table(block):
        return block.reshape((-1,) + ring.shape[1:])

    (
        coarse, delta_ring, pre, strip_pre, seam, cols2, strip_cols, down_cols, delta, line_rows,
    ) = call(
        forward_kernel,
        (
            shape((quarter, CH), BF16),
            ring,
            cell_rows,
            strip_rows,
            strip_rows,
            all_cols,
            shape((strips, 9 * CH), BF16),
            shape((quarter, 4 * CH), BF16),
            shape((cells, CH), BF16),
            line,
        ),
        [index, turn, table(mine), table(other), early, staged_cells],
        [
            pad,
            shape((4 * tiles, 3, EDGE + 8, CH), F32),
            wide,
            shape(x.shape, F32),
            cell_rows,
            shape((strips, 3 * CH), BF16),
        ],
        specs=[smem] + [vmem] * 5,
        cost=2,
    )
    grads, rest = call(
        gradient_kernel,
        (shape((2, 11 * CH, CH), F32), shape((cells + strips, 2 * CH), F32)),
        [
            index, turn, early, late, pre, strip_pre, seam, cols2, strip_cols, down_cols, delta,
            line_rows,
        ],
        [
            pad,
            all_cols,
            all_cols,
            shape((strips, 4 * CH), BF16),
            shape((strips, 3 * CH), BF16),
        ],
        specs=[smem] + [vmem] * 11,
        cost=4,
    )
    kept = (grads[0] + swap_core(grads[1])).astype(BF16)
    part = kept.shape[0] // plane
    across = swap_apart(delta_ring, "z", 1)
    pieces = lax.all_to_all(kept.reshape(plane, part, CH), PLANE, 0, 0)
    copies, pair = call(
        first_sum_kernel,
        (shape((deep, part, CH), BF16), shape((2,) + ring.shape, BF16)),
        [pieces, call(gate_kernel, flag, [across], cost=100), delta_ring, across],
    )
    along = [swap_apart(pair, "y", apart) for apart in (1, 2, 3)]
    pieces = lax.all_to_all(copies, DEPTH, 0, 0)
    copies, mine = call(
        second_sum_kernel,
        (shape((plane, part, CH), BF16), shape((4,) + pair.shape, BF16)),
        [pieces, call(gate_kernel, flag, along, cost=100), pair] + along,
    )
    other = swap_core(mine)
    summed = lax.all_to_all(copies, PLANE, 0, 0).reshape(-1, CH)
    input_grad, done = call(
        backward_kernel,
        (shape(x.shape, BF16), flag),
        [index, turn, table(mine), table(other), late, rest],
        [
            pad,
            all_cols,
            line,
            line,
            shape((strips + 32, 3 * CH), BF16),
            shape((strips, 3 * CH), BF16),
            shape((32, 3 * CH), F32),
            shape((strips + 32, 4 * CH), F32),
            wide,
            strip_rows,
            cell_rows,
        ],
        specs=[smem] + [vmem] * 5,
        cost=100,
    )
    summed = call(hold_kernel, shape(summed.shape, BF16), [summed, done])
    scale = 1.0 / math.sqrt(lax.axis_size(("w", "x")) * total_tiles * EDGE * EDGE)
    first_grad, second_grad, down_grad = call(
        functools.partial(finish_kernel, scale),
        tuple(shape((count, CH, CH), F32) for count in (9, 9, 4)),
        [summed, swap_core(summed)],
    )
    return (
        coarse.reshape((1, tiles, half, half, CH)),
        input_grad[None],
        first_grad.reshape(conv1_weight.shape),
        second_grad.reshape(conv2_weight.shape),
        down_grad.reshape(coarse_kernel_weight.shape),
    )


def solution(mesh):
    batch = mesh.shape["batch"]
    along_x = 4 if batch % 4 == 0 else 1
    fine = Mesh(
        mesh.devices.reshape(4, 2, 2, batch // along_x, along_x), ("y", "z", "c", "w", "x")
    )
    field = P(("w", "x"), ("y", "z", "c"), None, None, None)
    return jax.shard_map(
        shards,
        mesh=fine,
        in_specs=(field, P(), P(), P(), field, field, P(), P(), P()),
        out_specs=(field, field, P(), P(), P()),
        check_vma=False,
    )
```

```python
import functools
import math

import jax
import jax.numpy as jnp
from jax import lax
from jax.experimental import pallas as pl
from jax.experimental.pallas import tpu as pltpu
from jax.sharding import Mesh
from jax.sharding import PartitionSpec as P

PLANE = ("x", "y")
DEPTH = ("z", "w")
SLOPE = math.sqrt(2.0 / math.pi)
CUBIC = 0.044715
BF16 = jnp.bfloat16
F32 = jnp.float32
EDGE = 16
CH = 128


def swap_core(block):
    return lax.ppermute(block, "c", [(0, 1), (1, 0)])


def swap_apart(block, axis, apart):
    number = lax.axis_size(axis)
    return lax.ppermute(block, axis, [(i, i ^ apart) for i in range(number)])


def fetch(sources, targets, sems):
    copies = []
    for at, (source, target) in enumerate(zip(sources, targets)):
        copies.append(pltpu.make_async_copy(source, target, sems.at[at]))
        copies[-1].start()
    return copies


def finish(copies):
    for copy in copies:
        copy.wait()


def gelu(v):
    return 0.5 * v * (1.0 + jnp.tanh(SLOPE * (v + CUBIC * v * v * v)))


def gelu_slope(v):
    t = jnp.tanh(SLOPE * (v + CUBIC * v * v * v))
    return 0.5 * (1.0 + t) + (0.5 * SLOPE) * v * (1.0 - t * t) * (1.0 + (3.0 * CUBIC) * v * v)


def dot(left, right):
    return jnp.dot(left, right, preferred_element_type=F32)


def turned(turn, rows):
    high = rows.astype(BF16)
    low = (rows - high.astype(F32)).astype(BF16)
    return dot(turn, high) + dot(turn, low)


def as_rows(block):
    return block.reshape(-1, CH)


def lanes(at, count=1):
    return slice(at * CH, (at + count) * CH)


def strip(n):
    return slice(n * EDGE, (n + 1) * EDGE)


def as_cells(rows):
    return rows.reshape(-1, EDGE, EDGE, CH)


def fill_pad(pad_ref, rows):
    pad_ref[:, 1 : EDGE + 1, 1 : EDGE + 1, :] = as_cells(rows)


def windows(pad_ref, cols_ref):
    for a in range(3):
        for b in range(3):
            part = pad_ref[:, a : a + EDGE, b : b + EDGE, :].astype(BF16)
            cols_ref[:, lanes(3 * a + b)] = as_rows(part)


def triples(line_ref, cols_ref, order):
    for at, start in enumerate(order):
        part = line_ref[:, start : start + EDGE, :].astype(BF16)
        cols_ref[0 : line_ref.shape[0] * EDGE, lanes(at)] = as_rows(part)


def pick(rows_ref, at, count, side):
    chosen = pl.ds(pl.multiple_of(side * CH, CH), CH)
    return rows_ref[pl.ds(at, count), chosen]


def side_cells(tile, side, depth=0):
    near = (depth, EDGE - 1 - depth)[side in (1, 2)]
    if side % 2 == 0:
        return pl.ds(tile * EDGE * EDGE + near * EDGE, EDGE)
    return pl.ds(tile * EDGE * EDGE + near, EDGE, EDGE)


def add_sides(cells_ref, rows):
    for n in range(12):
        cells = side_cells(n % 3, n // 3)
        cells_ref[cells, :] = cells_ref[cells, :] + rows[strip(n)]


def put_seams(pad_ref, rows):
    for n in range(12):
        side, k = n // 3, n % 3
        place = (0, EDGE + 1, EDGE + 1, 0)[side]
        seam = rows[strip(n)]
        if side % 2 == 0:
            pad_ref[k, place, 1 : EDGE + 1, :] = seam
        else:
            for i in range(EDGE):
                pad_ref[k, 1 + i, place : place + 1, :] = seam[i : i + 1]


def near_at(n):
    return 8 * n


def lateral_at(j):
    return 96 + 8 * j


def frame_source(side, r, k):
    return ((r, k), (k, 2 - r), (2 - r, k), (k, r))[side]


def ring_kernel(x_ref, ring_ref, cells_ref):
    cells_ref[...] = as_rows(x_ref[...]).astype(F32)
    for n in range(12):
        for depth in range(2):
            rows = cells_ref[side_cells(n % 3, n // 3, depth), :].astype(BF16)
            ring_ref[n % 3, n // 3, depth] = rows


W1_SIDES, W2, TAIL, X = (slice(0, 512), slice(512, 640), slice(640, 768), slice(768, 896))
W2_BACK, W1_BACK, ADJOINT = slice(0, 128), slice(128, 256), slice(256, 768)


def index_kernel(near_ref, code_ref, slot_ref, index_ref, turn_hbm, turn_ref, sems):
    total = slot_ref.shape[0]
    tiles = 3
    core = lax.axis_index("c")
    at_y = lax.axis_index("y")
    at_z = lax.axis_index("z")
    first = ((at_y * 2 + at_z) * 2 + core) * tiles

    def look(i, found):
        here = slot_ref[i]
        return tuple(jnp.where(here == first + k, i, found[k]) for k in range(tiles))

    own = lax.fori_loop(0, total, look, (jnp.int32(0),) * tiles, unroll=8)

    def place(at, tile):
        slot = slot_ref[tile]
        owner = (slot * 171) >> 9
        local = slot - owner * tiles
        chip = ((owner >> 2) ^ at_y) * 2 + (((owner >> 1) & 1) ^ at_z)
        index_ref[at] = (owner + core) & 1
        index_ref[at + 1] = chip * tiles + local

    column = lax.broadcasted_iota(jnp.int32, (EDGE, 12 * EDGE), 1)
    row = lax.broadcasted_iota(jnp.int32, (EDGE, 12 * EDGE), 0)
    for n in range(12):
        side, k = n // tiles, n % tiles
        near = near_ref[side, own[k]]
        code = code_ref[side, own[k]]
        near_side = code >> 1
        reverse = code & 1
        place(near_at(n), near)
        index_ref[near_at(n) + 2] = near_side
        source = jnp.where(reverse == 1, EDGE - 1 - row, row) + n * EDGE
        turn_ref[strip(n), :] = jnp.where(column == source, 1.0, 0.0).astype(F32).astype(BF16)
        upright = near_side & 1
        far = jnp.where((near_side == 1) | (near_side == 2), 1, 0)
        for h in range(2):
            lateral = jnp.where(upright == 1, (0, 2)[h], (3, 1)[h])
            at = lateral_at(2 * n + h)
            place(at, near_ref[lateral, near])
            lateral_code = code_ref[lateral, near]
            index_ref[at + 2] = lateral_code >> 1
            index_ref[at + 3] = (far + lateral_code) & 1

    finish(fetch([turn_ref], [turn_hbm], sems))


def stage_kernel(
    index_ref, x_hbm, skip_hbm, down_hbm, w1_hbm, w2_hbm, wc_hbm,
    flag_ref, early_hbm, late_hbm, cells_hbm,
    x_ref, skip_ref, down_ref, w1_ref, w2_ref, wc_ref,
    early_ref, late_ref, cells_ref,
    pad_ref, cot_ref, cols_ref, wc_back_ref, in_sems, out_sems,
):
    arrivals = fetch(
        (w1_hbm, w2_hbm, wc_hbm, x_hbm, down_hbm, skip_hbm),
        (w1_ref, w2_ref, wc_ref, x_ref, down_ref, skip_ref),
        in_sems,
    )
    for at in range(8):
        flag_ref[at] = index_ref[at]
    pad_ref[...] = jnp.zeros_like(pad_ref)
    early_ref[704:, TAIL] = jnp.zeros_like(early_ref[704:, TAIL])
    early_ref[768:, X] = jnp.zeros_like(early_ref[768:, X])
    finish(arrivals)
    for side in range(4):
        for r in range(3):
            for k in range(3):
                a, b = frame_source(side, r, k)
                early_ref[lanes(3 * r + k), lanes(side)] = w1_ref[lanes(3 * a + b), :]
    early_ref[:, W2] = w2_ref[...]
    early_ref[:512, TAIL] = wc_ref[...]
    down = down_ref[...]
    early_ref[512:704, TAIL] = down
    x_rows = as_rows(x_ref[...])
    early_ref[:768, X] = x_rows
    departures = fetch([early_ref], [early_hbm], out_sems)

    def flip(block):
        return jnp.transpose(block.astype(F32)).astype(BF16)

    for a in range(3):
        for b in range(3):
            first_flip = flip(w1_ref[lanes(3 * a + b), :])
            second_flip = flip(w2_ref[lanes(3 * a + b), :])
            back = lanes(8 - 3 * a - b)
            late_ref[back, W1_BACK] = first_flip
            late_ref[back, W2_BACK] = second_flip
            for side in range(4):
                for r in range(2):
                    for k in range(3):
                        if frame_source(side, r, k) != (a, b):
                            continue
                        if r == 0:
                            late_ref[lanes(6 + k), lanes(2 + side)] = first_flip
                        late_ref[lanes(3 * r + k), lanes(2 + side)] = second_flip
    last = pltpu.make_async_copy(late_ref, late_hbm, out_sems.at[1])
    last.start()
    departures.append(last)
    for at in range(4):
        wc_back_ref[:, lanes(at)] = flip(wc_ref[lanes(at), :])
    spread_down = dot(down, wc_back_ref[...])
    half = EDGE // 2
    for a in range(2):
        for b in range(2):
            part = spread_down[:, lanes(2 * a + b)].reshape(-1, half, half, CH)
            cot_ref[:, pl.ds(a, half, 2), pl.ds(b, half, 2), :] = part
    cells_ref[:, lanes(1)] = as_rows(cot_ref[...] + skip_ref[...].astype(F32))
    fill_pad(pad_ref, x_rows.astype(F32))
    windows(pad_ref, cols_ref)
    cells_ref[:, lanes(0)] = dot(cols_ref[...], w1_ref[...])
    last = pltpu.make_async_copy(cells_ref, cells_hbm, out_sems.at[2])
    last.start()
    finish(departures + [last])


def table_row(mine_ref, other_ref, index_ref, at, depth):
    slot = index_ref[at + 1]
    side = index_ref[at + 2]
    mine = mine_ref[slot, side, depth]
    other = other_ref[slot, side, depth]
    return jnp.where(index_ref[at] == 0, mine.astype(F32), other.astype(F32))


def end_rows(mine_ref, other_ref, index_ref, j):
    row = table_row(mine_ref, other_ref, index_ref, lateral_at(j), 0)
    far = index_ref[lateral_at(j) + 3] == 1
    last = EDGE - 1
    return far, jnp.where(far, row[last:], row[:1]), jnp.where(far, row[last - 1 : last], row[1:2])


def forward_kernel(
    index_ref, turn_ref, mine_ref, other_ref, early_ref, staged_ref,
    coarse_ref, delta_ring_ref, pre_ref, strip_pre_ref, seam_ref, cols2_ref, strip_ref,
    down_cols_ref, delta_ref, line_ref,
    pad_ref, patch_ref, wide_ref, fine_ref, cells_ref, line_cols_ref,
):
    tiles = 3
    patch_ref[...] = jnp.zeros_like(patch_ref)
    pad_ref[...] = jnp.zeros_like(pad_ref)
    line_ref[...] = jnp.zeros_like(line_ref)
    turn = turn_ref[...]
    near = []
    own = []
    for n in range(12):
        own.append(mine_ref[n % tiles, n // tiles, 0])
        edge = table_row(mine_ref, other_ref, index_ref, near_at(n), 0)
        near.append(edge)
        patch_ref[n, 1, 1 : EDGE + 1, :] = edge
        patch_ref[n, 2, 1 : EDGE + 1, :] = table_row(
            mine_ref, other_ref, index_ref, near_at(n), 1
        )
        for h in range(2):
            _, outer, inner = end_rows(mine_ref, other_ref, index_ref, 2 * n + h)
            at = (0, EDGE + 1)[h]
            patch_ref[n, 1, at : at + 1, :] = outer
            patch_ref[n, 2, at : at + 1, :] = inner
    seams = dot(turn, jnp.concatenate(near, axis=0).astype(BF16))
    seam_ref[...] = seams
    own_turned = dot(turn, jnp.concatenate(own, axis=0))
    patch_ref[:, 0, 1 : EDGE + 1, :] = own_turned.reshape(12, EDGE, CH)
    for r in range(3):
        for b in range(3):
            part = patch_ref[:, r, b : b + EDGE, :].astype(BF16)
            strip_ref[:, lanes(3 * r + b)] = as_rows(part)
    wide_ref[...] = dot(strip_ref[...], early_ref[:, W1_SIDES])
    for n in range(12):
        strip_pre_ref[strip(n), :] = pick(wide_ref, n * EDGE, EDGE, index_ref[near_at(n) + 2])
    line_ref[:, 1 : EDGE + 1, :] = seams.reshape(12, EDGE, CH)
    triples(line_ref, line_cols_ref, (0, 1, 2))
    pre_ref[...] = staged_ref[:, lanes(0)]
    parts = []
    for side in range(4):
        rows = slice(side * tiles * EDGE, (side + 1) * tiles * EDGE)
        parts.append(dot(line_cols_ref[rows, :], early_ref[: 3 * CH, lanes(side)]))
    add_sides(pre_ref, jnp.concatenate(parts, axis=0))
    fill_pad(pad_ref, gelu(pre_ref[...]).astype(BF16).astype(F32))
    put_seams(pad_ref, dot(turn, gelu(strip_pre_ref[...]).astype(BF16)))
    windows(pad_ref, cols2_ref)
    second_pre = dot(cols2_ref[...], early_ref[:, W2])
    delta = (gelu_slope(second_pre) * staged_ref[:, lanes(1)]).astype(BF16)
    delta_ref[...] = delta
    cells_ref[...] = delta.astype(F32)
    for n in range(12):
        for depth in range(2):
            rows = cells_ref[side_cells(n % tiles, n // tiles, depth), :]
            delta_ring_ref[n % tiles, n // tiles, depth] = rows.astype(BF16)
            if depth == 0:
                line_ref[n, 1 : EDGE + 1, :] = rows
    fine_ref[...] = as_cells(gelu(second_pre).astype(BF16).astype(F32))
    half = EDGE // 2
    for a in range(2):
        for b in range(2):
            part = fine_ref[:, pl.ds(a, half, 2), pl.ds(b, half, 2), :]
            down_cols_ref[:, lanes(2 * a + b)] = as_rows(part).astype(BF16)
    coarse_ref[...] = dot(down_cols_ref[...], early_ref[:512, TAIL]).astype(BF16)


def gradient_kernel(
    index_ref, turn_ref, early_ref, late_ref, pre_ref, strip_pre_ref, seam_ref, cols2_ref, strip_ref, down_cols_ref, delta_ref, line_ref,
    grad_ref, rest_ref,
    pad_ref, cols_ref, cols3_ref, split_ref, line_cols_ref,
):
    tiles = 3
    core = lax.axis_index("c")

    def put_grad(at, block):
        half = at // 11
        grad_ref[jnp.where(core == half, 0, 1), lanes(at % 11), :] = jnp.transpose(block)

    def across_rows(rows):
        return jnp.transpose(rows.astype(F32)).astype(BF16)

    split_ref[...] = jnp.zeros_like(split_ref)
    turn = turn_ref[...]
    down_grad = dot(across_rows(early_ref[512:704, TAIL]), down_cols_ref[...])
    for at in range(4):
        put_grad(18 + at, down_grad[:, lanes(at)])
    delta = delta_ref[...]
    second_grad = dot(across_rows(delta), cols2_ref[...])
    for at in range(9):
        put_grad(9 + at, second_grad[:, lanes(at)])
    pad_ref[...] = jnp.zeros_like(pad_ref)
    fill_pad(pad_ref, delta.astype(F32))
    windows(pad_ref, cols3_ref)
    inner = dot(cols3_ref[...], late_ref[:, W2_BACK])
    rest_ref[:768, lanes(0)] = pre_ref[...]
    rest_ref[:768, lanes(1)] = inner
    inner_delta = (gelu_slope(pre_ref[...]) * inner).astype(BF16)
    triples(line_ref, line_cols_ref, (2, 1, 0))
    rims = []
    for side in range(4):
        rows = slice(side * tiles * EDGE, (side + 1) * tiles * EDGE)
        rims.append(dot(line_cols_ref[rows, :], late_ref[: 3 * CH, lanes(2 + side)]))
    sent = turned(turn, jnp.concatenate(rims, axis=0))
    rest_ref[768:, lanes(0)] = strip_pre_ref[...]
    rest_ref[768:, lanes(1)] = sent
    sent_delta = (gelu_slope(strip_pre_ref[...]) * sent).astype(BF16)
    for n in range(12):
        chosen = pl.ds(pl.multiple_of(index_ref[near_at(n) + 2] * CH, CH), CH)
        split_ref[strip(n), chosen] = sent_delta[strip(n)]
    sent_grad = dot(across_rows(split_ref[...]), strip_ref[...])
    fill_pad(pad_ref, early_ref[:768, X].astype(F32))
    put_seams(pad_ref, seam_ref[...])
    windows(pad_ref, cols_ref)
    first_grad = dot(across_rows(inner_delta), cols_ref[...])
    for a in range(3):
        for b in range(3):
            block = first_grad[:, lanes(3 * a + b)]
            for side in range(4):
                for r in range(3):
                    for k in range(3):
                        if frame_source(side, r, k) == (a, b):
                            block = block + sent_grad[lanes(side), lanes(3 * r + k)]
            put_grad(3 * a + b, block)


def backward_kernel(
    index_ref, turn_ref, mine_ref, other_ref, late_ref, rest_ref,
    out_ref, flag_ref,
    pad_ref, cols_ref, line_ref, deep_ref, line_cols_ref, deep_cols_ref, ends_ref, wide_ref,
    strip_wide_ref, cot_ref, cells_ref,
):
    flag_ref[...] = jnp.zeros_like(flag_ref)
    turn = turn_ref[...]
    line_ref[...] = jnp.zeros_like(line_ref)
    deep_ref[...] = jnp.zeros_like(deep_ref)
    ends_ref[...] = jnp.zeros_like(ends_ref)
    pad_ref[...] = jnp.zeros_like(pad_ref)
    for n in range(12):
        for depth, rows_ref in ((0, line_ref), (1, deep_ref)):
            rows_ref[n, 1 : EDGE + 1, :] = table_row(
                mine_ref, other_ref, index_ref, near_at(n), depth
            )
    for j in range(24):
        far, outer, inner = end_rows(mine_ref, other_ref, index_ref, j)
        blank = jnp.zeros_like(inner)
        ends_ref[j : j + 1, lanes(0)] = jnp.where(far, blank, inner)
        ends_ref[j : j + 1, lanes(1)] = outer
        ends_ref[j : j + 1, lanes(2)] = jnp.where(far, inner, blank)
    strip_rows = 12 * EDGE
    triples(line_ref, line_cols_ref, (2, 1, 0))
    line_cols_ref[strip_rows:, :] = ends_ref[...].astype(BF16)
    triples(deep_ref, deep_cols_ref, (2, 1, 0))
    wide_ref[...] = dot(line_cols_ref[...], late_ref[: 3 * CH, ADJOINT])
    strip_wide_ref[...] = dot(deep_cols_ref[...], late_ref[: 3 * CH, ADJOINT]) + dot(
        line_cols_ref[:strip_rows, :], late_ref[3 * CH : 6 * CH, ADJOINT]
    )
    cot_ref[...] = rest_ref[768:, lanes(1)]
    rims = []
    for n in range(12):
        side = index_ref[near_at(n) + 2]
        rims.append(pick(wide_ref, n * EDGE, EDGE, side))
        cot_ref[strip(n), :] += pick(strip_wide_ref, n * EDGE, EDGE, side)
        for h in range(2):
            j = 2 * n + h
            at = n * EDGE + (0, EDGE - 1)[h]
            cot_ref[at : at + 1, :] += pick(
                wide_ref, strip_rows + j, 1, index_ref[lateral_at(j) + 2]
            )
    cells_ref[...] = rest_ref[:768, lanes(1)]
    add_sides(cells_ref, turned(turn, jnp.concatenate(rims, axis=0)))
    delta = gelu_slope(rest_ref[:768, lanes(0)]) * cells_ref[...]
    fill_pad(pad_ref, delta.astype(BF16).astype(F32))
    windows(pad_ref, cols_ref)
    strip_delta = (gelu_slope(rest_ref[768:, lanes(0)]) * cot_ref[...]).astype(BF16).astype(F32)
    line_ref[:, 1 : EDGE + 1, :] = strip_delta.reshape(12, EDGE, CH)
    triples(line_ref, deep_cols_ref, (2, 1, 0))
    strip_wide_ref[...] = dot(deep_cols_ref[...], late_ref[6 * CH :, ADJOINT])
    rims = []
    for n in range(12):
        rims.append(pick(strip_wide_ref, n * EDGE, EDGE, index_ref[near_at(n) + 2]))
    cells_ref[...] = dot(cols_ref[...], late_ref[:, W1_BACK])
    add_sides(cells_ref, turned(turn, jnp.concatenate(rims, axis=0)))
    out_ref[...] = as_cells(cells_ref[...]).astype(BF16)


def first_table_kernel(*refs):
    table_ref = refs[-1]
    for at in range(4):
        table_ref[at, 0] = refs[at][...]
        table_ref[at, 1] = refs[4 + at][...]


def gate_kernel(*refs):
    refs[-1][...] = jnp.zeros_like(refs[-1])


def table_kernel(own_ref, one_ref, two_ref, three_ref, table_ref):
    for at, part_ref in enumerate((own_ref, one_ref, two_ref, three_ref)):
        table_ref[at] = part_ref[...]


def spread_sum(pieces_ref, copies_ref):
    total = jnp.sum(pieces_ref[...].astype(F32), axis=0).astype(BF16)
    for at in range(copies_ref.shape[0]):
        copies_ref[at] = total


def first_sum_kernel(pieces_ref, flag_ref, own_ref, across_ref, copies_ref, pair_ref):
    spread_sum(pieces_ref, copies_ref)
    pair_ref[0] = own_ref[...]
    pair_ref[1] = across_ref[...]


def second_sum_kernel(
    pieces_ref, flag_ref, own_ref, one_ref, two_ref, three_ref, copies_ref, table_ref
):
    spread_sum(pieces_ref, copies_ref)
    table_kernel(own_ref, one_ref, two_ref, three_ref, table_ref)


def hold_kernel(block_ref, flag_ref, out_ref):
    out_ref[...] = block_ref[...]


def finish_kernel(scale, mine_ref, other_ref, first_ref, second_ref, down_ref):
    core = lax.axis_index("c")
    for at in range(22):
        half = at // 11
        rows = slice(at % 11 * CH, (at % 11 + 1) * CH)
        block = jnp.where(core == half, mine_ref[rows, :], other_ref[rows, :])
        out_ref, base = ((first_ref, 0), (second_ref, 9), (down_ref, 18))[at // 9]
        out_ref[at - base] = block.astype(F32) * scale


def whole(space):
    return pl.BlockSpec(memory_space=space)


def shards(
    activations,
    conv1_weight,
    conv2_weight,
    coarse_kernel_weight,
    skip_cotangent,
    down_cotangent,
    face_neighbours,
    seam_codes,
    tile_slots,
):
    x = activations[0]
    tiles = x.shape[0]
    total_tiles = tile_slots.shape[0]
    cells = tiles * EDGE * EDGE
    strips = 4 * tiles * EDGE
    half = EDGE // 2
    quarter = tiles * half * half
    smem, vmem, hbm = whole(pltpu.SMEM), whole(pltpu.VMEM), whole(pltpu.HBM)
    shape = jax.ShapeDtypeStruct
    plane = lax.axis_size(PLANE)
    deep = lax.axis_size(DEPTH)
    pad = shape((tiles, EDGE + 2, EDGE + 8, CH), F32)
    line = shape((4 * tiles, EDGE + 8, CH), F32)
    ring = shape((tiles, 4, 2, EDGE, CH), BF16)

    def call(
        kernel, outs, operands, scratch=(), sems=(), specs=None, out_specs=None, cost=1, room=24
    ):
        single = not isinstance(outs, tuple)
        scratch = [pltpu.VMEM(one.shape, one.dtype) for one in scratch]
        scratch += [pltpu.SemaphoreType.DMA((count,)) for count in sems]
        return pl.pallas_call(
            kernel,
            out_shape=outs,
            in_specs=specs or [vmem] * len(operands),
            out_specs=out_specs or (vmem if single else (vmem,) * len(outs)),
            scratch_shapes=scratch,
            compiler_params=pltpu.CompilerParams(vmem_limit_bytes=room * 1024 * 1024),
            cost_estimate=pl.CostEstimate(
                flops=cost * cells * 18 * CH * CH, bytes_accessed=2 * 1024 * 1024, transcendentals=0
            ),
        )(*operands)

    wide = shape((strips, 4 * CH), F32)
    all_cols = shape((cells, 9 * CH), BF16)
    cell_rows = shape((cells, CH), F32)
    strip_rows = shape((strips, CH), F32)
    flag = shape((8, CH), F32)
    own_ring = call(ring_kernel, ring, [x], [cell_rows])
    across = swap_apart(own_ring, "z", 1)
    operands = [
        x,
        skip_cotangent[0],
        down_cotangent.reshape(-1, CH),
        conv1_weight.reshape(9 * CH, CH),
        conv2_weight.reshape(9 * CH, CH),
        coarse_kernel_weight.reshape(4 * CH, CH),
    ]
    turn_shape = shape((strips, strips), BF16)
    index, turn = call(
        index_kernel,
        (shape((296,), jnp.int32), turn_shape),
        [face_neighbours.T, seam_codes.T, tile_slots],
        [turn_shape],
        (1,),
        specs=[smem] * 3,
        out_specs=(smem, hbm),
        cost=4,
        room=60,
    )
    staged = (
        shape((9 * CH, 7 * CH), BF16),
        shape((9 * CH, 6 * CH), BF16),
        shape((cells, 2 * CH), F32),
    )
    ready, early, late, staged_cells = call(
        stage_kernel,
        (shape((8,), jnp.int32),) + staged,
        [index] + operands,
        tuple(operands) + staged
        + (pad, shape(x.shape, F32), all_cols, shape((CH, 4 * CH), BF16)),
        (len(operands), len(staged)),
        specs=[smem] + [hbm] * 6,
        out_specs=(smem,) + (hbm,) * 3,
        cost=100,
        room=60,
    )
    near_rings = [own_ring] + [swap_apart(own_ring, "y", apart) for apart in (1, 2, 3)]
    far_rings = [across] + [swap_apart(across, "y", apart) for apart in (1, 2, 3)]
    mine = call(
        first_table_kernel,
        shape((4, 2) + ring.shape, BF16),
        near_rings + far_rings + [index, ready],
        specs=[vmem] * 8 + [smem] * 2,
    )
    other = swap_core(mine)

    def table(block):
        return block.reshape((-1,) + ring.shape[1:])

    (
        coarse, delta_ring, pre, strip_pre, seam, cols2, strip_cols, down_cols, delta, line_rows,
    ) = call(
        forward_kernel,
        (
            shape((quarter, CH), BF16),
            ring,
            cell_rows,
            strip_rows,
            strip_rows,
            all_cols,
            shape((strips, 9 * CH), BF16),
            shape((quarter, 4 * CH), BF16),
            shape((cells, CH), BF16),
            line,
        ),
        [index, turn, table(mine), table(other), early, staged_cells],
        [
            pad,
            shape((4 * tiles, 3, EDGE + 8, CH), F32),
            wide,
            shape(x.shape, F32),
            cell_rows,
            shape((strips, 3 * CH), BF16),
        ],
        specs=[smem] + [vmem] * 5,
        cost=2,
    )
    grads, rest = call(
        gradient_kernel,
        (shape((2, 11 * CH, CH), F32), shape((cells + strips, 2 * CH), F32)),
        [
            index, turn, early, late, pre, strip_pre, seam, cols2, strip_cols, down_cols, delta,
            line_rows,
        ],
        [
            pad,
            all_cols,
            all_cols,
            shape((strips, 4 * CH), BF16),
            shape((strips, 3 * CH), BF16),
        ],
        specs=[smem] + [vmem] * 11,
        cost=4,
    )
    kept = (grads[0] + swap_core(grads[1])).astype(BF16)
    part = kept.shape[0] // plane
    across = swap_apart(delta_ring, "z", 1)
    pieces = lax.all_to_all(kept.reshape(plane, part, CH), PLANE, 0, 0)
    copies, pair = call(
        first_sum_kernel,
        (shape((deep, part, CH), BF16), shape((2,) + ring.shape, BF16)),
        [pieces, call(gate_kernel, flag, [across], cost=100), delta_ring, across],
    )
    along = [swap_apart(pair, "y", apart) for apart in (1, 2, 3)]
    pieces = lax.all_to_all(copies, DEPTH, 0, 0)
    copies, mine = call(
        second_sum_kernel,
        (shape((plane, part, CH), BF16), shape((4,) + pair.shape, BF16)),
        [pieces, call(gate_kernel, flag, along, cost=100), pair] + along,
    )
    other = swap_core(mine)
    summed = lax.all_to_all(copies, PLANE, 0, 0).reshape(-1, CH)
    input_grad, done = call(
        backward_kernel,
        (shape(x.shape, BF16), flag),
        [index, turn, table(mine), table(other), late, rest],
        [
            pad,
            all_cols,
            line,
            line,
            shape((strips + 32, 3 * CH), BF16),
            shape((strips, 3 * CH), BF16),
            shape((32, 3 * CH), F32),
            shape((strips + 32, 4 * CH), F32),
            wide,
            strip_rows,
            cell_rows,
        ],
        specs=[smem] + [vmem] * 5,
        cost=100,
    )
    summed = call(hold_kernel, shape(summed.shape, BF16), [summed, done])
    scale = 1.0 / math.sqrt(lax.axis_size(("w", "x")) * total_tiles * EDGE * EDGE)
    first_grad, second_grad, down_grad = call(
        functools.partial(finish_kernel, scale),
        tuple(shape((count, CH, CH), F32) for count in (9, 9, 4)),
        [summed, swap_core(summed)],
    )
    return (
        coarse.reshape((1, tiles, half, half, CH)),
        input_grad[None],
        first_grad.reshape(conv1_weight.shape),
        second_grad.reshape(conv2_weight.shape),
        down_grad.reshape(coarse_kernel_weight.shape),
    )


def solution(mesh):
    batch = mesh.shape["batch"]
    along_x = 4 if batch % 4 == 0 else 1
    fine = Mesh(
        mesh.devices.reshape(4, 2, 2, batch // along_x, along_x), ("y", "z", "c", "w", "x")
    )
    field = P(("w", "x"), ("y", "z", "c"), None, None, None)
    return jax.shard_map(
        shards,
        mesh=fine,
        in_specs=(field, P(), P(), P(), field, field, P(), P(), P()),
        out_specs=(field, field, P(), P(), P()),
        check_vma=False,
    )
```

```python
import functools
import math

import jax
import jax.numpy as jnp
from jax import lax
from jax.experimental import pallas as pl
from jax.experimental.pallas import tpu as pltpu
from jax.sharding import Mesh
from jax.sharding import PartitionSpec as P

PLANE = ("x", "y")
DEPTH = ("z", "w")
SLOPE = math.sqrt(2.0 / math.pi)
CUBIC = 0.044715
BF16 = jnp.bfloat16
F32 = jnp.float32
EDGE = 16
CH = 128


def swap_core(block):
    return lax.ppermute(block, "c", [(0, 1), (1, 0)])


def swap_apart(block, axis, apart):
    number = lax.axis_size(axis)
    return lax.ppermute(block, axis, [(i, i ^ apart) for i in range(number)])


def fetch(sources, targets, sems):
    copies = []
    for at, (source, target) in enumerate(zip(sources, targets)):
        copies.append(pltpu.make_async_copy(source, target, sems.at[at]))
        copies[-1].start()
    return copies


def finish(copies):
    for copy in copies:
        copy.wait()


def gelu(v):
    return 0.5 * v * (1.0 + jnp.tanh(SLOPE * (v + CUBIC * v * v * v)))


def gelu_slope(v):
    t = jnp.tanh(SLOPE * (v + CUBIC * v * v * v))
    return 0.5 * (1.0 + t) + (0.5 * SLOPE) * v * (1.0 - t * t) * (1.0 + (3.0 * CUBIC) * v * v)


def dot(left, right):
    return jnp.dot(left, right, preferred_element_type=F32)


def turned(turn, rows):
    high = rows.astype(BF16)
    low = (rows - high.astype(F32)).astype(BF16)
    return dot(turn, high) + dot(turn, low)


def as_rows(block):
    return block.reshape(-1, CH)


def lanes(at, count=1):
    return slice(at * CH, (at + count) * CH)


def strip(n):
    return slice(n * EDGE, (n + 1) * EDGE)


def as_cells(rows):
    return rows.reshape(-1, EDGE, EDGE, CH)


def fill_pad(pad_ref, rows):
    pad_ref[:, 1 : EDGE + 1, 1 : EDGE + 1, :] = as_cells(rows)


def windows(pad_ref, cols_ref):
    for a in range(3):
        for b in range(3):
            part = pad_ref[:, a : a + EDGE, b : b + EDGE, :].astype(BF16)
            cols_ref[:, lanes(3 * a + b)] = as_rows(part)


def triples(line_ref, cols_ref, order):
    for at, start in enumerate(order):
        part = line_ref[:, start : start + EDGE, :].astype(BF16)
        cols_ref[0 : line_ref.shape[0] * EDGE, lanes(at)] = as_rows(part)


def pick(rows_ref, at, count, side):
    chosen = pl.ds(pl.multiple_of(side * CH, CH), CH)
    return rows_ref[pl.ds(at, count), chosen]


def side_cells(tile, side, depth=0):
    near = (depth, EDGE - 1 - depth)[side in (1, 2)]
    if side % 2 == 0:
        return pl.ds(tile * EDGE * EDGE + near * EDGE, EDGE)
    return pl.ds(tile * EDGE * EDGE + near, EDGE, EDGE)


def add_sides(cells_ref, rows):
    for n in range(12):
        cells = side_cells(n % 3, n // 3)
        cells_ref[cells, :] = cells_ref[cells, :] + rows[strip(n)]


def put_seams(pad_ref, rows):
    for n in range(12):
        side, k = n // 3, n % 3
        place = (0, EDGE + 1, EDGE + 1, 0)[side]
        seam = rows[strip(n)]
        if side % 2 == 0:
            pad_ref[k, place, 1 : EDGE + 1, :] = seam
        else:
            for i in range(EDGE):
                pad_ref[k, 1 + i, place : place + 1, :] = seam[i : i + 1]


def near_at(n):
    return 8 * n


def lateral_at(j):
    return 96 + 8 * j


def frame_source(side, r, k):
    return ((r, k), (k, 2 - r), (2 - r, k), (k, r))[side]


def ring_kernel(x_ref, ring_ref, cells_ref):
    cells_ref[...] = as_rows(x_ref[...]).astype(F32)
    for n in range(12):
        for depth in range(2):
            rows = cells_ref[side_cells(n % 3, n // 3, depth), :].astype(BF16)
            ring_ref[n % 3, n // 3, depth] = rows


W1, W2, TAIL = slice(0, 128), slice(128, 256), slice(256, 384)
W2_BACK, W1_BACK, X = slice(0, 128), slice(128, 256), slice(256, 384)


def side_weights(source_ref, chosen, sides_ref, depth, back=False):
    for side in range(4):
        for r in range(depth):
            for k in range(3):
                a, b = frame_source(side, r, k)
                at = 8 - 3 * a - b if back else 3 * a + b
                sides_ref[lanes(3 * r + k), lanes(side)] = source_ref[lanes(at), chosen]


def index_kernel(near_ref, code_ref, slot_ref, index_ref, turn_hbm, turn_ref, sems):
    total = slot_ref.shape[0]
    tiles = 3
    core = lax.axis_index("c")
    at_y = lax.axis_index("y")
    at_z = lax.axis_index("z")
    first = ((at_y * 2 + at_z) * 2 + core) * tiles

    def look(i, found):
        here = slot_ref[i]
        return tuple(jnp.where(here == first + k, i, found[k]) for k in range(tiles))

    own = lax.fori_loop(0, total, look, (jnp.int32(0),) * tiles, unroll=8)

    def place(at, tile):
        slot = slot_ref[tile]
        owner = (slot * 171) >> 9
        local = slot - owner * tiles
        chip = ((owner >> 2) ^ at_y) * 2 + (((owner >> 1) & 1) ^ at_z)
        index_ref[at] = (owner + core) & 1
        index_ref[at + 1] = chip * tiles + local

    column = lax.broadcasted_iota(jnp.int32, (EDGE, 12 * EDGE), 1)
    row = lax.broadcasted_iota(jnp.int32, (EDGE, 12 * EDGE), 0)
    for n in range(12):
        side, k = n // tiles, n % tiles
        near = near_ref[side, own[k]]
        code = code_ref[side, own[k]]
        near_side = code >> 1
        reverse = code & 1
        place(near_at(n), near)
        index_ref[near_at(n) + 2] = near_side
        source = jnp.where(reverse == 1, EDGE - 1 - row, row) + n * EDGE
        turn_ref[strip(n), :] = jnp.where(column == source, 1.0, 0.0).astype(F32).astype(BF16)
        upright = near_side & 1
        far = jnp.where((near_side == 1) | (near_side == 2), 1, 0)
        for h in range(2):
            lateral = jnp.where(upright == 1, (0, 2)[h], (3, 1)[h])
            at = lateral_at(2 * n + h)
            place(at, near_ref[lateral, near])
            lateral_code = code_ref[lateral, near]
            index_ref[at + 2] = lateral_code >> 1
            index_ref[at + 3] = (far + lateral_code) & 1

    finish(fetch([turn_ref], [turn_hbm], sems))


def stage_kernel(
    index_ref, x_hbm, skip_hbm, down_hbm, w1_hbm, w2_hbm, wc_hbm,
    flag_ref, early_hbm, late_hbm, cells_hbm,
    x_ref, skip_ref, down_ref, w1_ref, w2_ref, wc_ref,
    early_ref, late_ref, cells_ref,
    pad_ref, cot_ref, cols_ref, wc_back_ref, in_sems, out_sems,
):
    arrivals = fetch(
        (w1_hbm, w2_hbm, wc_hbm, x_hbm, down_hbm, skip_hbm),
        (w1_ref, w2_ref, wc_ref, x_ref, down_ref, skip_ref),
        in_sems,
    )
    for at in range(8):
        flag_ref[at] = index_ref[at]
    pad_ref[...] = jnp.zeros_like(pad_ref)
    early_ref[704:, TAIL] = jnp.zeros_like(early_ref[704:, TAIL])
    late_ref[768:, X] = jnp.zeros_like(late_ref[768:, X])
    finish(arrivals)
    early_ref[:, W1] = w1_ref[...]
    early_ref[:, W2] = w2_ref[...]
    early_ref[:512, TAIL] = wc_ref[...]
    down = down_ref[...]
    early_ref[512:704, TAIL] = down
    x_rows = as_rows(x_ref[...])
    late_ref[:768, X] = x_rows
    departures = fetch([early_ref], [early_hbm], out_sems)

    def flip(block):
        return jnp.transpose(block.astype(F32)).astype(BF16)

    for a in range(3):
        for b in range(3):
            back = lanes(8 - 3 * a - b)
            late_ref[back, W1_BACK] = flip(w1_ref[lanes(3 * a + b), :])
            late_ref[back, W2_BACK] = flip(w2_ref[lanes(3 * a + b), :])
    last = pltpu.make_async_copy(late_ref, late_hbm, out_sems.at[1])
    last.start()
    departures.append(last)
    for at in range(4):
        wc_back_ref[:, lanes(at)] = flip(wc_ref[lanes(at), :])
    spread_down = dot(down, wc_back_ref[...])
    half = EDGE // 2
    for a in range(2):
        for b in range(2):
            part = spread_down[:, lanes(2 * a + b)].reshape(-1, half, half, CH)
            cot_ref[:, pl.ds(a, half, 2), pl.ds(b, half, 2), :] = part
    cells_ref[:, lanes(1)] = as_rows(cot_ref[...] + skip_ref[...].astype(F32))
    fill_pad(pad_ref, x_rows.astype(F32))
    windows(pad_ref, cols_ref)
    cells_ref[:, lanes(0)] = dot(cols_ref[...], w1_ref[...])
    last = pltpu.make_async_copy(cells_ref, cells_hbm, out_sems.at[2])
    last.start()
    finish(departures + [last])


def table_row(mine_ref, other_ref, index_ref, at, depth):
    slot = index_ref[at + 1]
    side = index_ref[at + 2]
    mine = mine_ref[slot, side, depth]
    other = other_ref[slot, side, depth]
    return jnp.where(index_ref[at] == 0, mine.astype(F32), other.astype(F32))


def end_rows(mine_ref, other_ref, index_ref, j):
    row = table_row(mine_ref, other_ref, index_ref, lateral_at(j), 0)
    far = index_ref[lateral_at(j) + 3] == 1
    last = EDGE - 1
    return far, jnp.where(far, row[last:], row[:1]), jnp.where(far, row[last - 1 : last], row[1:2])


def forward_kernel(
    index_ref, turn_ref, mine_ref, other_ref, early_ref, staged_ref,
    coarse_ref, delta_ring_ref, pre_ref, strip_pre_ref, seam_ref, cols2_ref, strip_ref,
    down_cols_ref, delta_ref, line_ref,
    pad_ref, patch_ref, wide_ref, fine_ref, cells_ref, line_cols_ref, sides_ref,
):
    tiles = 3
    side_weights(early_ref, W1, sides_ref, 3)
    patch_ref[...] = jnp.zeros_like(patch_ref)
    pad_ref[...] = jnp.zeros_like(pad_ref)
    line_ref[...] = jnp.zeros_like(line_ref)
    turn = turn_ref[...]
    near = []
    own = []
    for n in range(12):
        own.append(mine_ref[n % tiles, n // tiles, 0])
        edge = table_row(mine_ref, other_ref, index_ref, near_at(n), 0)
        near.append(edge)
        patch_ref[n, 1, 1 : EDGE + 1, :] = edge
        patch_ref[n, 2, 1 : EDGE + 1, :] = table_row(
            mine_ref, other_ref, index_ref, near_at(n), 1
        )
        for h in range(2):
            _, outer, inner = end_rows(mine_ref, other_ref, index_ref, 2 * n + h)
            at = (0, EDGE + 1)[h]
            patch_ref[n, 1, at : at + 1, :] = outer
            patch_ref[n, 2, at : at + 1, :] = inner
    seams = dot(turn, jnp.concatenate(near, axis=0).astype(BF16))
    seam_ref[...] = seams
    own_turned = dot(turn, jnp.concatenate(own, axis=0))
    patch_ref[:, 0, 1 : EDGE + 1, :] = own_turned.reshape(12, EDGE, CH)
    for r in range(3):
        for b in range(3):
            part = patch_ref[:, r, b : b + EDGE, :].astype(BF16)
            strip_ref[:, lanes(3 * r + b)] = as_rows(part)
    wide_ref[...] = dot(strip_ref[...], sides_ref[...])
    for n in range(12):
        strip_pre_ref[strip(n), :] = pick(wide_ref, n * EDGE, EDGE, index_ref[near_at(n) + 2])
    line_ref[:, 1 : EDGE + 1, :] = seams.reshape(12, EDGE, CH)
    triples(line_ref, line_cols_ref, (0, 1, 2))
    pre_ref[...] = staged_ref[:, lanes(0)]
    parts = []
    for side in range(4):
        rows = slice(side * tiles * EDGE, (side + 1) * tiles * EDGE)
        parts.append(dot(line_cols_ref[rows, :], sides_ref[: 3 * CH, lanes(side)]))
    add_sides(pre_ref, jnp.concatenate(parts, axis=0))
    fill_pad(pad_ref, gelu(pre_ref[...]).astype(BF16).astype(F32))
    put_seams(pad_ref, dot(turn, gelu(strip_pre_ref[...]).astype(BF16)))
    windows(pad_ref, cols2_ref)
    second_pre = dot(cols2_ref[...], early_ref[:, W2])
    delta = (gelu_slope(second_pre) * staged_ref[:, lanes(1)]).astype(BF16)
    delta_ref[...] = delta
    cells_ref[...] = delta.astype(F32)
    for n in range(12):
        for depth in range(2):
            rows = cells_ref[side_cells(n % tiles, n // tiles, depth), :]
            delta_ring_ref[n % tiles, n // tiles, depth] = rows.astype(BF16)
            if depth == 0:
                line_ref[n, 1 : EDGE + 1, :] = rows
    fine_ref[...] = as_cells(gelu(second_pre).astype(BF16).astype(F32))
    half = EDGE // 2
    for a in range(2):
        for b in range(2):
            part = fine_ref[:, pl.ds(a, half, 2), pl.ds(b, half, 2), :]
            down_cols_ref[:, lanes(2 * a + b)] = as_rows(part).astype(BF16)
    coarse_ref[...] = dot(down_cols_ref[...], early_ref[:512, TAIL]).astype(BF16)


def gradient_kernel(
    index_ref, turn_ref, early_ref, late_ref, pre_ref, strip_pre_ref, seam_ref, cols2_ref, strip_ref, down_cols_ref, delta_ref, line_ref,
    grad_ref, rest_ref,
    pad_ref, cols_ref, cols3_ref, split_ref, line_cols_ref, sides_ref,
):
    side_weights(late_ref, W2_BACK, sides_ref, 1, True)
    tiles = 3
    core = lax.axis_index("c")

    def put_grad(at, block):
        half = at // 11
        grad_ref[jnp.where(core == half, 0, 1), lanes(at % 11), :] = jnp.transpose(block)

    def across_rows(rows):
        return jnp.transpose(rows.astype(F32)).astype(BF16)

    split_ref[...] = jnp.zeros_like(split_ref)
    turn = turn_ref[...]
    down_grad = dot(across_rows(early_ref[512:704, TAIL]), down_cols_ref[...])
    for at in range(4):
        put_grad(18 + at, down_grad[:, lanes(at)])
    delta = delta_ref[...]
    second_grad = dot(across_rows(delta), cols2_ref[...])
    for at in range(9):
        put_grad(9 + at, second_grad[:, lanes(at)])
    pad_ref[...] = jnp.zeros_like(pad_ref)
    fill_pad(pad_ref, delta.astype(F32))
    windows(pad_ref, cols3_ref)
    inner = dot(cols3_ref[...], late_ref[:, W2_BACK])
    rest_ref[:768, lanes(0)] = pre_ref[...]
    rest_ref[:768, lanes(1)] = inner
    inner_delta = (gelu_slope(pre_ref[...]) * inner).astype(BF16)
    triples(line_ref, line_cols_ref, (2, 1, 0))
    rims = []
    for side in range(4):
        rows = slice(side * tiles * EDGE, (side + 1) * tiles * EDGE)
        rims.append(dot(line_cols_ref[rows, :], sides_ref[:, lanes(side)]))
    sent = turned(turn, jnp.concatenate(rims, axis=0))
    rest_ref[768:, lanes(0)] = strip_pre_ref[...]
    rest_ref[768:, lanes(1)] = sent
    sent_delta = (gelu_slope(strip_pre_ref[...]) * sent).astype(BF16)
    for n in range(12):
        chosen = pl.ds(pl.multiple_of(index_ref[near_at(n) + 2] * CH, CH), CH)
        split_ref[strip(n), chosen] = sent_delta[strip(n)]
    sent_grad = dot(across_rows(split_ref[...]), strip_ref[...])
    fill_pad(pad_ref, late_ref[:768, X].astype(F32))
    put_seams(pad_ref, seam_ref[...])
    windows(pad_ref, cols_ref)
    first_grad = dot(across_rows(inner_delta), cols_ref[...])
    for a in range(3):
        for b in range(3):
            block = first_grad[:, lanes(3 * a + b)]
            for side in range(4):
                for r in range(3):
                    for k in range(3):
                        if frame_source(side, r, k) == (a, b):
                            block = block + sent_grad[lanes(side), lanes(3 * r + k)]
            put_grad(3 * a + b, block)


def backward_kernel(
    index_ref, turn_ref, mine_ref, other_ref, late_ref, rest_ref,
    out_ref, flag_ref,
    pad_ref, cols_ref, line_ref, deep_ref, line_cols_ref, deep_cols_ref, ends_ref, wide_ref,
    strip_wide_ref, cot_ref, cells_ref, sides_ref, sides2_ref,
):
    side_weights(late_ref, W1_BACK, sides_ref, 1, True)
    side_weights(late_ref, W2_BACK, sides2_ref, 2, True)
    flag_ref[...] = jnp.zeros_like(flag_ref)
    turn = turn_ref[...]
    line_ref[...] = jnp.zeros_like(line_ref)
    deep_ref[...] = jnp.zeros_like(deep_ref)
    ends_ref[...] = jnp.zeros_like(ends_ref)
    pad_ref[...] = jnp.zeros_like(pad_ref)
    for n in range(12):
        for depth, rows_ref in ((0, line_ref), (1, deep_ref)):
            rows_ref[n, 1 : EDGE + 1, :] = table_row(
                mine_ref, other_ref, index_ref, near_at(n), depth
            )
    for j in range(24):
        far, outer, inner = end_rows(mine_ref, other_ref, index_ref, j)
        blank = jnp.zeros_like(inner)
        ends_ref[j : j + 1, lanes(0)] = jnp.where(far, blank, inner)
        ends_ref[j : j + 1, lanes(1)] = outer
        ends_ref[j : j + 1, lanes(2)] = jnp.where(far, inner, blank)
    strip_rows = 12 * EDGE
    triples(line_ref, line_cols_ref, (2, 1, 0))
    line_cols_ref[strip_rows:, :] = ends_ref[...].astype(BF16)
    triples(deep_ref, deep_cols_ref, (2, 1, 0))
    wide_ref[...] = dot(line_cols_ref[...], sides2_ref[: 3 * CH])
    strip_wide_ref[...] = dot(deep_cols_ref[...], sides2_ref[: 3 * CH]) + dot(
        line_cols_ref[:strip_rows, :], sides2_ref[3 * CH :]
    )
    cot_ref[...] = rest_ref[768:, lanes(1)]
    rims = []
    for n in range(12):
        side = index_ref[near_at(n) + 2]
        rims.append(pick(wide_ref, n * EDGE, EDGE, side))
        cot_ref[strip(n), :] += pick(strip_wide_ref, n * EDGE, EDGE, side)
        for h in range(2):
            j = 2 * n + h
            at = n * EDGE + (0, EDGE - 1)[h]
            cot_ref[at : at + 1, :] += pick(
                wide_ref, strip_rows + j, 1, index_ref[lateral_at(j) + 2]
            )
    cells_ref[...] = rest_ref[:768, lanes(1)]
    add_sides(cells_ref, turned(turn, jnp.concatenate(rims, axis=0)))
    delta = gelu_slope(rest_ref[:768, lanes(0)]) * cells_ref[...]
    fill_pad(pad_ref, delta.astype(BF16).astype(F32))
    windows(pad_ref, cols_ref)
    strip_delta = (gelu_slope(rest_ref[768:, lanes(0)]) * cot_ref[...]).astype(BF16).astype(F32)
    line_ref[:, 1 : EDGE + 1, :] = strip_delta.reshape(12, EDGE, CH)
    triples(line_ref, deep_cols_ref, (2, 1, 0))
    strip_wide_ref[...] = dot(deep_cols_ref[...], sides_ref[...])
    rims = []
    for n in range(12):
        rims.append(pick(strip_wide_ref, n * EDGE, EDGE, index_ref[near_at(n) + 2]))
    cells_ref[...] = dot(cols_ref[...], late_ref[:, W1_BACK])
    add_sides(cells_ref, turned(turn, jnp.concatenate(rims, axis=0)))
    out_ref[...] = as_cells(cells_ref[...]).astype(BF16)


def first_table_kernel(*refs):
    table_ref = refs[-1]
    for at in range(4):
        table_ref[at, 0] = refs[at][...]
        table_ref[at, 1] = refs[4 + at][...]


def gate_kernel(*refs):
    refs[-1][...] = jnp.zeros_like(refs[-1])


def table_kernel(own_ref, one_ref, two_ref, three_ref, table_ref):
    for at, part_ref in enumerate((own_ref, one_ref, two_ref, three_ref)):
        table_ref[at] = part_ref[...]


def spread_sum(pieces_ref, copies_ref):
    total = jnp.sum(pieces_ref[...].astype(F32), axis=0).astype(BF16)
    for at in range(copies_ref.shape[0]):
        copies_ref[at] = total


def first_sum_kernel(pieces_ref, flag_ref, own_ref, across_ref, copies_ref, pair_ref):
    spread_sum(pieces_ref, copies_ref)
    pair_ref[0] = own_ref[...]
    pair_ref[1] = across_ref[...]


def second_sum_kernel(
    pieces_ref, flag_ref, own_ref, one_ref, two_ref, three_ref, copies_ref, table_ref
):
    spread_sum(pieces_ref, copies_ref)
    table_kernel(own_ref, one_ref, two_ref, three_ref, table_ref)


def keep_kernel(grads_ref, got_ref, kept_ref):
    kept_ref[...] = (grads_ref[0] + got_ref[...]).astype(BF16)


def hold_kernel(block_ref, flag_ref, out_ref):
    out_ref[...] = block_ref[...]


def finish_kernel(scale, mine_ref, other_ref, first_ref, second_ref, down_ref):
    core = lax.axis_index("c")
    for at in range(22):
        half = at // 11
        rows = slice(at % 11 * CH, (at % 11 + 1) * CH)
        block = jnp.where(core == half, mine_ref[rows, :], other_ref[rows, :])
        out_ref, base = ((first_ref, 0), (second_ref, 9), (down_ref, 18))[at // 9]
        out_ref[at - base] = block.astype(F32) * scale


def whole(space):
    return pl.BlockSpec(memory_space=space)


def shards(
    activations,
    conv1_weight,
    conv2_weight,
    coarse_kernel_weight,
    skip_cotangent,
    down_cotangent,
    face_neighbours,
    seam_codes,
    tile_slots,
):
    x = activations[0]
    tiles = x.shape[0]
    total_tiles = tile_slots.shape[0]
    cells = tiles * EDGE * EDGE
    strips = 4 * tiles * EDGE
    half = EDGE // 2
    quarter = tiles * half * half
    smem, vmem, hbm = whole(pltpu.SMEM), whole(pltpu.VMEM), whole(pltpu.HBM)
    shape = jax.ShapeDtypeStruct
    plane = lax.axis_size(PLANE)
    deep = lax.axis_size(DEPTH)
    pad = shape((tiles, EDGE + 2, EDGE + 8, CH), F32)
    line = shape((4 * tiles, EDGE + 8, CH), F32)
    ring = shape((tiles, 4, 2, EDGE, CH), BF16)

    def call(
        kernel, outs, operands, scratch=(), sems=(), specs=None, out_specs=None, cost=1, room=24
    ):
        single = not isinstance(outs, tuple)
        scratch = [pltpu.VMEM(one.shape, one.dtype) for one in scratch]
        scratch += [pltpu.SemaphoreType.DMA((count,)) for count in sems]
        return pl.pallas_call(
            kernel,
            out_shape=outs,
            in_specs=specs or [vmem] * len(operands),
            out_specs=out_specs or (vmem if single else (vmem,) * len(outs)),
            scratch_shapes=scratch,
            compiler_params=pltpu.CompilerParams(vmem_limit_bytes=room * 1024 * 1024),
            cost_estimate=pl.CostEstimate(
                flops=cost * cells * 18 * CH * CH, bytes_accessed=2 * 1024 * 1024, transcendentals=0
            ),
        )(*operands)

    wide = shape((strips, 4 * CH), F32)
    all_cols = shape((cells, 9 * CH), BF16)
    cell_rows = shape((cells, CH), F32)
    strip_rows = shape((strips, CH), F32)
    flag = shape((8, CH), F32)
    own_ring = call(ring_kernel, ring, [x], [cell_rows])
    across = swap_apart(own_ring, "z", 1)
    operands = [
        x,
        skip_cotangent[0],
        down_cotangent.reshape(-1, CH),
        conv1_weight.reshape(9 * CH, CH),
        conv2_weight.reshape(9 * CH, CH),
        coarse_kernel_weight.reshape(4 * CH, CH),
    ]
    turn_shape = shape((strips, strips), BF16)
    index, turn = call(
        index_kernel,
        (shape((296,), jnp.int32), turn_shape),
        [face_neighbours.T, seam_codes.T, tile_slots],
        [turn_shape],
        (1,),
        specs=[smem] * 3,
        out_specs=(smem, hbm),
        cost=4,
        room=60,
    )
    staged = (
        shape((9 * CH, 3 * CH), BF16),
        shape((9 * CH, 3 * CH), BF16),
        shape((cells, 2 * CH), F32),
    )
    ready, early, late, staged_cells = call(
        stage_kernel,
        (shape((8,), jnp.int32),) + staged,
        [index] + operands,
        tuple(operands) + staged
        + (pad, shape(x.shape, F32), all_cols, shape((CH, 4 * CH), BF16)),
        (len(operands), len(staged)),
        specs=[smem] + [hbm] * 6,
        out_specs=(smem,) + (hbm,) * 3,
        cost=100,
        room=50,
    )
    near_rings = [own_ring] + [swap_apart(own_ring, "y", apart) for apart in (1, 2, 3)]
    far_rings = [across] + [swap_apart(across, "y", apart) for apart in (1, 2, 3)]
    mine = call(
        first_table_kernel,
        shape((4, 2) + ring.shape, BF16),
        near_rings + far_rings + [index, ready],
        specs=[vmem] * 8 + [smem] * 2,
    )
    other = swap_core(mine)

    def table(block):
        return block.reshape((-1,) + ring.shape[1:])

    (
        coarse, delta_ring, pre, strip_pre, seam, cols2, strip_cols, down_cols, delta, line_rows,
    ) = call(
        forward_kernel,
        (
            shape((quarter, CH), BF16),
            ring,
            cell_rows,
            strip_rows,
            strip_rows,
            all_cols,
            shape((strips, 9 * CH), BF16),
            shape((quarter, 4 * CH), BF16),
            shape((cells, CH), BF16),
            line,
        ),
        [index, turn, table(mine), table(other), early, staged_cells],
        [
            pad,
            shape((4 * tiles, 3, EDGE + 8, CH), F32),
            wide,
            shape(x.shape, F32),
            cell_rows,
            shape((strips, 3 * CH), BF16),
            shape((9 * CH, 4 * CH), BF16),
        ],
        specs=[smem] + [vmem] * 5,
        cost=2,
    )
    grads, rest = call(
        gradient_kernel,
        (shape((2, 11 * CH, CH), F32), shape((cells + strips, 2 * CH), F32)),
        [
            index, turn, early, late, pre, strip_pre, seam, cols2, strip_cols, down_cols, delta,
            line_rows,
        ],
        [
            pad,
            all_cols,
            all_cols,
            shape((strips, 4 * CH), BF16),
            shape((strips, 3 * CH), BF16),
            shape((3 * CH, 4 * CH), BF16),
        ],
        specs=[smem] + [vmem] * 11,
        cost=4,
    )
    kept = call(keep_kernel, shape(grads.shape[1:], BF16), [grads, swap_core(grads[1])])
    part = kept.shape[0] // plane
    across = swap_apart(delta_ring, "z", 1)
    pieces = lax.all_to_all(kept.reshape(plane, part, CH), PLANE, 0, 0)
    copies, pair = call(
        first_sum_kernel,
        (shape((deep, part, CH), BF16), shape((2,) + ring.shape, BF16)),
        [pieces, call(gate_kernel, flag, [across], cost=100), delta_ring, across],
    )
    along = [swap_apart(pair, "y", apart) for apart in (1, 2, 3)]
    pieces = lax.all_to_all(copies, DEPTH, 0, 0)
    copies, mine = call(
        second_sum_kernel,
        (shape((plane, part, CH), BF16), shape((4,) + pair.shape, BF16)),
        [pieces, call(gate_kernel, flag, along, cost=100), pair] + along,
    )
    other = swap_core(mine)
    summed = lax.all_to_all(copies, PLANE, 0, 0).reshape(-1, CH)
    input_grad, done = call(
        backward_kernel,
        (shape(x.shape, BF16), flag),
        [index, turn, table(mine), table(other), late, rest],
        [
            pad,
            all_cols,
            line,
            line,
            shape((strips + 32, 3 * CH), BF16),
            shape((strips, 3 * CH), BF16),
            shape((32, 3 * CH), F32),
            shape((strips + 32, 4 * CH), F32),
            wide,
            strip_rows,
            cell_rows,
            shape((3 * CH, 4 * CH), BF16),
            shape((6 * CH, 4 * CH), BF16),
        ],
        specs=[smem] + [vmem] * 5,
        cost=100,
    )
    summed = call(hold_kernel, shape(summed.shape, BF16), [summed, done])
    scale = 1.0 / math.sqrt(lax.axis_size(("w", "x")) * total_tiles * EDGE * EDGE)
    first_grad, second_grad, down_grad = call(
        functools.partial(finish_kernel, scale),
        tuple(shape((count, CH, CH), F32) for count in (9, 9, 4)),
        [summed, swap_core(summed)],
    )
    return (
        coarse.reshape((1, tiles, half, half, CH)),
        input_grad[None],
        first_grad.reshape(conv1_weight.shape),
        second_grad.reshape(conv2_weight.shape),
        down_grad.reshape(coarse_kernel_weight.shape),
    )


def solution(mesh):
    batch = mesh.shape["batch"]
    along_x = 4 if batch % 4 == 0 else 1
    fine = Mesh(
        mesh.devices.reshape(4, 2, 2, batch // along_x, along_x), ("y", "z", "c", "w", "x")
    )
    field = P(("w", "x"), ("y", "z", "c"), None, None, None)
    return jax.shard_map(
        shards,
        mesh=fine,
        in_specs=(field, P(), P(), P(), field, field, P(), P(), P()),
        out_specs=(field, field, P(), P(), P()),
        check_vma=False,
    )
```

```python
import functools
import math

import jax
import jax.numpy as jnp
from jax import lax
from jax.experimental import pallas as pl
from jax.experimental.pallas import tpu as pltpu
from jax.sharding import Mesh
from jax.sharding import PartitionSpec as P

PLANE = ("x", "y")
DEPTH = ("z", "w")
SLOPE = math.sqrt(2.0 / math.pi)
CUBIC = 0.044715
BF16 = jnp.bfloat16
F32 = jnp.float32
EDGE = 16
CH = 128


def swap_core(block):
    return lax.ppermute(block, "c", [(0, 1), (1, 0)])


def swap_apart(block, axis, apart):
    number = lax.axis_size(axis)
    return lax.ppermute(block, axis, [(i, i ^ apart) for i in range(number)])


def fetch(sources, targets, sems):
    copies = []
    for at, (source, target) in enumerate(zip(sources, targets)):
        copies.append(pltpu.make_async_copy(source, target, sems.at[at]))
        copies[-1].start()
    return copies


def finish(copies):
    for copy in copies:
        copy.wait()


def gelu(v):
    return 0.5 * v * (1.0 + jnp.tanh(SLOPE * (v + CUBIC * v * v * v)))


def gelu_slope(v):
    t = jnp.tanh(SLOPE * (v + CUBIC * v * v * v))
    return 0.5 * (1.0 + t) + (0.5 * SLOPE) * v * (1.0 - t * t) * (1.0 + (3.0 * CUBIC) * v * v)


def dot(left, right):
    return jnp.dot(left, right, preferred_element_type=F32)


def turned(turn, rows):
    high = rows.astype(BF16)
    low = (rows - high.astype(F32)).astype(BF16)
    return dot(turn, high) + dot(turn, low)


def as_rows(block):
    return block.reshape(-1, CH)


def lanes(at, count=1):
    return slice(at * CH, (at + count) * CH)


def strip(n):
    return slice(n * EDGE, (n + 1) * EDGE)


def as_cells(rows):
    return rows.reshape(-1, EDGE, EDGE, CH)


def fill_pad(pad_ref, rows):
    pad_ref[:, 1 : EDGE + 1, 1 : EDGE + 1, :] = as_cells(rows)


def windows(pad_ref, cols_ref):
    for a in range(3):
        for b in range(3):
            part = pad_ref[:, a : a + EDGE, b : b + EDGE, :].astype(BF16)
            cols_ref[:, lanes(3 * a + b)] = as_rows(part)


def triples(line_ref, cols_ref, order):
    for at, start in enumerate(order):
        part = line_ref[:, start : start + EDGE, :].astype(BF16)
        cols_ref[0 : line_ref.shape[0] * EDGE, lanes(at)] = as_rows(part)


def pick(rows_ref, at, count, side):
    chosen = pl.ds(pl.multiple_of(side * CH, CH), CH)
    return rows_ref[pl.ds(at, count), chosen]


def side_cells(tile, side, depth=0):
    near = (depth, EDGE - 1 - depth)[side in (1, 2)]
    if side % 2 == 0:
        return pl.ds(tile * EDGE * EDGE + near * EDGE, EDGE)
    return pl.ds(tile * EDGE * EDGE + near, EDGE, EDGE)


def add_sides(cells_ref, rows):
    for n in range(12):
        cells = side_cells(n % 3, n // 3)
        cells_ref[cells, :] = cells_ref[cells, :] + rows[strip(n)]


def put_seams(pad_ref, rows):
    for n in range(12):
        side, k = n // 3, n % 3
        place = (0, EDGE + 1, EDGE + 1, 0)[side]
        seam = rows[strip(n)]
        if side % 2 == 0:
            pad_ref[k, place, 1 : EDGE + 1, :] = seam
        else:
            for i in range(EDGE):
                pad_ref[k, 1 + i, place : place + 1, :] = seam[i : i + 1]


def near_at(n):
    return 8 * n


def lateral_at(j):
    return 96 + 8 * j


def frame_source(side, r, k):
    return ((r, k), (k, 2 - r), (2 - r, k), (k, r))[side]


def ring_kernel(x_ref, ring_ref, cells_ref):
    cells_ref[:768] = as_rows(x_ref[...]).astype(F32)
    for n in range(12):
        for depth in range(2):
            rows = cells_ref[side_cells(n % 3, n // 3, depth), :].astype(BF16)
            ring_ref[n % 3, n // 3, depth] = rows


W1, W2, TAIL = slice(0, 128), slice(128, 256), slice(256, 384)
W2_BACK, W1_BACK, X = slice(0, 128), slice(128, 256), slice(256, 384)


def side_weights(source_ref, chosen, sides_ref, depth, back=False):
    for side in range(4):
        for r in range(depth):
            for k in range(3):
                a, b = frame_source(side, r, k)
                at = 8 - 3 * a - b if back else 3 * a + b
                sides_ref[lanes(3 * r + k), lanes(side)] = source_ref[lanes(at), chosen]


def index_kernel(near_ref, code_ref, slot_ref, index_ref, turn_hbm, turn_ref, sems):
    total = slot_ref.shape[0]
    tiles = 3
    core = lax.axis_index("c")
    at_y = lax.axis_index("y")
    at_z = lax.axis_index("z")
    first = ((at_y * 2 + at_z) * 2 + core) * tiles

    def look(i, found):
        here = slot_ref[i]
        return tuple(jnp.where(here == first + k, i, found[k]) for k in range(tiles))

    own = lax.fori_loop(0, total, look, (jnp.int32(0),) * tiles, unroll=8)

    def place(at, tile):
        slot = slot_ref[tile]
        owner = (slot * 171) >> 9
        local = slot - owner * tiles
        chip = ((owner >> 2) ^ at_y) * 2 + (((owner >> 1) & 1) ^ at_z)
        index_ref[at] = (owner + core) & 1
        index_ref[at + 1] = chip * tiles + local

    column = lax.broadcasted_iota(jnp.int32, (EDGE, 12 * EDGE), 1)
    row = lax.broadcasted_iota(jnp.int32, (EDGE, 12 * EDGE), 0)
    for n in range(12):
        side, k = n // tiles, n % tiles
        near = near_ref[side, own[k]]
        code = code_ref[side, own[k]]
        near_side = code >> 1
        reverse = code & 1
        place(near_at(n), near)
        index_ref[near_at(n) + 2] = near_side
        source = jnp.where(reverse == 1, EDGE - 1 - row, row) + n * EDGE
        turn_ref[strip(n), :] = jnp.where(column == source, 1.0, 0.0).astype(F32).astype(BF16)
        upright = near_side & 1
        far = jnp.where((near_side == 1) | (near_side == 2), 1, 0)
        for h in range(2):
            lateral = jnp.where(upright == 1, (0, 2)[h], (3, 1)[h])
            at = lateral_at(2 * n + h)
            place(at, near_ref[lateral, near])
            lateral_code = code_ref[lateral, near]
            index_ref[at + 2] = lateral_code >> 1
            index_ref[at + 3] = (far + lateral_code) & 1

    finish(fetch([turn_ref], [turn_hbm], sems))


def stage_kernel(
    index_ref, x_hbm, skip_hbm, down_hbm, w1_hbm, w2_hbm, wc_hbm,
    flag_ref, early_hbm, late_hbm, cells_hbm,
    x_ref, skip_ref, down_ref, w1_ref, w2_ref, wc_ref,
    early_ref, late_ref, cells_ref,
    pad_ref, cot_ref, cols_ref, wc_back_ref, in_sems, out_sems,
):
    arrivals = fetch(
        (w1_hbm, w2_hbm, wc_hbm, x_hbm, down_hbm, skip_hbm),
        (w1_ref, w2_ref, wc_ref, x_ref, down_ref, skip_ref),
        in_sems,
    )
    for at in range(8):
        flag_ref[at] = index_ref[at]
    pad_ref[...] = jnp.zeros_like(pad_ref)
    early_ref[704:, TAIL] = jnp.zeros_like(early_ref[704:, TAIL])
    late_ref[768:, X] = jnp.zeros_like(late_ref[768:, X])
    finish(arrivals)
    early_ref[:, W1] = w1_ref[...]
    early_ref[:, W2] = w2_ref[...]
    early_ref[:512, TAIL] = wc_ref[...]
    down = down_ref[...]
    early_ref[512:704, TAIL] = down
    x_rows = as_rows(x_ref[...])
    late_ref[:768, X] = x_rows
    departures = fetch([early_ref], [early_hbm], out_sems)

    def flip(block):
        return jnp.transpose(block.astype(F32)).astype(BF16)

    for a in range(3):
        for b in range(3):
            back = lanes(8 - 3 * a - b)
            late_ref[back, W1_BACK] = flip(w1_ref[lanes(3 * a + b), :])
            late_ref[back, W2_BACK] = flip(w2_ref[lanes(3 * a + b), :])
    last = pltpu.make_async_copy(late_ref, late_hbm, out_sems.at[1])
    last.start()
    departures.append(last)
    for at in range(4):
        wc_back_ref[:, lanes(at)] = flip(wc_ref[lanes(at), :])
    spread_down = dot(down, wc_back_ref[...])
    half = EDGE // 2
    for a in range(2):
        for b in range(2):
            part = spread_down[:, lanes(2 * a + b)].reshape(-1, half, half, CH)
            cot_ref[:, pl.ds(a, half, 2), pl.ds(b, half, 2), :] = part
    spread_rows = cot_ref[:, :EDGE, :EDGE, :]
    cells_ref[:, lanes(1)] = as_rows(spread_rows + skip_ref[...].astype(F32))
    fill_pad(pad_ref, x_rows.astype(F32))
    windows(pad_ref, cols_ref)
    cells_ref[:, lanes(0)] = dot(cols_ref[...], w1_ref[...])
    last = pltpu.make_async_copy(cells_ref, cells_hbm, out_sems.at[2])
    last.start()
    finish(departures + [last])


def table_row(mine_ref, other_ref, index_ref, at, depth):
    slot = index_ref[at + 1]
    side = index_ref[at + 2]
    mine = mine_ref[slot, side, depth]
    other = other_ref[slot, side, depth]
    return jnp.where(index_ref[at] == 0, mine.astype(F32), other.astype(F32))


def end_rows(mine_ref, other_ref, index_ref, j):
    row = table_row(mine_ref, other_ref, index_ref, lateral_at(j), 0)
    far = index_ref[lateral_at(j) + 3] == 1
    last = EDGE - 1
    return far, jnp.where(far, row[last:], row[:1]), jnp.where(far, row[last - 1 : last], row[1:2])


def forward_kernel(
    index_ref, turn_ref, mine_ref, other_ref, early_ref, staged_ref,
    coarse_ref, delta_ring_ref, pre_ref, strip_pre_ref, seam_ref, cols2_ref, strip_ref,
    down_cols_ref, delta_ref, line_ref,
    pad_ref, patch_ref, wide_ref, fine_ref, cells_ref, line_cols_ref, sides_ref,
):
    tiles = 3
    side_weights(early_ref, W1, sides_ref, 3)
    patch_ref[...] = jnp.zeros_like(patch_ref)
    pad_ref[...] = jnp.zeros_like(pad_ref)
    line_ref[...] = jnp.zeros_like(line_ref)
    turn = turn_ref[...]
    near = []
    own = []
    for n in range(12):
        own.append(mine_ref[n % tiles, n // tiles, 0])
        edge = table_row(mine_ref, other_ref, index_ref, near_at(n), 0)
        near.append(edge)
        patch_ref[n, 1, 1 : EDGE + 1, :] = edge
        patch_ref[n, 2, 1 : EDGE + 1, :] = table_row(
            mine_ref, other_ref, index_ref, near_at(n), 1
        )
        for h in range(2):
            _, outer, inner = end_rows(mine_ref, other_ref, index_ref, 2 * n + h)
            at = (0, EDGE + 1)[h]
            patch_ref[n, 1, at : at + 1, :] = outer
            patch_ref[n, 2, at : at + 1, :] = inner
    seams = dot(turn, jnp.concatenate(near, axis=0).astype(BF16))
    seam_ref[...] = seams
    own_turned = dot(turn, jnp.concatenate(own, axis=0))
    patch_ref[:, 0, 1 : EDGE + 1, :] = own_turned.reshape(12, EDGE, CH)
    for r in range(3):
        for b in range(3):
            part = patch_ref[:, r, b : b + EDGE, :].astype(BF16)
            strip_ref[:, lanes(3 * r + b)] = as_rows(part)
    wide_ref[...] = dot(strip_ref[...], sides_ref[...])
    for n in range(12):
        strip_pre_ref[strip(n), :] = pick(wide_ref, n * EDGE, EDGE, index_ref[near_at(n) + 2])
    line_ref[:, 1 : EDGE + 1, :] = seams.reshape(12, EDGE, CH)
    triples(line_ref, line_cols_ref, (0, 1, 2))
    cells_ref[:768] = staged_ref[:, lanes(0)]
    parts = []
    for side in range(4):
        rows = slice(side * tiles * EDGE, (side + 1) * tiles * EDGE)
        parts.append(dot(line_cols_ref[rows, :], sides_ref[: 3 * CH, lanes(side)]))
    add_sides(cells_ref, jnp.concatenate(parts, axis=0))
    first_pre = cells_ref[:768]
    pre_ref[...] = first_pre
    fill_pad(pad_ref, gelu(first_pre).astype(BF16).astype(F32))
    put_seams(pad_ref, dot(turn, gelu(strip_pre_ref[...]).astype(BF16)))
    windows(pad_ref, cols2_ref)
    second_pre = dot(cols2_ref[...], early_ref[:, W2])
    delta = (gelu_slope(second_pre) * staged_ref[:, lanes(1)]).astype(BF16)
    delta_ref[...] = delta
    cells_ref[:768] = delta.astype(F32)
    for n in range(12):
        for depth in range(2):
            rows = cells_ref[side_cells(n % tiles, n // tiles, depth), :]
            delta_ring_ref[n % tiles, n // tiles, depth] = rows.astype(BF16)
            if depth == 0:
                line_ref[n, 1 : EDGE + 1, :] = rows
    fine_ref[:, :EDGE, :EDGE, :] = as_cells(gelu(second_pre).astype(BF16).astype(F32))
    half = EDGE // 2
    for a in range(2):
        for b in range(2):
            part = fine_ref[:, pl.ds(a, half, 2), pl.ds(b, half, 2), :]
            down_cols_ref[:, lanes(2 * a + b)] = as_rows(part).astype(BF16)
    coarse_ref[...] = dot(down_cols_ref[...], early_ref[:512, TAIL]).astype(BF16)


def gradient_kernel(
    index_ref, turn_ref, early_ref, late_ref, pre_ref, strip_pre_ref, seam_ref, cols2_ref, strip_ref, down_cols_ref, delta_ref, line_ref,
    grad_ref, rest_ref,
    pad_ref, cols_ref, cols3_ref, split_ref, line_cols_ref, sides_ref,
):
    side_weights(late_ref, W2_BACK, sides_ref, 1, True)
    tiles = 3
    core = lax.axis_index("c")

    def put_grad(at, block):
        half = at // 11
        grad_ref[jnp.where(core == half, 0, 1), lanes(at % 11), :] = jnp.transpose(block)

    def across_rows(rows):
        return jnp.transpose(rows.astype(F32)).astype(BF16)

    split_ref[...] = jnp.zeros_like(split_ref)
    turn = turn_ref[...]
    down_grad = dot(across_rows(early_ref[512:704, TAIL]), down_cols_ref[...])
    for at in range(4):
        put_grad(18 + at, down_grad[:, lanes(at)])
    delta = delta_ref[...]
    second_grad = dot(across_rows(delta), cols2_ref[...])
    for at in range(9):
        put_grad(9 + at, second_grad[:, lanes(at)])
    pad_ref[...] = jnp.zeros_like(pad_ref)
    fill_pad(pad_ref, delta.astype(F32))
    windows(pad_ref, cols3_ref)
    inner = dot(cols3_ref[...], late_ref[:, W2_BACK])
    rest_ref[:768, lanes(0)] = pre_ref[...]
    rest_ref[:768, lanes(1)] = inner
    inner_delta = (gelu_slope(pre_ref[...]) * inner).astype(BF16)
    triples(line_ref, line_cols_ref, (2, 1, 0))
    rims = []
    for side in range(4):
        rows = slice(side * tiles * EDGE, (side + 1) * tiles * EDGE)
        rims.append(dot(line_cols_ref[rows, :], sides_ref[:, lanes(side)]))
    sent = turned(turn, jnp.concatenate(rims, axis=0))
    rest_ref[768:, lanes(0)] = strip_pre_ref[...]
    rest_ref[768:, lanes(1)] = sent
    sent_delta = (gelu_slope(strip_pre_ref[...]) * sent).astype(BF16)
    for n in range(12):
        chosen = pl.ds(pl.multiple_of(index_ref[near_at(n) + 2] * CH, CH), CH)
        split_ref[strip(n), chosen] = sent_delta[strip(n)]
    sent_grad = dot(across_rows(split_ref[...]), strip_ref[...])
    fill_pad(pad_ref, late_ref[:768, X].astype(F32))
    put_seams(pad_ref, seam_ref[...])
    windows(pad_ref, cols_ref)
    first_grad = dot(across_rows(inner_delta), cols_ref[...])
    for a in range(3):
        for b in range(3):
            block = first_grad[:, lanes(3 * a + b)]
            for side in range(4):
                for r in range(3):
                    for k in range(3):
                        if frame_source(side, r, k) == (a, b):
                            block = block + sent_grad[lanes(side), lanes(3 * r + k)]
            put_grad(3 * a + b, block)


def backward_kernel(
    index_ref, turn_ref, mine_ref, other_ref, late_ref, rest_ref,
    out_ref, flag_ref,
    pad_ref, cols_ref, line_ref, deep_ref, line_cols_ref, deep_cols_ref, ends_ref, wide_ref,
    strip_wide_ref, cot_ref, cells_ref, sides_ref, sides2_ref,
):
    side_weights(late_ref, W1_BACK, sides_ref, 1, True)
    side_weights(late_ref, W2_BACK, sides2_ref, 2, True)
    flag_ref[...] = jnp.zeros_like(flag_ref)
    turn = turn_ref[...]
    line_ref[...] = jnp.zeros_like(line_ref)
    deep_ref[...] = jnp.zeros_like(deep_ref)
    ends_ref[...] = jnp.zeros_like(ends_ref)
    pad_ref[...] = jnp.zeros_like(pad_ref)
    for n in range(12):
        for depth, rows_ref in ((0, line_ref), (1, deep_ref)):
            rows_ref[n, 1 : EDGE + 1, :] = table_row(
                mine_ref, other_ref, index_ref, near_at(n), depth
            )
    for j in range(24):
        far, outer, inner = end_rows(mine_ref, other_ref, index_ref, j)
        blank = jnp.zeros_like(inner)
        ends_ref[j : j + 1, lanes(0)] = jnp.where(far, blank, inner)
        ends_ref[j : j + 1, lanes(1)] = outer
        ends_ref[j : j + 1, lanes(2)] = jnp.where(far, inner, blank)
    strip_rows = 12 * EDGE
    triples(line_ref, line_cols_ref, (2, 1, 0))
    line_cols_ref[strip_rows:, :] = ends_ref[...].astype(BF16)
    triples(deep_ref, deep_cols_ref, (2, 1, 0))
    wide_ref[...] = dot(line_cols_ref[...], sides2_ref[: 3 * CH])
    strip_wide_ref[...] = dot(deep_cols_ref[...], sides2_ref[: 3 * CH]) + dot(
        line_cols_ref[:strip_rows, :], sides2_ref[3 * CH :]
    )
    cot_ref[...] = rest_ref[768:, lanes(1)]
    rims = []
    for n in range(12):
        side = index_ref[near_at(n) + 2]
        rims.append(pick(wide_ref, n * EDGE, EDGE, side))
        cot_ref[strip(n), :] += pick(strip_wide_ref, n * EDGE, EDGE, side)
        for h in range(2):
            j = 2 * n + h
            at = n * EDGE + (0, EDGE - 1)[h]
            cot_ref[at : at + 1, :] += pick(
                wide_ref, strip_rows + j, 1, index_ref[lateral_at(j) + 2]
            )
    cells_ref[:768] = rest_ref[:768, lanes(1)]
    add_sides(cells_ref, turned(turn, jnp.concatenate(rims, axis=0)))
    delta = gelu_slope(rest_ref[:768, lanes(0)]) * cells_ref[:768]
    fill_pad(pad_ref, delta.astype(BF16).astype(F32))
    windows(pad_ref, cols_ref)
    strip_delta = (gelu_slope(rest_ref[768:, lanes(0)]) * cot_ref[...]).astype(BF16).astype(F32)
    line_ref[:, 1 : EDGE + 1, :] = strip_delta.reshape(12, EDGE, CH)
    triples(line_ref, deep_cols_ref, (2, 1, 0))
    strip_wide_ref[...] = dot(deep_cols_ref[...], sides_ref[...])
    rims = []
    for n in range(12):
        rims.append(pick(strip_wide_ref, n * EDGE, EDGE, index_ref[near_at(n) + 2]))
    cells_ref[:768] = dot(cols_ref[...], late_ref[:, W1_BACK])
    add_sides(cells_ref, turned(turn, jnp.concatenate(rims, axis=0)))
    out_ref[...] = as_cells(cells_ref[:768]).astype(BF16)


def first_table_kernel(*refs):
    table_ref = refs[-1]
    for at in range(4):
        table_ref[at, 0] = refs[at][...]
        table_ref[at, 1] = refs[4 + at][...]


def gate_kernel(*refs):
    refs[-1][...] = jnp.zeros_like(refs[-1])


def table_kernel(own_ref, one_ref, two_ref, three_ref, table_ref):
    for at, part_ref in enumerate((own_ref, one_ref, two_ref, three_ref)):
        table_ref[at] = part_ref[...]


def spread_sum(pieces_ref, copies_ref):
    total = jnp.sum(pieces_ref[...].astype(F32), axis=0).astype(BF16)
    for at in range(copies_ref.shape[0]):
        copies_ref[at] = total


def first_sum_kernel(pieces_ref, flag_ref, own_ref, across_ref, copies_ref, pair_ref):
    spread_sum(pieces_ref, copies_ref)
    pair_ref[0] = own_ref[...]
    pair_ref[1] = across_ref[...]


def second_sum_kernel(
    pieces_ref, flag_ref, own_ref, one_ref, two_ref, three_ref, copies_ref, table_ref
):
    spread_sum(pieces_ref, copies_ref)
    table_kernel(own_ref, one_ref, two_ref, three_ref, table_ref)


def keep_kernel(grads_ref, got_ref, kept_ref):
    kept_ref[...] = (grads_ref[0] + got_ref[...]).astype(BF16)


def hold_kernel(block_ref, flag_ref, out_ref):
    out_ref[...] = block_ref[...]


def finish_kernel(scale, mine_ref, other_ref, first_ref, second_ref, down_ref):
    core = lax.axis_index("c")
    for at in range(22):
        half = at // 11
        rows = slice(at % 11 * CH, (at % 11 + 1) * CH)
        block = jnp.where(core == half, mine_ref[rows, :], other_ref[rows, :])
        out_ref, base = ((first_ref, 0), (second_ref, 9), (down_ref, 18))[at // 9]
        out_ref[at - base] = block.astype(F32) * scale


def whole(space):
    return pl.BlockSpec(memory_space=space)


def shards(
    activations,
    conv1_weight,
    conv2_weight,
    coarse_kernel_weight,
    skip_cotangent,
    down_cotangent,
    face_neighbours,
    seam_codes,
    tile_slots,
):
    x = activations[0]
    tiles = x.shape[0]
    total_tiles = tile_slots.shape[0]
    cells = tiles * EDGE * EDGE
    strips = 4 * tiles * EDGE
    half = EDGE // 2
    quarter = tiles * half * half
    smem, vmem, hbm = whole(pltpu.SMEM), whole(pltpu.VMEM), whole(pltpu.HBM)
    shape = jax.ShapeDtypeStruct
    plane = lax.axis_size(PLANE)
    deep = lax.axis_size(DEPTH)
    pad = shape((tiles, EDGE + 2, EDGE + 8, CH), F32)
    line = shape((4 * tiles, EDGE + 8, CH), F32)
    ring = shape((tiles, 4, 2, EDGE, CH), BF16)

    def call(
        kernel, outs, operands, scratch=(), sems=(), specs=None, out_specs=None, cost=1, room=24
    ):
        single = not isinstance(outs, tuple)
        scratch = [pltpu.VMEM(one.shape, one.dtype) for one in scratch]
        scratch += [pltpu.SemaphoreType.DMA((count,)) for count in sems]
        return pl.pallas_call(
            kernel,
            out_shape=outs,
            in_specs=specs or [vmem] * len(operands),
            out_specs=out_specs or (vmem if single else (vmem,) * len(outs)),
            scratch_shapes=scratch,
            compiler_params=pltpu.CompilerParams(vmem_limit_bytes=room * 1024 * 1024),
            cost_estimate=pl.CostEstimate(
                flops=cost * cells * 18 * CH * CH, bytes_accessed=2 * 1024 * 1024, transcendentals=0
            ),
        )(*operands)

    wide = shape((strips, 4 * CH), F32)
    all_cols = shape((cells, 9 * CH), BF16)
    cell_rows = shape((cells, CH), F32)
    strip_rows = shape((strips, CH), F32)
    roomy_rows = shape((cells + EDGE * EDGE, CH), F32)
    flag = shape((8, CH), F32)
    own_ring = call(ring_kernel, ring, [x], [roomy_rows])
    across = swap_apart(own_ring, "z", 1)
    operands = [
        x,
        skip_cotangent[0],
        down_cotangent.reshape(-1, CH),
        conv1_weight.reshape(9 * CH, CH),
        conv2_weight.reshape(9 * CH, CH),
        coarse_kernel_weight.reshape(4 * CH, CH),
    ]
    turn_shape = shape((strips, strips), BF16)
    index, turn = call(
        index_kernel,
        (shape((296,), jnp.int32), turn_shape),
        [face_neighbours.T, seam_codes.T, tile_slots],
        [turn_shape],
        (1,),
        specs=[smem] * 3,
        out_specs=(smem, hbm),
        cost=4,
        room=60,
    )
    staged = (
        shape((9 * CH, 3 * CH), BF16),
        shape((9 * CH, 3 * CH), BF16),
        shape((cells, 2 * CH), F32),
    )
    ready, early, late, staged_cells = call(
        stage_kernel,
        (shape((8,), jnp.int32),) + staged,
        [index] + operands,
        tuple(operands) + staged
        + (pad, pad, all_cols, shape((CH, 4 * CH), BF16)),
        (len(operands), len(staged)),
        specs=[smem] + [hbm] * 6,
        out_specs=(smem,) + (hbm,) * 3,
        cost=100,
        room=50,
    )
    near_rings = [own_ring] + [swap_apart(own_ring, "y", apart) for apart in (1, 2, 3)]
    far_rings = [across] + [swap_apart(across, "y", apart) for apart in (1, 2, 3)]
    mine = call(
        first_table_kernel,
        shape((4, 2) + ring.shape, BF16),
        near_rings + far_rings + [index, ready],
        specs=[vmem] * 8 + [smem] * 2,
    )
    other = swap_core(mine)

    def table(block):
        return block.reshape((-1,) + ring.shape[1:])

    (
        coarse, delta_ring, pre, strip_pre, seam, cols2, strip_cols, down_cols, delta, line_rows,
    ) = call(
        forward_kernel,
        (
            shape((quarter, CH), BF16),
            ring,
            cell_rows,
            strip_rows,
            strip_rows,
            all_cols,
            shape((strips, 9 * CH), BF16),
            shape((quarter, 4 * CH), BF16),
            shape((cells, CH), BF16),
            line,
        ),
        [index, turn, table(mine), table(other), early, staged_cells],
        [
            pad,
            shape((4 * tiles, 3, EDGE + 8, CH), F32),
            wide,
            pad,
            roomy_rows,
            shape((strips, 3 * CH), BF16),
            shape((9 * CH, 4 * CH), BF16),
        ],
        specs=[smem] + [vmem] * 5,
        cost=2,
    )
    grads, rest = call(
        gradient_kernel,
        (shape((2, 11 * CH, CH), F32), shape((cells + strips, 2 * CH), F32)),
        [
            index, turn, early, late, pre, strip_pre, seam, cols2, strip_cols, down_cols, delta,
            line_rows,
        ],
        [
            pad,
            all_cols,
            all_cols,
            shape((strips, 4 * CH), BF16),
            shape((strips, 3 * CH), BF16),
            shape((3 * CH, 4 * CH), BF16),
        ],
        specs=[smem] + [vmem] * 11,
        cost=4,
    )
    kept = call(keep_kernel, shape(grads.shape[1:], BF16), [grads, swap_core(grads[1])])
    part = kept.shape[0] // plane
    across = swap_apart(delta_ring, "z", 1)
    pieces = lax.all_to_all(kept.reshape(plane, part, CH), PLANE, 0, 0)
    copies, pair = call(
        first_sum_kernel,
        (shape((deep, part, CH), BF16), shape((2,) + ring.shape, BF16)),
        [pieces, call(gate_kernel, flag, [across], cost=100), delta_ring, across],
    )
    along = [swap_apart(pair, "y", apart) for apart in (1, 2, 3)]
    pieces = lax.all_to_all(copies, DEPTH, 0, 0)
    copies, mine = call(
        second_sum_kernel,
        (shape((plane, part, CH), BF16), shape((4,) + pair.shape, BF16)),
        [pieces, call(gate_kernel, flag, along, cost=100), pair] + along,
    )
    other = swap_core(mine)
    summed = lax.all_to_all(copies, PLANE, 0, 0).reshape(-1, CH)
    input_grad, done = call(
        backward_kernel,
        (shape(x.shape, BF16), flag),
        [index, turn, table(mine), table(other), late, rest],
        [
            pad,
            all_cols,
            line,
            line,
            shape((strips + 32, 3 * CH), BF16),
            shape((strips, 3 * CH), BF16),
            shape((32, 3 * CH), F32),
            shape((strips + 32, 4 * CH), F32),
            wide,
            strip_rows,
            roomy_rows,
            shape((3 * CH, 4 * CH), BF16),
            shape((6 * CH, 4 * CH), BF16),
        ],
        specs=[smem] + [vmem] * 5,
        cost=100,
    )
    summed = call(hold_kernel, shape(summed.shape, BF16), [summed, done])
    scale = 1.0 / math.sqrt(lax.axis_size(("w", "x")) * total_tiles * EDGE * EDGE)
    first_grad, second_grad, down_grad = call(
        functools.partial(finish_kernel, scale),
        tuple(shape((count, CH, CH), F32) for count in (9, 9, 4)),
        [summed, swap_core(summed)],
    )
    return (
        coarse.reshape((1, tiles, half, half, CH)),
        input_grad[None],
        first_grad.reshape(conv1_weight.shape),
        second_grad.reshape(conv2_weight.shape),
        down_grad.reshape(coarse_kernel_weight.shape),
    )


def solution(mesh):
    batch = mesh.shape["batch"]
    along_x = 4 if batch % 4 == 0 else 1
    fine = Mesh(
        mesh.devices.reshape(4, 2, 2, batch // along_x, along_x), ("y", "z", "c", "w", "x")
    )
    field = P(("w", "x"), ("y", "z", "c"), None, None, None)
    return jax.shard_map(
        shards,
        mesh=fine,
        in_specs=(field, P(), P(), P(), field, field, P(), P(), P()),
        out_specs=(field, field, P(), P(), P()),
        check_vma=False,
    )
```

```python
import functools
import math

import jax
import jax.numpy as jnp
from jax import lax
from jax.experimental import pallas as pl
from jax.experimental.pallas import tpu as pltpu
from jax.sharding import Mesh
from jax.sharding import PartitionSpec as P

PLANE = ("x", "y")
DEPTH = ("z", "w")
SLOPE = math.sqrt(2.0 / math.pi)
CUBIC = 0.044715
BF16 = jnp.bfloat16
F32 = jnp.float32
EDGE = 16
CH = 128


def swap_core(block):
    return lax.ppermute(block, "c", [(0, 1), (1, 0)])


def swap_apart(block, axis, apart):
    number = lax.axis_size(axis)
    return lax.ppermute(block, axis, [(i, i ^ apart) for i in range(number)])


def fetch(sources, targets, sems):
    copies = []
    for at, (source, target) in enumerate(zip(sources, targets)):
        copies.append(pltpu.make_async_copy(source, target, sems.at[at]))
        copies[-1].start()
    return copies


def finish(copies):
    for copy in copies:
        copy.wait()


def gelu(v):
    return 0.5 * v * (1.0 + jnp.tanh(SLOPE * (v + CUBIC * v * v * v)))


def gelu_slope(v):
    t = jnp.tanh(SLOPE * (v + CUBIC * v * v * v))
    return 0.5 * (1.0 + t) + (0.5 * SLOPE) * v * (1.0 - t * t) * (1.0 + (3.0 * CUBIC) * v * v)


def dot(left, right):
    return jnp.dot(left, right, preferred_element_type=F32)


def turned(turn, rows):
    high = rows.astype(BF16)
    low = (rows - high.astype(F32)).astype(BF16)
    return dot(turn, high) + dot(turn, low)


def as_rows(block):
    return block.reshape(-1, CH)


def lanes(at, count=1):
    return slice(at * CH, (at + count) * CH)


def strip(n):
    return slice(n * EDGE, (n + 1) * EDGE)


def as_cells(rows):
    return rows.reshape(-1, EDGE, EDGE, CH)


def fill_pad(pad_ref, rows):
    pad_ref[:, 1 : EDGE + 1, 1 : EDGE + 1, :] = as_cells(rows)


def windows(pad_ref, cols_ref):
    for a in range(3):
        for b in range(3):
            part = pad_ref[:, a : a + EDGE, b : b + EDGE, :].astype(BF16)
            cols_ref[:, lanes(3 * a + b)] = as_rows(part)


def triples(line_ref, cols_ref, order):
    for at, start in enumerate(order):
        part = line_ref[:, start : start + EDGE, :].astype(BF16)
        cols_ref[0 : line_ref.shape[0] * EDGE, lanes(at)] = as_rows(part)


def pick(rows_ref, at, count, side):
    chosen = pl.ds(pl.multiple_of(side * CH, CH), CH)
    return rows_ref[pl.ds(at, count), chosen]


def side_cells(tile, side, depth=0):
    near = (depth, EDGE - 1 - depth)[side in (1, 2)]
    if side % 2 == 0:
        return pl.ds(tile * EDGE * EDGE + near * EDGE, EDGE)
    return pl.ds(tile * EDGE * EDGE + near, EDGE, EDGE)


def add_sides(cells_ref, rows):
    for n in range(12):
        cells = side_cells(n % 3, n // 3)
        cells_ref[cells, :] = cells_ref[cells, :] + rows[strip(n)]


def put_seams(pad_ref, rows):
    for n in range(12):
        side, k = n // 3, n % 3
        place = (0, EDGE + 1, EDGE + 1, 0)[side]
        seam = rows[strip(n)]
        if side % 2 == 0:
            pad_ref[k, place, 1 : EDGE + 1, :] = seam
        else:
            for i in range(EDGE):
                pad_ref[k, 1 + i, place : place + 1, :] = seam[i : i + 1]


def near_at(n):
    return 8 * n


def lateral_at(j):
    return 96 + 8 * j


def frame_source(side, r, k):
    return ((r, k), (k, 2 - r), (2 - r, k), (k, r))[side]


def ring_kernel(x_ref, ring_ref, cells_ref):
    cells_ref[:768] = as_rows(x_ref[...]).astype(F32)
    for n in range(12):
        for depth in range(2):
            rows = cells_ref[side_cells(n % 3, n // 3, depth), :].astype(BF16)
            ring_ref[n % 3, n // 3, depth] = rows


W1, W2, TAIL = slice(0, 128), slice(128, 256), slice(256, 384)
W2_BACK, W1_BACK, X = slice(0, 128), slice(128, 256), slice(256, 384)


def side_weights(source_ref, chosen, sides_ref, depth, back=False):
    for side in range(4):
        for r in range(depth):
            for k in range(3):
                a, b = frame_source(side, r, k)
                at = 8 - 3 * a - b if back else 3 * a + b
                sides_ref[lanes(3 * r + k), lanes(side)] = source_ref[lanes(at), chosen]


def index_kernel(near_ref, code_ref, slot_ref, index_ref, turn_hbm, turn_ref, sems):
    total = slot_ref.shape[0]
    tiles = 3
    core = lax.axis_index("c")
    at_y = lax.axis_index("y")
    at_z = lax.axis_index("z")
    first = ((at_y * 2 + at_z) * 2 + core) * tiles

    def look(i, found):
        here = slot_ref[i]
        return tuple(jnp.where(here == first + k, i, found[k]) for k in range(tiles))

    own = lax.fori_loop(0, total, look, (jnp.int32(0),) * tiles, unroll=8)

    def place(at, tile):
        slot = slot_ref[tile]
        owner = (slot * 171) >> 9
        local = slot - owner * tiles
        chip = ((owner >> 2) ^ at_y) * 2 + (((owner >> 1) & 1) ^ at_z)
        index_ref[at] = (owner + core) & 1
        index_ref[at + 1] = chip * tiles + local

    column = lax.broadcasted_iota(jnp.int32, (EDGE, 12 * EDGE), 1)
    row = lax.broadcasted_iota(jnp.int32, (EDGE, 12 * EDGE), 0)
    for n in range(12):
        side, k = n // tiles, n % tiles
        near = near_ref[side, own[k]]
        code = code_ref[side, own[k]]
        near_side = code >> 1
        reverse = code & 1
        place(near_at(n), near)
        index_ref[near_at(n) + 2] = near_side
        source = jnp.where(reverse == 1, EDGE - 1 - row, row) + n * EDGE
        turn_ref[strip(n), :] = jnp.where(column == source, 1.0, 0.0).astype(F32).astype(BF16)
        upright = near_side & 1
        far = jnp.where((near_side == 1) | (near_side == 2), 1, 0)
        for h in range(2):
            lateral = jnp.where(upright == 1, (0, 2)[h], (3, 1)[h])
            at = lateral_at(2 * n + h)
            place(at, near_ref[lateral, near])
            lateral_code = code_ref[lateral, near]
            index_ref[at + 2] = lateral_code >> 1
            index_ref[at + 3] = (far + lateral_code) & 1

    finish(fetch([turn_ref], [turn_hbm], sems))


def stage_kernel(
    index_ref, x_hbm, skip_hbm, down_hbm, w1_hbm, w2_hbm, wc_hbm,
    flag_ref, early_hbm, late_hbm, cells_hbm,
    x_ref, skip_ref, down_ref, w1_ref, w2_ref, wc_ref,
    early_ref, late_ref, cells_ref,
    pad_ref, cot_ref, cols_ref, wc_back_ref, in_sems, out_sems,
):
    arrivals = fetch(
        (w1_hbm, w2_hbm, wc_hbm, x_hbm, down_hbm, skip_hbm),
        (w1_ref, w2_ref, wc_ref, x_ref, down_ref, skip_ref),
        in_sems,
    )
    for at in range(8):
        flag_ref[at] = index_ref[at]
    pad_ref[...] = jnp.zeros_like(pad_ref)
    early_ref[704:, TAIL] = jnp.zeros_like(early_ref[704:, TAIL])
    late_ref[768:, X] = jnp.zeros_like(late_ref[768:, X])
    finish(arrivals)
    early_ref[:, W1] = w1_ref[...]
    early_ref[:, W2] = w2_ref[...]
    early_ref[:512, TAIL] = wc_ref[...]
    down = down_ref[...]
    early_ref[512:704, TAIL] = down
    x_rows = as_rows(x_ref[...])
    late_ref[:768, X] = x_rows
    departures = fetch([early_ref], [early_hbm], out_sems)

    def flip(block):
        return jnp.transpose(block.astype(F32)).astype(BF16)

    for a in range(3):
        for b in range(3):
            back = lanes(8 - 3 * a - b)
            late_ref[back, W1_BACK] = flip(w1_ref[lanes(3 * a + b), :])
            late_ref[back, W2_BACK] = flip(w2_ref[lanes(3 * a + b), :])
    last = pltpu.make_async_copy(late_ref, late_hbm, out_sems.at[1])
    last.start()
    departures.append(last)
    for at in range(4):
        wc_back_ref[:, lanes(at)] = flip(wc_ref[lanes(at), :])
    spread_down = dot(down, wc_back_ref[...])
    half = EDGE // 2
    for a in range(2):
        for b in range(2):
            part = spread_down[:, lanes(2 * a + b)].reshape(-1, half, half, CH)
            cot_ref[:, pl.ds(a, half, 2), pl.ds(b, half, 2), :] = part
    spread_rows = cot_ref[:, :EDGE, :EDGE, :]
    cells_ref[:, lanes(1)] = as_rows(spread_rows + skip_ref[...].astype(F32))
    fill_pad(pad_ref, x_rows.astype(F32))
    windows(pad_ref, cols_ref)
    cells_ref[:, lanes(0)] = dot(cols_ref[...], w1_ref[...])
    last = pltpu.make_async_copy(cells_ref, cells_hbm, out_sems.at[2])
    last.start()
    finish(departures + [last])


def table_row(mine_ref, other_ref, index_ref, at, depth):
    slot = index_ref[at + 1]
    side = index_ref[at + 2]
    mine = mine_ref[slot, side, depth]
    other = other_ref[slot, side, depth]
    return jnp.where(index_ref[at] == 0, mine.astype(F32), other.astype(F32))


def end_rows(mine_ref, other_ref, index_ref, j):
    row = table_row(mine_ref, other_ref, index_ref, lateral_at(j), 0)
    far = index_ref[lateral_at(j) + 3] == 1
    last = EDGE - 1
    return far, jnp.where(far, row[last:], row[:1]), jnp.where(far, row[last - 1 : last], row[1:2])


def forward_kernel(
    index_ref, turn_ref, mine_ref, other_ref, early_ref, staged_ref,
    coarse_ref, delta_ring_ref, pre_ref, strip_pre_ref, seam_ref, cols2_ref, strip_ref,
    down_cols_ref, delta_ref, line_ref,
    pad_ref, patch_ref, wide_ref, fine_ref, cells_ref, line_cols_ref, sides_ref,
):
    tiles = 3
    side_weights(early_ref, W1, sides_ref, 3)
    patch_ref[...] = jnp.zeros_like(patch_ref)
    pad_ref[...] = jnp.zeros_like(pad_ref)
    line_ref[...] = jnp.zeros_like(line_ref)
    turn = turn_ref[...]
    near = []
    own = []
    for n in range(12):
        own.append(mine_ref[n % tiles, n // tiles, 0])
        edge = table_row(mine_ref, other_ref, index_ref, near_at(n), 0)
        near.append(edge)
        patch_ref[n, 1, 1 : EDGE + 1, :] = edge
        patch_ref[n, 2, 1 : EDGE + 1, :] = table_row(
            mine_ref, other_ref, index_ref, near_at(n), 1
        )
        for h in range(2):
            _, outer, inner = end_rows(mine_ref, other_ref, index_ref, 2 * n + h)
            at = (0, EDGE + 1)[h]
            patch_ref[n, 1, at : at + 1, :] = outer
            patch_ref[n, 2, at : at + 1, :] = inner
    seams = dot(turn, jnp.concatenate(near, axis=0).astype(BF16))
    seam_ref[...] = seams
    own_turned = dot(turn, jnp.concatenate(own, axis=0))
    patch_ref[:, 0, 1 : EDGE + 1, :] = own_turned.reshape(12, EDGE, CH)
    for r in range(3):
        for b in range(3):
            part = patch_ref[:, r, b : b + EDGE, :].astype(BF16)
            strip_ref[:, lanes(3 * r + b)] = as_rows(part)
    wide_ref[...] = dot(strip_ref[...], sides_ref[...])
    for n in range(12):
        strip_pre_ref[strip(n), :] = pick(wide_ref, n * EDGE, EDGE, index_ref[near_at(n) + 2])
    line_ref[:, 1 : EDGE + 1, :] = seams.reshape(12, EDGE, CH)
    triples(line_ref, line_cols_ref, (0, 1, 2))
    cells_ref[:768] = staged_ref[:, lanes(0)]
    parts = []
    for side in range(4):
        rows = slice(side * tiles * EDGE, (side + 1) * tiles * EDGE)
        parts.append(dot(line_cols_ref[rows, :], sides_ref[: 3 * CH, lanes(side)]))
    add_sides(cells_ref, jnp.concatenate(parts, axis=0))
    first_pre = cells_ref[:768]
    pre_ref[...] = first_pre
    fill_pad(pad_ref, gelu(first_pre).astype(BF16).astype(F32))
    put_seams(pad_ref, dot(turn, gelu(strip_pre_ref[...]).astype(BF16)))
    windows(pad_ref, cols2_ref)
    second_pre = dot(cols2_ref[...], early_ref[:, W2])
    delta = (gelu_slope(second_pre) * staged_ref[:, lanes(1)]).astype(BF16)
    delta_ref[...] = delta
    cells_ref[:768] = delta.astype(F32)
    for n in range(12):
        for depth in range(2):
            rows = cells_ref[side_cells(n % tiles, n // tiles, depth), :]
            delta_ring_ref[n % tiles, n // tiles, depth] = rows.astype(BF16)
            if depth == 0:
                line_ref[n, 1 : EDGE + 1, :] = rows
    fine_ref[:, :EDGE, :EDGE, :] = as_cells(gelu(second_pre).astype(BF16).astype(F32))
    half = EDGE // 2
    for a in range(2):
        for b in range(2):
            part = fine_ref[:, pl.ds(a, half, 2), pl.ds(b, half, 2), :]
            down_cols_ref[:, lanes(2 * a + b)] = as_rows(part).astype(BF16)
    coarse_ref[...] = dot(down_cols_ref[...], early_ref[:512, TAIL]).astype(BF16)


def gradient_kernel(
    index_ref, turn_ref, early_ref, late_ref, pre_ref, strip_pre_ref, seam_ref, cols2_ref, strip_ref, down_cols_ref, delta_ref, line_ref,
    grad_ref, rest_ref,
    pad_ref, cols_ref, cols3_ref, split_ref, line_cols_ref, sides_ref,
):
    side_weights(late_ref, W2_BACK, sides_ref, 1, True)
    tiles = 3
    core = lax.axis_index("c")

    def put_grad(at, block):
        half = at // 11
        grad_ref[jnp.where(core == half, 0, 1), lanes(at % 11), :] = jnp.transpose(block)

    def across_rows(rows):
        return jnp.transpose(rows.astype(F32)).astype(BF16)

    split_ref[...] = jnp.zeros_like(split_ref)
    turn = turn_ref[...]
    down_grad = dot(across_rows(early_ref[512:704, TAIL]), down_cols_ref[...])
    for at in range(4):
        put_grad(18 + at, down_grad[:, lanes(at)])
    delta = delta_ref[...]
    second_grad = dot(across_rows(delta), cols2_ref[...])
    for at in range(9):
        put_grad(9 + at, second_grad[:, lanes(at)])
    pad_ref[...] = jnp.zeros_like(pad_ref)
    fill_pad(pad_ref, delta.astype(F32))
    windows(pad_ref, cols3_ref)
    inner = dot(cols3_ref[...], late_ref[:, W2_BACK])
    rest_ref[:768, lanes(0)] = pre_ref[...]
    rest_ref[:768, lanes(1)] = inner
    inner_delta = (gelu_slope(pre_ref[...]) * inner).astype(BF16)
    triples(line_ref, line_cols_ref, (2, 1, 0))
    rims = []
    for side in range(4):
        rows = slice(side * tiles * EDGE, (side + 1) * tiles * EDGE)
        rims.append(dot(line_cols_ref[rows, :], sides_ref[:, lanes(side)]))
    sent = turned(turn, jnp.concatenate(rims, axis=0))
    rest_ref[768:, lanes(0)] = strip_pre_ref[...]
    rest_ref[768:, lanes(1)] = sent
    sent_delta = (gelu_slope(strip_pre_ref[...]) * sent).astype(BF16)
    for n in range(12):
        chosen = pl.ds(pl.multiple_of(index_ref[near_at(n) + 2] * CH, CH), CH)
        split_ref[strip(n), chosen] = sent_delta[strip(n)]
    sent_grad = dot(across_rows(split_ref[...]), strip_ref[...])
    fill_pad(pad_ref, late_ref[:768, X].astype(F32))
    put_seams(pad_ref, seam_ref[...])
    windows(pad_ref, cols_ref)
    first_grad = dot(across_rows(inner_delta), cols_ref[...])
    for a in range(3):
        for b in range(3):
            block = first_grad[:, lanes(3 * a + b)]
            for side in range(4):
                for r in range(3):
                    for k in range(3):
                        if frame_source(side, r, k) == (a, b):
                            block = block + sent_grad[lanes(side), lanes(3 * r + k)]
            put_grad(3 * a + b, block)


def backward_kernel(
    index_ref, turn_ref, mine_ref, other_ref, late_ref, rest_ref,
    out_ref, flag_ref,
    pad_ref, cols_ref, line_ref, deep_ref, line_cols_ref, deep_cols_ref, ends_ref, wide_ref,
    strip_wide_ref, cot_ref, cells_ref, sides_ref, sides2_ref,
):
    side_weights(late_ref, W1_BACK, sides_ref, 1, True)
    side_weights(late_ref, W2_BACK, sides2_ref, 2, True)
    flag_ref[...] = jnp.zeros_like(flag_ref)
    turn = turn_ref[...]
    line_ref[...] = jnp.zeros_like(line_ref)
    deep_ref[...] = jnp.zeros_like(deep_ref)
    ends_ref[...] = jnp.zeros_like(ends_ref)
    pad_ref[...] = jnp.zeros_like(pad_ref)
    for n in range(12):
        for depth, rows_ref in ((0, line_ref), (1, deep_ref)):
            rows_ref[n, 1 : EDGE + 1, :] = table_row(
                mine_ref, other_ref, index_ref, near_at(n), depth
            )
    for j in range(24):
        far, outer, inner = end_rows(mine_ref, other_ref, index_ref, j)
        blank = jnp.zeros_like(inner)
        ends_ref[j : j + 1, lanes(0)] = jnp.where(far, blank, inner)
        ends_ref[j : j + 1, lanes(1)] = outer
        ends_ref[j : j + 1, lanes(2)] = jnp.where(far, inner, blank)
    strip_rows = 12 * EDGE
    triples(line_ref, line_cols_ref, (2, 1, 0))
    line_cols_ref[strip_rows:, :] = ends_ref[...].astype(BF16)
    triples(deep_ref, deep_cols_ref, (2, 1, 0))
    wide_ref[...] = dot(line_cols_ref[...], sides2_ref[: 3 * CH])
    strip_wide_ref[...] = dot(deep_cols_ref[...], sides2_ref[: 3 * CH]) + dot(
        line_cols_ref[:strip_rows, :], sides2_ref[3 * CH :]
    )
    cot_ref[...] = rest_ref[768:, lanes(1)]
    rims = []
    for n in range(12):
        side = index_ref[near_at(n) + 2]
        rims.append(pick(wide_ref, n * EDGE, EDGE, side))
        cot_ref[strip(n), :] += pick(strip_wide_ref, n * EDGE, EDGE, side)
        for h in range(2):
            j = 2 * n + h
            at = n * EDGE + (0, EDGE - 1)[h]
            cot_ref[at : at + 1, :] += pick(
                wide_ref, strip_rows + j, 1, index_ref[lateral_at(j) + 2]
            )
    cells_ref[:768] = rest_ref[:768, lanes(1)]
    add_sides(cells_ref, turned(turn, jnp.concatenate(rims, axis=0)))
    delta = gelu_slope(rest_ref[:768, lanes(0)]) * cells_ref[:768]
    fill_pad(pad_ref, delta.astype(BF16).astype(F32))
    windows(pad_ref, cols_ref)
    strip_delta = (gelu_slope(rest_ref[768:, lanes(0)]) * cot_ref[...]).astype(BF16).astype(F32)
    line_ref[:, 1 : EDGE + 1, :] = strip_delta.reshape(12, EDGE, CH)
    triples(line_ref, deep_cols_ref, (2, 1, 0))
    strip_wide_ref[...] = dot(deep_cols_ref[...], sides_ref[...])
    rims = []
    for n in range(12):
        rims.append(pick(strip_wide_ref, n * EDGE, EDGE, index_ref[near_at(n) + 2]))
    cells_ref[:768] = dot(cols_ref[...], late_ref[:, W1_BACK])
    add_sides(cells_ref, turned(turn, jnp.concatenate(rims, axis=0)))
    out_ref[...] = as_cells(cells_ref[:768]).astype(BF16)


def first_table_kernel(*refs):
    table_ref = refs[-1]
    for at in range(4):
        table_ref[at, 0] = refs[at][...]
        table_ref[at, 1] = refs[4 + at][...]


def gate_kernel(*refs):
    refs[-1][...] = jnp.zeros_like(refs[-1])


def table_kernel(own_ref, one_ref, two_ref, three_ref, table_ref):
    for at, part_ref in enumerate((own_ref, one_ref, two_ref, three_ref)):
        table_ref[at] = part_ref[...]


def spread_sum(pieces_ref, copies_ref):
    total = jnp.sum(pieces_ref[...].astype(F32), axis=0).astype(BF16)
    for at in range(copies_ref.shape[0]):
        copies_ref[at] = total


def first_sum_kernel(pieces_ref, flag_ref, own_ref, across_ref, copies_ref, pair_ref):
    spread_sum(pieces_ref, copies_ref)
    pair_ref[0] = own_ref[...]
    pair_ref[1] = across_ref[...]


def second_sum_kernel(
    pieces_ref, flag_ref, own_ref, one_ref, two_ref, three_ref, copies_ref, table_ref
):
    spread_sum(pieces_ref, copies_ref)
    table_kernel(own_ref, one_ref, two_ref, three_ref, table_ref)


def keep_kernel(grads_ref, got_ref, kept_ref):
    kept_ref[...] = (grads_ref[0] + got_ref[...]).astype(BF16)


def hold_kernel(block_ref, flag_ref, out_ref):
    out_ref[...] = block_ref[...]


def finish_kernel(
    scale, mine_ref, other_ref, first_hbm, second_hbm, down_hbm, first_ref, second_ref, down_ref,
    sems,
):
    copies = []
    core = lax.axis_index("c")
    for at in range(22):
        half = at // 11
        rows = slice(at % 11 * CH, (at % 11 + 1) * CH)
        block = jnp.where(core == half, mine_ref[rows, :], other_ref[rows, :])
        out_ref, base = ((first_ref, 0), (second_ref, 9), (down_ref, 18))[at // 9]
        out_ref[at - base] = block.astype(F32) * scale
        if at in (8, 17, 21):
            out_hbm = (first_hbm, second_hbm, down_hbm)[at // 9]
            copies.append(pltpu.make_async_copy(out_ref, out_hbm, sems.at[at // 9]))
            copies[-1].start()
    finish(copies)


def whole(space):
    return pl.BlockSpec(memory_space=space)


def shards(
    activations,
    conv1_weight,
    conv2_weight,
    coarse_kernel_weight,
    skip_cotangent,
    down_cotangent,
    face_neighbours,
    seam_codes,
    tile_slots,
):
    x = activations[0]
    tiles = x.shape[0]
    total_tiles = tile_slots.shape[0]
    cells = tiles * EDGE * EDGE
    strips = 4 * tiles * EDGE
    half = EDGE // 2
    quarter = tiles * half * half
    smem, vmem, hbm = whole(pltpu.SMEM), whole(pltpu.VMEM), whole(pltpu.HBM)
    shape = jax.ShapeDtypeStruct
    plane = lax.axis_size(PLANE)
    deep = lax.axis_size(DEPTH)
    pad = shape((tiles, EDGE + 2, EDGE + 8, CH), F32)
    line = shape((4 * tiles, EDGE + 8, CH), F32)
    ring = shape((tiles, 4, 2, EDGE, CH), BF16)

    def call(
        kernel, outs, operands, scratch=(), sems=(), specs=None, out_specs=None, cost=1, room=24
    ):
        single = not isinstance(outs, tuple)
        scratch = [pltpu.VMEM(one.shape, one.dtype) for one in scratch]
        scratch += [pltpu.SemaphoreType.DMA((count,)) for count in sems]
        return pl.pallas_call(
            kernel,
            out_shape=outs,
            in_specs=specs or [vmem] * len(operands),
            out_specs=out_specs or (vmem if single else (vmem,) * len(outs)),
            scratch_shapes=scratch,
            compiler_params=pltpu.CompilerParams(vmem_limit_bytes=room * 1024 * 1024),
            cost_estimate=pl.CostEstimate(
                flops=cost * cells * 18 * CH * CH, bytes_accessed=2 * 1024 * 1024, transcendentals=0
            ),
        )(*operands)

    wide = shape((strips, 4 * CH), F32)
    all_cols = shape((cells, 9 * CH), BF16)
    cell_rows = shape((cells, CH), F32)
    strip_rows = shape((strips, CH), F32)
    roomy_rows = shape((cells + EDGE * EDGE, CH), F32)
    flag = shape((8, CH), F32)
    own_ring = call(ring_kernel, ring, [x], [roomy_rows])
    across = swap_apart(own_ring, "z", 1)
    operands = [
        x,
        skip_cotangent[0],
        down_cotangent.reshape(-1, CH),
        conv1_weight.reshape(9 * CH, CH),
        conv2_weight.reshape(9 * CH, CH),
        coarse_kernel_weight.reshape(4 * CH, CH),
    ]
    turn_shape = shape((strips, strips), BF16)
    index, turn = call(
        index_kernel,
        (shape((296,), jnp.int32), turn_shape),
        [face_neighbours.T, seam_codes.T, tile_slots],
        [turn_shape],
        (1,),
        specs=[smem] * 3,
        out_specs=(smem, hbm),
        cost=4,
        room=60,
    )
    staged = (
        shape((9 * CH, 3 * CH), BF16),
        shape((9 * CH, 3 * CH), BF16),
        shape((cells, 2 * CH), F32),
    )
    ready, early, late, staged_cells = call(
        stage_kernel,
        (shape((8,), jnp.int32),) + staged,
        [index] + operands,
        tuple(operands) + staged
        + (pad, pad, all_cols, shape((CH, 4 * CH), BF16)),
        (len(operands), len(staged)),
        specs=[smem] + [hbm] * 6,
        out_specs=(smem,) + (hbm,) * 3,
        cost=100,
        room=50,
    )
    near_rings = [own_ring] + [swap_apart(own_ring, "y", apart) for apart in (1, 2, 3)]
    far_rings = [across] + [swap_apart(across, "y", apart) for apart in (1, 2, 3)]
    mine = call(
        first_table_kernel,
        shape((4, 2) + ring.shape, BF16),
        near_rings + far_rings + [index, ready],
        specs=[vmem] * 8 + [smem] * 2,
    )
    other = swap_core(mine)

    def table(block):
        return block.reshape((-1,) + ring.shape[1:])

    (
        coarse, delta_ring, pre, strip_pre, seam, cols2, strip_cols, down_cols, delta, line_rows,
    ) = call(
        forward_kernel,
        (
            shape((quarter, CH), BF16),
            ring,
            cell_rows,
            strip_rows,
            strip_rows,
            all_cols,
            shape((strips, 9 * CH), BF16),
            shape((quarter, 4 * CH), BF16),
            shape((cells, CH), BF16),
            line,
        ),
        [index, turn, table(mine), table(other), early, staged_cells],
        [
            pad,
            shape((4 * tiles, 3, EDGE + 8, CH), F32),
            wide,
            pad,
            roomy_rows,
            shape((strips, 3 * CH), BF16),
            shape((9 * CH, 4 * CH), BF16),
        ],
        specs=[smem] + [vmem] * 5,
        cost=2,
    )
    grads, rest = call(
        gradient_kernel,
        (shape((2, 11 * CH, CH), F32), shape((cells + strips, 2 * CH), F32)),
        [
            index, turn, early, late, pre, strip_pre, seam, cols2, strip_cols, down_cols, delta,
            line_rows,
        ],
        [
            pad,
            all_cols,
            all_cols,
            shape((strips, 4 * CH), BF16),
            shape((strips, 3 * CH), BF16),
            shape((3 * CH, 4 * CH), BF16),
        ],
        specs=[smem] + [vmem] * 11,
        cost=4,
    )
    kept = call(keep_kernel, shape(grads.shape[1:], BF16), [grads, swap_core(grads[1])])
    part = kept.shape[0] // plane
    across = swap_apart(delta_ring, "z", 1)
    pieces = lax.all_to_all(kept.reshape(plane, part, CH), PLANE, 0, 0)
    copies, pair = call(
        first_sum_kernel,
        (shape((deep, part, CH), BF16), shape((2,) + ring.shape, BF16)),
        [pieces, call(gate_kernel, flag, [across], cost=100), delta_ring, across],
    )
    along = [swap_apart(pair, "y", apart) for apart in (1, 2, 3)]
    pieces = lax.all_to_all(copies, DEPTH, 0, 0)
    copies, mine = call(
        second_sum_kernel,
        (shape((plane, part, CH), BF16), shape((4,) + pair.shape, BF16)),
        [pieces, call(gate_kernel, flag, along, cost=100), pair] + along,
    )
    other = swap_core(mine)
    summed = lax.all_to_all(copies, PLANE, 0, 0).reshape(-1, CH)
    input_grad, done = call(
        backward_kernel,
        (shape(x.shape, BF16), flag),
        [index, turn, table(mine), table(other), late, rest],
        [
            pad,
            all_cols,
            line,
            line,
            shape((strips + 32, 3 * CH), BF16),
            shape((strips, 3 * CH), BF16),
            shape((32, 3 * CH), F32),
            shape((strips + 32, 4 * CH), F32),
            wide,
            strip_rows,
            roomy_rows,
            shape((3 * CH, 4 * CH), BF16),
            shape((6 * CH, 4 * CH), BF16),
        ],
        specs=[smem] + [vmem] * 5,
        cost=100,
    )
    summed = call(hold_kernel, shape(summed.shape, BF16), [summed, done])
    scale = 1.0 / math.sqrt(lax.axis_size(("w", "x")) * total_tiles * EDGE * EDGE)
    first_grad, second_grad, down_grad = call(
        functools.partial(finish_kernel, scale),
        tuple(shape((count, CH, CH), F32) for count in (9, 9, 4)),
        [summed, swap_core(summed)],
        [shape((count, CH, CH), F32) for count in (9, 9, 4)],
        (3,),
        out_specs=(hbm,) * 3,
    )
    return (
        coarse.reshape((1, tiles, half, half, CH)),
        input_grad[None],
        first_grad.reshape(conv1_weight.shape),
        second_grad.reshape(conv2_weight.shape),
        down_grad.reshape(coarse_kernel_weight.shape),
    )


def solution(mesh):
    batch = mesh.shape["batch"]
    along_x = 4 if batch % 4 == 0 else 1
    fine = Mesh(
        mesh.devices.reshape(4, 2, 2, batch // along_x, along_x), ("y", "z", "c", "w", "x")
    )
    field = P(("w", "x"), ("y", "z", "c"), None, None, None)
    return jax.shard_map(
        shards,
        mesh=fine,
        in_specs=(field, P(), P(), P(), field, field, P(), P(), P()),
        out_specs=(field, field, P(), P(), P()),
        check_vma=False,
    )
```
